32 devices in a mesh: dp: 8 (over y, x, core), tensor: 4 (over z).
Axes of the slice: x: 2, y: 2, z: 4, core: 2. Of those that a mesh axis runs over, the one named last changes fastest.
Arguments:
- inputs: bfloat16 [16384, 768], P(('dp', 'tensor')), may hold values from -6 to 6
- attention_gain: float32 [768], replicated, may hold values from 0.5 to 1.5
- feedforward_gain: float32 [768], replicated, may hold values from 0.5 to 1.5
- query_weight: bfloat16 [768, 768], P('dp', 'tensor'), may hold values from -0.109375 to 0.109375
- key_weight: bfloat16 [768, 768], P('dp', 'tensor'), may hold values from -0.109375 to 0.109375
- value_weight: bfloat16 [768, 768], P('dp', 'tensor'), may hold values from -0.21875 to 0.21875
- output_weight: bfloat16 [768, 768], P('tensor', 'dp'), may hold values from -1.75 to 1.75
- inner_weight: bfloat16 [768, 3072], P('dp', 'tensor'), may hold values from -0.21875 to 0.21875
- outer_weight: bfloat16 [3072, 768], P('tensor', 'dp'), may hold values from -0.15625 to 0.15625
- bias_table: float32 [32, 12], P(None, 'tensor'), may hold values from -6 to 6
- block_index: int32 [8, 2048], P('dp'), may hold values from 0 to 7, never falling along the last dimension, each value on 1 to 512 neighbouring positions
- position_bucket: int32 [4095], replicated, may hold values from 0 to 31
- cotangent: bfloat16 [16384, 768], P(('dp', 'tensor')), may hold values from -6 to 6
Outputs:
- layer_output: bfloat16 [16384, 768], P(('dp', 'tensor'))
- input_grad: bfloat16 [16384, 768], P(('dp', 'tensor'))
- attention_gain_grad: float32 [768], replicated
- feedforward_gain_grad: float32 [768], replicated
- query_grad: float32 [768, 768], P('dp', 'tensor')
- key_grad: float32 [768, 768], P('dp', 'tensor')
- value_grad: float32 [768, 768], P('dp', 'tensor')
- output_grad: float32 [768, 768], P('tensor', 'dp')
- inner_grad: float32 [768, 3072], P('dp', 'tensor')
- outer_grad: float32 [3072, 768], P('tensor', 'dp')
- table_grad: float32 [32, 12], replicated
The draws below stay inside these ranges and needn't reach their ends.
Inputs may be any that keep to these rules, and one draw needn't show every extreme that they name: `block_index`: in each sequence's row of 2048 positions the block numbers never fall; a block holds 1 to 512 positions, and some block holds exactly 512.
All inputs are finite; a program needn't handle non-finite values.
Results may differ from the reference program's by a relative error of at most 0.018.
Values may be sent and summed in bfloat16 or wider, within the bound.
No kernel may reach another device: no remote copies, remote signals or barrier semaphores. Data moves between devices by JAX's collectives and lax.ppermute only.
A program may use at most 192 MiB of HBM per device.

```python
import math
import jax
import jax.numpy as jnp
import numpy as np
from jax import lax

D = 768
H = 12
DH = 64
FF = 3072
BUCKETS = 32
LEN = 2048
NBLK = 8
MAXBLK = 512
NSEQ = 8
TOKENS = 16384


def touch_ends(values, rng, least, largest):
    index_at = [jax.random.randint(jax.random.fold_in(rng, axis), (), 0, length) for axis, length in enumerate(values.shape)]
    longest = values.shape.index(max(values.shape))
    next_to = index_at[:longest] + [(index_at[longest] + 1) % values.shape[longest]] + index_at[longest + 1:]
    return values.at[tuple(index_at)].set(least).at[tuple(next_to)].set(largest)


def block_scale(rng, shape, pieces, low, top_value):
    loudness = 1.0
    for position, blocks in pieces:
        steps = jax.random.uniform(jax.random.fold_in(jax.random.fold_in(rng, 6), position), (blocks,), jnp.float32, low / len(pieces), top_value / len(pieces))
        loudness = loudness * jnp.repeat(jnp.exp(steps), shape[position] // blocks).reshape((-1,) + (1,) * (len(shape) - 1 - position))
    return loudness


def length_profile(amount, total, bound, lean):
    portions = [(1 << 20) // math.isqrt(standing ** lean) + 1 for standing in range(2, amount + 1)]
    spare, counts = total - bound - (amount - 1), [1] * (amount - 1)
    while spare > 0:
        free = [i for i in range(amount - 1) if counts[i] < bound]
        whole, left = sum([portions[i] for i in free]), spare
        for i in free:
            addition = min(bound - counts[i], max(1, left * portions[i] // whole), spare)
            counts[i] = counts[i] + addition
            spare = spare - addition
    return np.array([bound] + counts)


def uneven(key, number_of, total, bound, slope):
    if number_of == 2:
        one = jax.random.randint(key, (), max(1, total - bound), min(bound, total - 1) + 1)
        return jnp.stack([one, total - one])
    lengths = jnp.asarray(length_profile(number_of, total, bound, slope), jnp.int32)
    pairs = (number_of - 1) // 2
    donor, sink = lengths[1:1 + 2 * pairs:2], lengths[2:2 + 2 * pairs:2]
    room = jnp.minimum(donor - 1, bound - sink)
    moved = jax.random.randint(jax.random.fold_in(key, 1), (pairs,), 0, 1 << 20) % (room + 1)
    lengths = lengths.at[1:1 + 2 * pairs:2].set(donor - moved).at[2:2 + 2 * pairs:2].set(sink + moved)
    return lengths[jax.random.permutation(jax.random.fold_in(key, 2), number_of)]


def scatter_about(stream_key, shape, deviation, most, pieces=(), held_as=jnp.bfloat16):
    values = jax.random.normal(stream_key, shape, jnp.float32) * deviation
    if len(pieces) > 0:
        values = block_scale(stream_key, shape, pieces, -0.22, 0.18) * values
    return jnp.clip(values, min=-most, max=most).astype(held_as)


def setup_inputs(seed: int = 0) -> dict:
    key_of = jax.random.split(jax.random.key(seed), 14)
    return {
        "inputs": scatter_about(key_of[0], (TOKENS, D), 1.0, 6.0, ((0, 32),)),
        "attention_gain": jnp.clip(1.0 + 0.1 * jax.random.normal(key_of[1], (D,), jnp.float32), 0.5, 1.5),
        "feedforward_gain": jnp.clip(1.0 + 0.1 * jax.random.normal(key_of[2], (D,), jnp.float32), 0.5, 1.5),
        "query_weight": scatter_about(key_of[3], (D, H * DH), (4 * D) ** -0.5, 0.109375, ((0, 8), (1, 4))),
        "key_weight": scatter_about(key_of[4], (D, H * DH), (4 * D) ** -0.5, 0.109375, ((0, 8), (1, 4))),
        "value_weight": scatter_about(key_of[5], (D, H * DH), D ** -0.5, 0.21875, ((0, 8), (1, 4))),
        "output_weight": scatter_about(key_of[6], (H * DH, D), (H * DH // 64) ** -0.5, 1.75, ((0, 4), (1, 8))),
        "inner_weight": scatter_about(key_of[7], (D, FF), D ** -0.5, 0.21875, ((0, 8), (1, 4))),
        "outer_weight": scatter_about(key_of[8], (FF, D), (FF // 2) ** -0.5, 0.15625, ((0, 4), (1, 8))),
        "bias_table": scatter_about(key_of[9], (BUCKETS, H), 1.0, 6.0, ((1, 4),), jnp.float32),
        "block_index": jax.vmap(lambda own: jnp.searchsorted(jnp.cumsum(uneven(own, NBLK, LEN, MAXBLK, 0)), jnp.arange(LEN), side="right"))(jax.random.split(key_of[10], NSEQ)).reshape((NSEQ, LEN)).astype(jnp.int32),
        "position_bucket": touch_ends(jax.random.randint(key_of[11], (2 * LEN - 1,), 0, BUCKETS), jax.random.fold_in(key_of[11], 1), 0, BUCKETS - 1).astype(jnp.int32),
        "cotangent": scatter_about(key_of[12], (TOKENS, D), 1.0, 6.0, ((0, 32),)),
    }


EPSILON = 1e-06
MASKED = -1e+30

@jax.custom_vjp
def low(v):
    return lax.optimization_barrier(v.astype(jnp.bfloat16)).astype(jnp.float32)

@jax.custom_vjp
def low_back(v):
    return v

def low_keep(v):
    return (low(v), None)

def low_pass(kept, grad):
    return (grad,)

def back_keep(v):
    return (v, None)

def back_low(kept, grad):
    return (low(grad),)
low.defvjp(low_keep, low_pass)
low_back.defvjp(back_keep, back_low)

def both_ways(value):
    return low(low_back(value))

def product(left, right):
    return jnp.dot(left, right, precision=lax.Precision.HIGHEST, preferred_element_type=jnp.float32)

def rms_norm(values, gain):
    return values * lax.rsqrt(lax.optimization_barrier(jnp.mean(values * values, axis=-1, keepdims=True)) + EPSILON) * gain

def attention(query_rows, key_rows, value_rows, bias_offset, block_row):
    block_width = min(512, LEN)
    firsts = jnp.arange(LEN // block_width, dtype=jnp.int32) * block_width
    key_place = jnp.arange(LEN, dtype=jnp.int32)

    @jax.checkpoint
    def one_block(first_row):
        query_block = lax.dynamic_slice_in_dim(query_rows, first_row, block_width, 0)
        query_place = first_row + jnp.arange(block_width, dtype=jnp.int32)
        offsets = key_place[None, :] - query_place[:, None] + (LEN - 1)
        bias_block = jnp.transpose(bias_offset[offsets], (2, 0, 1))
        scores = jnp.einsum('qhd,khd->hqk', query_block, key_rows, precision=lax.Precision.HIGHEST) + bias_block
        scores = low_back(scores)
        query_blocks = lax.dynamic_slice_in_dim(block_row, first_row, block_width, 0)
        allowed = block_row[None, :] <= query_blocks[:, None]
        scores = jnp.where(allowed[None], scores, MASKED)
        weights = low(jax.nn.softmax(scores, axis=-1))
        return jnp.einsum('hqk,khd->qhd', weights, value_rows, precision=lax.Precision.HIGHEST)
    mixtures = lax.map(one_block, firsts)
    return mixtures.reshape(LEN, H * DH)

def layer(inputs, attention_gain, feedforward_gain, query_weight, key_weight, value_weight, output_weight, inner_weight, outer_weight, bias_table, block_index, position_bucket):
    bias_offset = bias_table[position_bucket]

    def one_sequence(packed):
        sequence_rows, block_row = packed
        normed = low(rms_norm(sequence_rows, attention_gain))
        query_rows = both_ways(product(normed, query_weight)).reshape(LEN, H, DH)
        key_rows = both_ways(product(normed, key_weight)).reshape(LEN, H, DH)
        value_rows = both_ways(product(normed, value_weight)).reshape(LEN, H, DH)
        mixture = both_ways(attention(query_rows, key_rows, value_rows, bias_offset, block_row))
        hidden = sequence_rows + low_back(product(mixture, output_weight))
        second = low(rms_norm(hidden, feedforward_gain))
        inner = low_back(product(second, inner_weight))
        active = both_ways(jax.nn.gelu(inner, approximate=False))
        return hidden + product(active, outer_weight)
    result = lax.map(one_sequence, (inputs.reshape(-1, LEN, D), block_index))
    return result.reshape(-1, D)

def reference(inputs, attention_gain, feedforward_gain, query_weight, key_weight, value_weight, output_weight, inner_weight, outer_weight, bias_table, block_index, position_bucket, cotangent):

    def forward(inputs32, gain_first, gain_second, query32, key32, value32, output32, inner32, outer32, table32):
        return layer(inputs32, gain_first, gain_second, query32, key32, value32, output32, inner32, outer32, table32, block_index, position_bucket)
    primals = (inputs.astype(jnp.float32), attention_gain, feedforward_gain, query_weight.astype(jnp.float32), key_weight.astype(jnp.float32), value_weight.astype(jnp.float32), output_weight.astype(jnp.float32), inner_weight.astype(jnp.float32), outer_weight.astype(jnp.float32), bias_table)
    result, pullback = jax.vjp(forward, *primals)
    grads = pullback(cotangent.astype(jnp.float32))
    factor = 1.0 / math.sqrt(TOKENS)
    return (result.astype(jnp.bfloat16), grads[0].astype(jnp.bfloat16), grads[1] * factor, grads[2] * factor, grads[3] * factor, grads[4] * factor, grads[5] * factor, grads[6] * factor, grads[7] * factor, grads[8] * factor, grads[9] * factor)
```

```python
import math

import jax
import jax.numpy as jnp
from jax import lax
from jax.experimental import pallas as pl
from jax.experimental.pallas import tpu as pltpu
from jax.sharding import PartitionSpec as P

H = 12
EPSILON = 1e-06
MASKED = -1e30
TILE = 256
AHEAD = 2
BLOCKS = 8
VMEM_LIMIT = 60 * 1024 * 1024
f32, bf16 = jnp.float32, jnp.bfloat16


def dot(left, right, contract=((1,), (0,))):
    return lax.dot_general(left, right, (contract, ((), ())), preferred_element_type=f32)


def norm_forward(values, gain):
    inverse = lax.rsqrt(jnp.mean(values * values, axis=-1, keepdims=True) + EPSILON)
    scaled = values * inverse
    return scaled, inverse, (scaled * gain).astype(bf16)


def norm_backward(grad_normed, scaled, inverse, gain):
    grad_scaled = grad_normed * gain
    return inverse * (
        grad_scaled - scaled * jnp.mean(grad_scaled * scaled, axis=-1, keepdims=True)
    )


def gelu_parts(values):
    cumulative = 0.5 * (1.0 + lax.erf(values * (1.0 / math.sqrt(2.0))))
    density = jnp.exp(-0.5 * values * values) * (1.0 / math.sqrt(2.0 * math.pi))
    return values * cumulative, cumulative + values * density


def whole(shape):
    return pl.BlockSpec(shape, lambda *_: (0,) * len(shape), pipeline_mode=pl.Buffered(1))


def params():
    return pltpu.CompilerParams(vmem_limit_bytes=VMEM_LIMIT)


def bias_rows(bias_table, position_bucket):
    bucket = jnp.concatenate([position_bucket, jnp.zeros((1,), jnp.int32)])[::-1]
    names = jnp.arange(bias_table.shape[0], dtype=jnp.int32)
    onehot = (bucket[None, :] == names[:, None]).astype(f32)
    rows = lax.dot_general(
        bias_table, onehot, (((0,), (0,)), ((), ())), precision=lax.Precision.HIGHEST
    )
    return rows[:, None, :], onehot


def bias_kernel(row_ref, out_ref):
    tiles = out_ref.shape[1]

    def one(place, _):
        start = pl.multiple_of((tiles - 1 - place) * TILE, TILE)
        piece = row_ref[0, :, pl.ds(start, 2 * TILE)]
        spread = jnp.broadcast_to(piece, (TILE, 2 * TILE))
        out_ref[0, place] = pltpu.roll(spread, 0, 1, stride=1, stride_axis=0)[:, TILE:]
        return 0

    lax.fori_loop(0, tiles, one, 0)


def bias_tiles(rows, length):
    heads = rows.shape[0]
    count = length // TILE
    rows = rows[:, :, (count - 1 - AHEAD) * TILE :]
    tiles = count + AHEAD
    return pl.pallas_call(
        bias_kernel,
        grid=(heads,),
        in_specs=[pl.BlockSpec((1, 1, rows.shape[2]), lambda h: (h, 0, 0))],
        out_specs=pl.BlockSpec((1, tiles, TILE, TILE), lambda h: (h, 0, 0, 0)),
        out_shape=jax.ShapeDtypeStruct((heads, tiles, TILE, TILE), f32),
        compiler_params=params(),
        name="bias_tiles",
    )(rows)


def table_part(bands, onehot, length):
    heads, tiles = bands.shape[:2]
    pieces = bands[:, ::-1, 0, :]
    pad = jnp.zeros((heads, 1, TILE), f32)
    line = jnp.concatenate([pieces[:, :, :TILE], pad], 1) + jnp.concatenate(
        [pad, pieces[:, :, TILE:]], 1
    )
    line = line.reshape(heads, (tiles + 1) * TILE)
    base = (length // TILE - 1 - AHEAD) * TILE
    return lax.dot_general(
        onehot[:, base : base + line.shape[1]],
        line,
        (((1,), (1,)), ((), ())),
        precision=lax.Precision.HIGHEST,
    )


def spans(block_row):
    length = block_row.shape[0]
    names = jnp.arange(BLOCKS, dtype=jnp.int32)[:, None]
    upto = jnp.sum(block_row[None, :] <= names, axis=1, dtype=jnp.int32)
    end = jnp.sum(jnp.where(block_row[None, :] == names, upto[:, None], 0), axis=0, dtype=jnp.int32)
    by_tile = end.reshape(length // TILE, TILE)
    full = by_tile[:, 0] // TILE
    most = (by_tile[:, TILE - 1] + TILE - 1) // TILE
    places = jnp.arange(length // TILE, dtype=jnp.int32)[:, None]
    least = jnp.sum(most[None, :] <= places, axis=1, dtype=jnp.int32)
    clear = jnp.sum(full[None, :] <= places, axis=1, dtype=jnp.int32)
    return end.reshape(1, length), full, most, least, clear


def forward_kernel(full_ref, most_ref, qt_ref, kt_ref, vt_ref, bias_ref, end_ref, ot_ref, lse_ref, k_ref, acc_ref, stat_ref):
    heads = qt_ref.shape[0]
    count = kt_ref.shape[2] // TILE
    query = pl.program_id(0)

    @pl.when(query == 0)
    def _():
        for h in range(heads):
            k_ref[h] = kt_ref[h].T

    acc_ref[...] = jnp.zeros_like(acc_ref)
    stat_ref[0] = jnp.full(stat_ref.shape[1:], -jnp.inf, f32)
    stat_ref[1] = jnp.zeros(stat_ref.shape[1:], f32)

    def step(key, masked):
        start = pl.multiple_of(key * TILE, TILE)
        if masked:
            keep = lax.broadcasted_iota(jnp.int32, (TILE, TILE), 0) + start < end_ref[...]
        for h in range(heads):
            scores = dot(k_ref[h, pl.ds(start, TILE), :], qt_ref[h])
            scores = scores + bias_ref[h, key - query + count - 1]
            if masked:
                scores = jnp.where(keep, scores, MASKED)
            old = stat_ref[0, h]
            new = jnp.maximum(old, jnp.max(scores, axis=0, keepdims=True))
            weights = jnp.exp(scores - new)
            scale = jnp.exp(old - new)
            stat_ref[0, h] = new
            stat_ref[1, h] = stat_ref[1, h] * scale + jnp.sum(weights, axis=0, keepdims=True)
            acc_ref[h] = acc_ref[h] * scale + dot(
                vt_ref[h, :, pl.ds(start, TILE)], weights.astype(bf16)
            )

    def full_step(key, _):
        step(key, False)
        return 0

    def edge_step(key, _):
        step(key, True)
        return 0

    lax.fori_loop(0, full_ref[query], full_step, 0)
    lax.fori_loop(full_ref[query], most_ref[query], edge_step, 0)
    for h in range(heads):
        total = stat_ref[1, h]
        ot_ref[0, h] = (acc_ref[h] * (1.0 / total)).astype(bf16)
        lse_ref[h] = stat_ref[0, h] + jnp.log(total)


def attend_forward(qt, kt, vt, bias, end, full, most, parts):
    heads, size, length = qt.shape
    count = length // TILE
    each = count // parts
    smem = pl.BlockSpec(memory_space=pltpu.SMEM)
    return pl.pallas_call(
        forward_kernel,
        grid=(count,),
        in_specs=[
            smem,
            smem,
            pl.BlockSpec((heads, size, TILE), lambda i: (0, 0, i)),
            whole(kt.shape),
            whole(vt.shape),
            whole(bias.shape),
            pl.BlockSpec((1, TILE), lambda i: (0, i)),
        ],
        out_specs=[
            pl.BlockSpec((1, heads, size, TILE), lambda i: (i // each, 0, 0, i % each)),
            pl.BlockSpec((heads, 1, TILE), lambda i: (0, 0, i)),
        ],
        out_shape=[
            jax.ShapeDtypeStruct((parts, heads, size, length // parts), bf16),
            jax.ShapeDtypeStruct((heads, 1, length), f32),
        ],
        scratch_shapes=[
            pltpu.VMEM((heads, length, size), bf16),
            pltpu.VMEM((heads, size, TILE), f32),
            pltpu.VMEM((2, heads, 1, TILE), f32),
        ],
        compiler_params=params(),
        name="attend_forward",
    )(full, most, qt, kt, vt, bias, end)


def backward_kernel(
    least_ref, clear_ref, qt_ref, kt_ref, vt_ref, ot_ref, got_ref, lse_ref, bias_ref, end_ref,
    out_ref, band_out_ref,
    q_ref, go_ref, dqt_acc, dk_acc, dv_acc, delta_ref, band_ref,
):
    heads, size, length = qt_ref.shape
    count = length // TILE
    parts = got_ref.shape[0]
    each = count // parts
    key = pl.program_id(0)
    key_cols = pl.ds(pl.multiple_of(key * TILE, TILE), TILE)

    @pl.when(key == 0)
    def _():
        dqt_acc[...] = jnp.zeros_like(dqt_acc)
        band_ref[...] = jnp.zeros_like(band_ref)
        for h in range(heads):
            q_ref[h] = qt_ref[h].T
            for part in range(parts):
                rows = pl.ds(part * (length // parts), length // parts)
                grad = got_ref[part, h]
                go_ref[h, rows, :] = grad.T
                delta_ref[h, :, rows] = jnp.sum(
                    ot_ref[part, h].astype(f32) * grad.astype(f32), axis=0, keepdims=True
                )

    dk_acc[...] = jnp.zeros_like(dk_acc)
    dv_acc[...] = jnp.zeros_like(dv_acc)
    kt = [kt_ref[h, :, key_cols] for h in range(heads)]
    k = [tile.T for tile in kt]
    v = [vt_ref[h, :, key_cols].T for h in range(heads)]

    def step(query, masked):
        cols = pl.ds(pl.multiple_of(query * TILE, TILE), TILE)
        part = query // each
        inner = pl.ds(pl.multiple_of((query % each) * TILE, TILE), TILE)
        if masked:
            keep = lax.broadcasted_iota(jnp.int32, (TILE, TILE), 0) + key * TILE < end_ref[:, cols]
        place = key - query + count - 1
        for h in range(heads):
            scores = dot(k[h], qt_ref[h, :, cols])
            scores = scores + bias_ref[h, place]
            if masked:
                scores = jnp.where(keep, scores, MASKED)
            weights = jnp.exp(scores - lse_ref[h, :, cols])
            grad_weights = dot(v[h], got_ref[part, h, :, inner])
            grad_scores = weights * (grad_weights - delta_ref[h, :, cols])
            rounded = grad_scores.astype(bf16)
            band_ref[h, place] += grad_scores
            dv_acc[h] += dot(weights.astype(bf16), go_ref[h, cols, :])
            dk_acc[h] += dot(rounded, q_ref[h, cols, :])
            dqt_acc[h, :, cols] += dot(kt[h], rounded)

    def edge_step(query, _):
        step(query, True)
        return 0

    def full_step(query, _):
        step(query, False)
        return 0

    lax.fori_loop(least_ref[key], clear_ref[key], edge_step, 0)
    lax.fori_loop(clear_ref[key], count, full_step, 0)
    for h in range(heads):
        out_ref[1, h, :, key_cols] = dk_acc[h].T.astype(bf16)
        out_ref[2, h, :, key_cols] = dv_acc[h].T.astype(bf16)

    @pl.when(key == count - 1)
    def _():
        out_ref[0] = dqt_acc[...].astype(bf16)

        def one(place, _):
            for h in range(heads):
                band = band_ref[h, place]
                zero = jnp.zeros((TILE // 2, TILE // 2), f32)
                upper, lower = band[: TILE // 2], band[TILE // 2 :]
                lines = jnp.concatenate([zero, zero, upper], axis=1) + jnp.concatenate(
                    [zero, lower, zero], axis=1
                )
                half = TILE // 4
                while half >= 8:
                    lines = lines[:half] + pltpu.roll(lines[half:], 2 * TILE - half, 1)
                    half //= 2
                total = lines[0:1]
                for row in range(1, 8):
                    total = total + pltpu.roll(lines[row : row + 1], 2 * TILE - row, 1)
                band_out_ref[h, place] = total
            return 0

        lax.fori_loop(0, band_ref.shape[1], one, 0)


def attend_backward(qt, kt, vt, ot, got, lse, bias, end, least, clear):
    heads, size, length = qt.shape
    count = length // TILE
    tiles = bias.shape[1]
    smem = pl.BlockSpec(memory_space=pltpu.SMEM)
    operands = (qt, kt, vt, ot, got, lse, bias, end)
    outs = [((3, heads, size, length), bf16), ((heads, tiles, 1, 2 * TILE), f32)]
    return pl.pallas_call(
        backward_kernel,
        grid=(count,),
        in_specs=[smem, smem] + [whole(a.shape) for a in operands],
        out_specs=[whole(shape) for shape, _ in outs],
        out_shape=[jax.ShapeDtypeStruct(shape, kind) for shape, kind in outs],
        scratch_shapes=[
            pltpu.VMEM((heads, length, size), bf16),
            pltpu.VMEM((heads, length, size), bf16),
            pltpu.VMEM((heads, size, length), f32),
            pltpu.VMEM((heads, TILE, size), f32),
            pltpu.VMEM((heads, TILE, size), f32),
            pltpu.VMEM((heads, 1, length), f32),
            pltpu.VMEM((heads, tiles, TILE, TILE), f32),
        ],
        compiler_params=params(),
        name="attend_backward",
    )(least, clear, *operands)


def feed_kernel(second_ref, grad_ref, weight_ref, out_ref, dsecond_ref, grads_ref):
    width = second_ref.shape[1]

    @pl.when(pl.program_id(0) == 0)
    def _():
        out_ref[...] = jnp.zeros_like(out_ref)
        dsecond_ref[...] = jnp.zeros_like(dsecond_ref)

    second = second_ref[...]
    grad = grad_ref[...]
    hidden = weight_ref.shape[2] // 2
    inner = weight_ref[0, :, :hidden]
    outer = weight_ref[0, :, hidden:]
    grad_active = dot(grad, outer).astype(bf16).astype(f32)
    units = dot(second, inner)
    active, slope = gelu_parts(units)
    active = active.astype(bf16)
    grad_units = (grad_active * slope).astype(bf16)
    out_ref[...] += dot(active, outer, ((1,), (1,)))
    dsecond_ref[...] += dot(grad_units, inner, ((1,), (1,)))
    grads_ref[0, :, :hidden] = dot(second, grad_units, ((0,), (0,))).astype(bf16)
    grads_ref[0, :, hidden:] = dot(grad, active, ((0,), (0,))).astype(bf16)


def feed_forward(second, grad, weights):
    rows, width = second.shape
    parts, _, columns = weights.shape
    return pl.pallas_call(
        feed_kernel,
        grid=(parts,),
        in_specs=[
            whole(second.shape),
            whole(grad.shape),
            pl.BlockSpec((1, width, columns), lambda i: (i, 0, 0)),
        ],
        out_specs=[
            whole((rows, width)),
            whole((rows, width)),
            pl.BlockSpec((1, width, columns), lambda i: (i, 0, 0)),
        ],
        out_shape=[
            jax.ShapeDtypeStruct((rows, width), f32),
            jax.ShapeDtypeStruct((rows, width), f32),
            jax.ShapeDtypeStruct(weights.shape, bf16),
        ],
        compiler_params=params(),
        name="feed_forward",
    )(second, grad, weights)


def body(
    inputs,
    attention_gain,
    feedforward_gain,
    query_weight,
    key_weight,
    value_weight,
    output_weight,
    inner_weight,
    outer_weight,
    bias_table,
    block_index,
    position_bucket,
    cotangent,
):
    length = block_index.shape[1]
    parts = lax.axis_size("tensor")
    groups = lax.axis_size("dp")
    factor = 1.0 / math.sqrt(block_index.shape[0] * length * groups)
    heads = bias_table.shape[1]
    width = inputs.shape[1]
    size = query_weight.shape[1] // heads
    columns = heads * size

    packed_attention = jnp.concatenate([query_weight, key_weight, value_weight], axis=1)
    packed_feed = jnp.concatenate([inner_weight, outer_weight.T], axis=1)
    attention_full = lax.all_gather(packed_attention, "dp", axis=0, tiled=True)
    output_full = lax.all_gather(output_weight.T, ("tensor", "dp"), axis=0, tiled=True).reshape(
        parts, width, columns
    )
    feed_full = lax.all_gather(packed_feed, ("tensor", "dp"), axis=0, tiled=True).reshape(
        parts, width, packed_feed.shape[1]
    )

    rows, onehot = bias_rows(bias_table, position_bucket)
    bias = bias_tiles(rows, length)
    end, full, most, least, clear = spans(block_index[0])

    inputs_wide = inputs.astype(f32)
    scaled_first, inverse_first, normed_local = norm_forward(inputs_wide, attention_gain)
    normed = lax.all_gather(normed_local, "tensor", axis=0, tiled=True)
    qkv = dot(attention_full, normed, ((0,), (1,))).astype(bf16).reshape(3, heads, size, length)
    qt, kt, vt = qkv[0], qkv[1], qkv[2]
    ot, lse = attend_forward(qt, kt, vt, bias, end, full, most, parts)
    mix = lax.all_to_all(ot.reshape(parts, columns, length // parts), "tensor", 0, 0)
    hidden = inputs_wide + sum(dot(mix[z], output_full[z], ((0,), (1,))) for z in range(parts))
    scaled_second, inverse_second, second = norm_forward(hidden, feedforward_gain)
    feed_out, grad_second, feed_grads = feed_forward(second, cotangent, feed_full)
    layer_output = (hidden + feed_out).astype(bf16)
    feedforward_part = jnp.sum(grad_second * scaled_second, axis=0)
    grad_hidden = cotangent.astype(f32) + norm_backward(
        grad_second, scaled_second, inverse_second, feedforward_gain
    )
    grad_mix_rows = grad_hidden.astype(bf16)
    output_grads = jnp.stack(
        [dot(grad_mix_rows, mix[z], ((0,), (1,))) for z in range(parts)]
    ).astype(bf16)
    grad_mix = jnp.stack(
        [dot(output_full[z], grad_mix_rows, ((0,), (1,))) for z in range(parts)]
    ).astype(bf16)
    got = lax.all_to_all(grad_mix, "tensor", 0, 0).reshape(ot.shape)
    dqkv, bands = attend_backward(qt, kt, vt, ot, got, lse, bias, end, least, clear)
    dqkv = dqkv.reshape(3 * columns, length)
    attention_grads = dot(normed, dqkv, ((0,), (1,)))
    grad_normed = dot(dqkv, attention_full, ((0,), (1,)))
    grad_first = lax.psum_scatter(
        grad_normed.astype(bf16), "tensor", scatter_dimension=0, tiled=True
    ).astype(f32)
    input_grad = (
        grad_hidden + norm_backward(grad_first, scaled_first, inverse_first, attention_gain)
    ).astype(bf16)
    attention_part = jnp.sum(grad_first * scaled_first, axis=0)

    table_local = table_part(bands, onehot, length)
    table_whole = lax.dynamic_update_slice(
        jnp.zeros((table_local.shape[0], H), f32),
        table_local,
        (jnp.zeros((), jnp.int32), lax.axis_index("tensor") * heads),
    )
    attention_gain_grad, feedforward_gain_grad, table_grad = lax.psum(
        (attention_part * factor, feedforward_part * factor, table_whole * factor), ("dp", "tensor")
    )

    attention_share = (
        lax.psum_scatter(attention_grads.astype(bf16), "dp", scatter_dimension=0, tiled=True)
        .astype(f32)
        * factor
    )
    output_share = (
        lax.psum_scatter(
            output_grads.reshape(parts * width, columns),
            ("tensor", "dp"),
            scatter_dimension=0,
            tiled=True,
        ).astype(f32)
        * factor
    )
    feed_share = (
        lax.psum_scatter(
            feed_grads.reshape(parts * width, packed_feed.shape[1]),
            ("tensor", "dp"),
            scatter_dimension=0,
            tiled=True,
        ).astype(f32)
        * factor
    )
    hidden_units = inner_weight.shape[1]
    return (
        layer_output,
        input_grad,
        attention_gain_grad,
        feedforward_gain_grad,
        attention_share[:, :columns],
        attention_share[:, columns : 2 * columns],
        attention_share[:, 2 * columns :],
        output_share.T,
        feed_share[:, :hidden_units],
        feed_share[:, hidden_units:].T,
        table_grad,
    )


def solution(mesh):
    tokens = P(("dp", "tensor"), None)
    by_rows = P("dp", "tensor")
    by_columns = P("tensor", "dp")
    placed = (
        tokens, P(), P(), by_rows, by_rows, by_rows, by_columns, by_rows, by_columns,
        P(None, "tensor"), P("dp", None), P(), tokens,
    )
    results = (
        tokens, tokens, P(), P(), by_rows, by_rows, by_rows, by_columns, by_rows, by_columns, P(),
    )
    return jax.shard_map(body, mesh=mesh, in_specs=placed, out_specs=results, check_vma=False)
```

```python
import math

import jax
import jax.numpy as jnp
from jax import lax
from jax.experimental import pallas as pl
from jax.experimental.pallas import tpu as pltpu
from jax.sharding import Mesh, PartitionSpec as P

H = 12
EPSILON = 1e-06
MASKED = -1e30
TILE = 256
AHEAD = 2
BLOCKS = 8
VMEM_LIMIT = 60 * 1024 * 1024
f32, bf16 = jnp.float32, jnp.bfloat16


def dot(left, right, contract=((1,), (0,))):
    return lax.dot_general(left, right, (contract, ((), ())), preferred_element_type=f32)


def norm_forward(values, gain):
    inverse = lax.rsqrt(jnp.mean(values * values, axis=-1, keepdims=True) + EPSILON)
    scaled = values * inverse
    return scaled, inverse, (scaled * gain).astype(bf16)


def norm_backward(grad_normed, scaled, inverse, gain):
    grad_scaled = grad_normed * gain
    return inverse * (
        grad_scaled - scaled * jnp.mean(grad_scaled * scaled, axis=-1, keepdims=True)
    )


def gelu_parts(values):
    cumulative = 0.5 * (1.0 + lax.erf(values * (1.0 / math.sqrt(2.0))))
    density = jnp.exp(-0.5 * values * values) * (1.0 / math.sqrt(2.0 * math.pi))
    return values * cumulative, cumulative + values * density


def whole(shape):
    return pl.BlockSpec(shape, lambda *_: (0,) * len(shape), pipeline_mode=pl.Buffered(1))


def params():
    return pltpu.CompilerParams(vmem_limit_bytes=VMEM_LIMIT)


def bias_rows(bias_table, position_bucket):
    bucket = jnp.concatenate([position_bucket, jnp.zeros((1,), jnp.int32)])[::-1]
    names = jnp.arange(bias_table.shape[0], dtype=jnp.int32)
    onehot = (bucket[None, :] == names[:, None]).astype(f32)
    rows = lax.dot_general(
        bias_table, onehot, (((0,), (0,)), ((), ())), precision=lax.Precision.HIGHEST
    )
    return rows[:, None, :], onehot


def bias_kernel(row_ref, out_ref):
    tiles = out_ref.shape[1]

    def one(place, _):
        start = pl.multiple_of((tiles - 1 - place) * TILE, TILE)
        piece = row_ref[0, :, pl.ds(start, 2 * TILE)]
        spread = jnp.broadcast_to(piece, (TILE, 2 * TILE))
        out_ref[0, place] = pltpu.roll(spread, 0, 1, stride=1, stride_axis=0)[:, TILE:]
        return 0

    lax.fori_loop(0, tiles, one, 0)


def bias_tiles(rows, length):
    heads = rows.shape[0]
    count = length // TILE
    rows = rows[:, :, (count - 1 - AHEAD) * TILE :]
    tiles = count + AHEAD
    return pl.pallas_call(
        bias_kernel,
        grid=(heads,),
        in_specs=[pl.BlockSpec((1, 1, rows.shape[2]), lambda h: (h, 0, 0))],
        out_specs=pl.BlockSpec((1, tiles, TILE, TILE), lambda h: (h, 0, 0, 0)),
        out_shape=jax.ShapeDtypeStruct((heads, tiles, TILE, TILE), f32),
        compiler_params=params(),
        name="bias_tiles",
    )(rows)


def table_part(bands, onehot, length):
    heads, tiles = bands.shape[:2]
    pieces = bands[:, ::-1, 0, :]
    pad = jnp.zeros((heads, 1, TILE), f32)
    line = jnp.concatenate([pieces[:, :, :TILE], pad], 1) + jnp.concatenate(
        [pad, pieces[:, :, TILE:]], 1
    )
    line = line.reshape(heads, (tiles + 1) * TILE)
    base = (length // TILE - 1 - AHEAD) * TILE
    return lax.dot_general(
        onehot[:, base : base + line.shape[1]],
        line,
        (((1,), (1,)), ((), ())),
        precision=lax.Precision.HIGHEST,
    )


def spans(block_row):
    length = block_row.shape[0]
    names = jnp.arange(BLOCKS, dtype=jnp.int32)[:, None]
    upto = jnp.sum(block_row[None, :] <= names, axis=1, dtype=jnp.int32)
    end = jnp.sum(jnp.where(block_row[None, :] == names, upto[:, None], 0), axis=0, dtype=jnp.int32)
    by_tile = end.reshape(length // TILE, TILE)
    full = by_tile[:, 0] // TILE
    most = (by_tile[:, TILE - 1] + TILE - 1) // TILE
    places = jnp.arange(length // TILE, dtype=jnp.int32)[:, None]
    least = jnp.sum(most[None, :] <= places, axis=1, dtype=jnp.int32)
    clear = jnp.sum(full[None, :] <= places, axis=1, dtype=jnp.int32)
    return end.reshape(1, length), full, most, least, clear


def forward_kernel(full_ref, most_ref, slot_ref, group_ref, *refs):
    parts = slot_ref.shape[0]
    pieces = refs[:parts]
    bias_ref, end_ref, ot_ref, lse_ref, qt_ref, k_ref, vt_ref, acc_ref, stat_ref = refs[parts:]
    heads, size, length = qt_ref.shape
    count = length // TILE
    each = count // parts
    query = pl.program_id(0)

    @pl.when(query == 0)
    def _():
        for i, piece in enumerate(pieces):
            places = pl.ds(pl.multiple_of(slot_ref[i] * (length // parts), TILE), length // parts)
            for h in range(heads):
                qt_ref[h, :, places] = piece[h]
                k_ref[h, places, :] = piece[heads + h].T
                vt_ref[h, :, places] = piece[2 * heads + h]

    own = pl.ds(pl.multiple_of(query * TILE, TILE), TILE)
    acc_ref[...] = jnp.zeros_like(acc_ref)
    stat_ref[0] = jnp.full(stat_ref.shape[1:], -jnp.inf, f32)
    stat_ref[1] = jnp.zeros(stat_ref.shape[1:], f32)

    def step(key, masked):
        start = pl.multiple_of(key * TILE, TILE)
        if masked:
            keep = lax.broadcasted_iota(jnp.int32, (TILE, TILE), 0) + start < end_ref[...]
        for h in range(heads):
            scores = dot(k_ref[h, pl.ds(start, TILE), :], qt_ref[h, :, own])
            scores = scores + bias_ref[h, key - query + count - 1]
            if masked:
                scores = jnp.where(keep, scores, MASKED)
            old = stat_ref[0, h]
            new = jnp.maximum(old, jnp.max(scores, axis=0, keepdims=True))
            weights = jnp.exp(scores - new)
            scale = jnp.exp(old - new)
            stat_ref[0, h] = new
            stat_ref[1, h] = stat_ref[1, h] * scale + jnp.sum(weights, axis=0, keepdims=True)
            acc_ref[h] = acc_ref[h] * scale + dot(
                vt_ref[h, :, pl.ds(start, TILE)], weights.astype(bf16)
            )

    def full_step(key, _):
        step(key, False)
        return 0

    def edge_step(key, _):
        step(key, True)
        return 0

    lax.fori_loop(0, full_ref[query], full_step, 0)
    lax.fori_loop(full_ref[query], most_ref[query], edge_step, 0)
    turn = lax.rem(query // each - group_ref[0] + parts, parts)
    inner = pl.ds(pl.multiple_of(lax.rem(query, each) * TILE, TILE), TILE)
    for h in range(heads):
        total = stat_ref[1, h]
        ot_ref[turn, h, :, inner] = (acc_ref[h] * (1.0 / total)).astype(bf16)
        lse_ref[h] = stat_ref[0, h] + jnp.log(total)


def attend_forward(pieces, bias, end, full, most, slots, group):
    parts = len(pieces)
    triple, size, part_length = pieces[0].shape
    heads, length = triple // 3, parts * part_length
    count = length // TILE
    smem = pl.BlockSpec(memory_space=pltpu.SMEM)
    return pl.pallas_call(
        forward_kernel,
        grid=(count,),
        in_specs=[smem] * 4
        + [whole(piece.shape) for piece in pieces]
        + [whole(bias.shape), pl.BlockSpec((1, TILE), lambda i: (0, i))],
        out_specs=[
            whole((parts, heads, size, part_length)),
            pl.BlockSpec((heads, 1, TILE), lambda i: (0, 0, i)),
        ],
        out_shape=[
            jax.ShapeDtypeStruct((parts, heads, size, part_length), bf16),
            jax.ShapeDtypeStruct((heads, 1, length), f32),
        ],
        scratch_shapes=[
            pltpu.VMEM((heads, size, length), bf16),
            pltpu.VMEM((heads, length, size), bf16),
            pltpu.VMEM((heads, size, length), bf16),
            pltpu.VMEM((heads, size, TILE), f32),
            pltpu.VMEM((2, heads, 1, TILE), f32),
        ],
        compiler_params=params(),
        name="attend_forward",
    )(full, most, slots, group, *pieces, bias, end)


def backward_kernel(least_ref, clear_ref, slot_ref, group_ref, *refs):
    parts = slot_ref.shape[0]
    pieces, grads = refs[:parts], refs[parts : 2 * parts]
    (
        ot_ref, lse_ref, bias_ref, end_ref, out_ref, band_out_ref,
        qt_ref, kt_ref, vt_ref, got_ref, q_ref, go_ref,
        dqt_acc, dk_acc, dv_acc, delta_ref, band_ref,
    ) = refs[2 * parts :]
    heads, size, length = qt_ref.shape
    count = length // TILE
    each = count // parts
    part_length = length // parts
    key = pl.program_id(0)
    key_cols = pl.ds(pl.multiple_of(key * TILE, TILE), TILE)

    @pl.when(key == 0)
    def _():
        dqt_acc[...] = jnp.zeros_like(dqt_acc)
        band_ref[...] = jnp.zeros_like(band_ref)
        for i, piece in enumerate(pieces):
            places = pl.ds(pl.multiple_of(slot_ref[i] * part_length, TILE), part_length)
            for h in range(heads):
                qt_ref[h, :, places] = piece[h]
                q_ref[h, places, :] = piece[h].T
                kt_ref[h, :, places] = piece[heads + h]
                vt_ref[h, :, places] = piece[2 * heads + h]
        for turn, grad_piece in enumerate(grads):
            part = lax.rem(group_ref[0] + turn, parts)
            places = pl.ds(pl.multiple_of(part * part_length, TILE), part_length)
            for h in range(heads):
                grad = grad_piece[h]
                got_ref[h, :, places] = grad
                go_ref[h, places, :] = grad.T
                delta_ref[h, :, places] = jnp.sum(
                    ot_ref[turn, h].astype(f32) * grad.astype(f32), axis=0, keepdims=True
                )

    dk_acc[...] = jnp.zeros_like(dk_acc)
    dv_acc[...] = jnp.zeros_like(dv_acc)
    kt = [kt_ref[h, :, key_cols] for h in range(heads)]
    k = [tile.T for tile in kt]
    v = [vt_ref[h, :, key_cols].T for h in range(heads)]

    def step(query, masked):
        cols = pl.ds(pl.multiple_of(query * TILE, TILE), TILE)
        if masked:
            keep = lax.broadcasted_iota(jnp.int32, (TILE, TILE), 0) + key * TILE < end_ref[:, cols]
        place = key - query + count - 1
        for h in range(heads):
            scores = dot(k[h], qt_ref[h, :, cols])
            scores = scores + bias_ref[h, place]
            if masked:
                scores = jnp.where(keep, scores, MASKED)
            weights = jnp.exp(scores - lse_ref[h, :, cols])
            grad_weights = dot(v[h], got_ref[h, :, cols])
            grad_scores = weights * (grad_weights - delta_ref[h, :, cols])
            rounded = grad_scores.astype(bf16)
            band_ref[h, place] += grad_scores
            dv_acc[h] += dot(weights.astype(bf16), go_ref[h, cols, :])
            dk_acc[h] += dot(rounded, q_ref[h, cols, :])
            dqt_acc[h, :, cols] += dot(kt[h], rounded)

    def edge_step(query, _):
        step(query, True)
        return 0

    def full_step(query, _):
        step(query, False)
        return 0

    lax.fori_loop(least_ref[key], clear_ref[key], edge_step, 0)
    lax.fori_loop(clear_ref[key], count, full_step, 0)
    slot = jnp.int32(0)
    for i in range(parts):
        slot = jnp.where(slot_ref[i] == key // each, i, slot)
    inner = pl.ds(pl.multiple_of(lax.rem(key, each) * TILE, TILE), TILE)
    for h in range(heads):
        out_ref[slot, heads + h, :, inner] = dk_acc[h].T.astype(bf16)
        out_ref[slot, 2 * heads + h, :, inner] = dv_acc[h].T.astype(bf16)

    @pl.when(key == count - 1)
    def _():
        for i in range(parts):
            places = pl.ds(pl.multiple_of(slot_ref[i] * part_length, TILE), part_length)
            for h in range(heads):
                out_ref[i, h] = dqt_acc[h, :, places].astype(bf16)

        def one(place, _):
            for h in range(heads):
                band = band_ref[h, place]
                zero = jnp.zeros((TILE // 2, TILE // 2), f32)
                upper, lower = band[: TILE // 2], band[TILE // 2 :]
                lines = jnp.concatenate([zero, zero, upper], axis=1) + jnp.concatenate(
                    [zero, lower, zero], axis=1
                )
                half = TILE // 4
                while half >= 8:
                    lines = lines[:half] + pltpu.roll(lines[half:], 2 * TILE - half, 1)
                    half //= 2
                total = lines[0:1]
                for row in range(1, 8):
                    total = total + pltpu.roll(lines[row : row + 1], 2 * TILE - row, 1)
                band_out_ref[h, place] = total
            return 0

        lax.fori_loop(0, band_ref.shape[1], one, 0)


def attend_backward(pieces, grads, ot, lse, bias, end, least, clear, slots, group):
    parts = len(pieces)
    triple, size, part_length = pieces[0].shape
    heads, length = triple // 3, parts * part_length
    count = length // TILE
    tiles = bias.shape[1]
    smem = pl.BlockSpec(memory_space=pltpu.SMEM)
    operands = (*pieces, *grads, ot, lse, bias, end)
    outs = [((parts, triple, size, part_length), bf16), ((heads, tiles, 1, 2 * TILE), f32)]
    by_columns = pltpu.VMEM((heads, size, length), bf16)
    by_rows = pltpu.VMEM((heads, length, size), bf16)
    return pl.pallas_call(
        backward_kernel,
        grid=(count,),
        in_specs=[smem] * 4 + [whole(a.shape) for a in operands],
        out_specs=[whole(shape) for shape, _ in outs],
        out_shape=[jax.ShapeDtypeStruct(shape, kind) for shape, kind in outs],
        scratch_shapes=[by_columns] * 4
        + [by_rows] * 2
        + [
            pltpu.VMEM((heads, size, length), f32),
            pltpu.VMEM((heads, TILE, size), f32),
            pltpu.VMEM((heads, TILE, size), f32),
            pltpu.VMEM((heads, 1, length), f32),
            pltpu.VMEM((heads, tiles, TILE, TILE), f32),
        ],
        compiler_params=params(),
        name="attend_backward",
    )(least, clear, slots, group, *operands)


def middle_kernel(place_ref, *refs):
    parts = place_ref.shape[0] - 1
    mixes = refs[:parts]
    x_ref, g_ref, gain_ref, own_ref, other_ref, out_ref, gh_ref, gain_grad_ref = refs[
        parts : parts + 8
    ]
    gots = refs[parts + 8 : 2 * parts + 8]
    keep_ref, send_ref, w_ref, grad_ref, second_ref, acc_ref, back_ref, load_sem, store_sem = refs[
        2 * parts + 8 :
    ]
    core = place_ref[parts]
    width = x_ref.shape[1]
    columns = mixes[0].shape[0]
    feed = own_ref.shape[3] - 256
    hidden_units = feed // 2
    late, early = pl.ds(feed, 256), pl.ds(0, feed)

    def loads(z, which, cols):
        pairs = [(own_ref, core), (other_ref, 1 - core)]
        return [
            pltpu.make_async_copy(
                src.at[z, :, :, cols], w_ref.at[z, :, at, :, cols], load_sem.at[z, which, i]
            )
            for i, (src, at) in enumerate(pairs)
        ]

    def stores(z, which, cols):
        pairs = [(keep_ref, core), (send_ref, 1 - core)]
        return [
            pltpu.make_async_copy(
                grad_ref.at[z, :, at, :, cols], dst.at[z, :, :, cols], store_sem.at[z, which, i]
            )
            for i, (dst, at) in enumerate(pairs)
        ]

    for z in range(parts):
        for copy in loads(z, 0, late):
            copy.start()
    for z in range(parts):
        for copy in loads(z, 1, early):
            copy.start()
    for z in range(parts):
        for copy in loads(z, 0, late):
            copy.wait()

    def output_rows(turn):
        return w_ref[place_ref[turn], :, :, :, feed : feed + columns].reshape(width, columns)

    hidden = x_ref[...].astype(f32)
    for turn in range(parts):
        hidden = hidden + dot(mixes[turn][...], output_rows(turn), ((0,), (1,)))
    inverse = lax.rsqrt(jnp.mean(hidden * hidden, axis=-1, keepdims=True) + EPSILON)
    second_ref[...] = (hidden * inverse * gain_ref[...]).astype(bf16)
    acc_ref[...] = hidden
    back_ref[...] = jnp.zeros_like(back_ref)
    gh_ref[...] = hidden * inverse

    def hidden_part(z, _):
        for copy in loads(z, 1, early):
            copy.wait()
        inner = w_ref[z, :, :, :, :hidden_units].reshape(width, hidden_units)
        outer = w_ref[z, :, :, :, hidden_units:feed].reshape(width, hidden_units)
        second = second_ref[...]
        grad = g_ref[...]
        grad_active = dot(grad, outer).astype(bf16).astype(f32)
        active, slope = gelu_parts(dot(second, inner))
        active = active.astype(bf16)
        grad_units = (grad_active * slope).astype(bf16)
        acc_ref[...] += dot(active, outer, ((1,), (1,)))
        back_ref[...] += dot(grad_units, inner, ((1,), (1,)))
        shape = (*grad_ref.shape[1:4], hidden_units)
        grad_ref[z, :, :, :, :hidden_units] = (
            dot(second, grad_units, ((0,), (0,))).astype(bf16).reshape(shape)
        )
        grad_ref[z, :, :, :, hidden_units:feed] = (
            dot(grad, active, ((0,), (0,))).astype(bf16).reshape(shape)
        )
        for copy in stores(z, 1, early):
            copy.start()
        return 0

    lax.fori_loop(0, parts, hidden_part, 0)
    out_ref[...] = acc_ref[...].astype(bf16)
    scaled = gh_ref[...]
    grad_second = back_ref[...]
    gain_grad_ref[...] = jnp.sum(grad_second * scaled, axis=0, keepdims=True)
    grad_scaled = grad_second * gain_ref[...]
    grad_hidden = g_ref[...].astype(f32) + inverse * (
        grad_scaled - scaled * jnp.mean(grad_scaled * scaled, axis=-1, keepdims=True)
    )
    gh_ref[...] = grad_hidden
    rounded = grad_hidden.astype(bf16)
    for turn in range(parts):
        gots[turn][...] = dot(output_rows(turn), rounded, ((0,), (1,))).astype(bf16)
        grads = dot(rounded, mixes[turn][...], ((0,), (1,))).astype(bf16)
        grad_ref[place_ref[turn], :, :, :, feed : feed + columns] = grads.reshape(
            *grad_ref.shape[1:4], columns
        )
        grad_ref[place_ref[turn], :, :, :, feed + columns :] = jnp.zeros(
            (*grad_ref.shape[1:4], 256 - columns), bf16
        )
    for z in range(parts):
        for copy in stores(z, 0, late):
            copy.start()
    for z in range(parts):
        for copy in stores(z, 0, late) + stores(z, 1, early):
            copy.wait()


def middle(place, mixes, inputs, cotangent, gain, own, other):
    rows, width = inputs.shape
    parts, planes, each, columns = own.shape
    smem = pl.BlockSpec(memory_space=pltpu.SMEM)
    hbm = pl.BlockSpec(memory_space=pl.ANY)
    held = pltpu.VMEM((parts, planes, 2, each, columns), bf16)
    token_shape = jax.ShapeDtypeStruct((rows, width), f32)
    gain = gain.reshape(1, width)
    dense = [*mixes, inputs, cotangent, gain]
    outs = [
        jax.ShapeDtypeStruct((rows, width), bf16),
        token_shape,
        jax.ShapeDtypeStruct((1, width), f32),
        *[jax.ShapeDtypeStruct(mix.shape, bf16) for mix in mixes],
    ]
    return pl.pallas_call(
        middle_kernel,
        in_specs=[smem] + [whole(a.shape) for a in dense] + [hbm, hbm],
        out_specs=[whole(a.shape) for a in outs] + [hbm, hbm],
        out_shape=outs + [jax.ShapeDtypeStruct(own.shape, bf16)] * 2,
        scratch_shapes=[
            held,
            held,
            pltpu.VMEM((rows, width), bf16),
            pltpu.VMEM((rows, width), f32),
            pltpu.VMEM((rows, width), f32),
            pltpu.SemaphoreType.DMA((parts, 2, 2)),
            pltpu.SemaphoreType.DMA((parts, 2, 2)),
        ],
        compiler_params=params(),
        name="middle",
    )(place, *dense, own, other)


def flat(pairs, parts):
    return [(c * parts + z, d * parts + y) for (c, z), (d, y) in pairs]


def routes(parts):
    half = parts // 2
    devices = [(c, z) for c in range(2) for z in range(parts)]

    def group(c, z):
        return (z % half) * 2 + c

    gather = [
        flat([((0, z), (0, z - 1)) for z in (1, 2, 3)] + [((1, z), (1, z + 1)) for z in (0, 1, 2)], parts),
        flat([((0, z), (0, z - 1)) for z in (1, 2)] + [((1, z), (1, z + 1)) for z in (1, 2)], parts),
        flat([((0, 1), (0, 0)), ((0, 0), (0, 1)), ((1, 2), (1, 3)), ((1, 3), (1, 2))], parts),
    ]
    rounds = [
        flat([((c, z), (z // half, (group(c, z) + r) % parts)) for c, z in devices], parts)
        for r in range(parts)
    ]
    weights = [
        flat([((z // half ^ flip, group(c, z)), (c, z)) for c, z in devices], parts)
        for flip in range(2)
    ]
    return gather, rounds, weights


def back(pairs):
    return [(target, source) for source, target in pairs]


SWAP = [(0, 1), (1, 0)]
LINE = ("core", "tensor")
EVERY = ("tensor", "plane")


def body(
    inputs,
    attention_gain,
    feedforward_gain,
    query_weight,
    key_weight,
    value_weight,
    output_weight,
    inner_weight,
    outer_weight,
    bias_table,
    block_index,
    position_bucket,
    cotangent,
):
    length = block_index.shape[1]
    parts = lax.axis_size("tensor")
    planes = lax.axis_size("plane")
    factor = 1.0 / math.sqrt(block_index.shape[0] * length * planes * 2)
    heads = bias_table.shape[1]
    width = inputs.shape[1]
    size = query_weight.shape[1] // heads
    columns = heads * size
    each = query_weight.shape[0]
    hidden_units = inner_weight.shape[1]
    core, z = lax.axis_index("core"), lax.axis_index("tensor")
    half = parts // 2
    lower = z < half
    owner = core == z // half
    outer_chip = (z == 0) | (z == parts - 1)
    group = (z % half) * 2 + core
    gather, rounds, weight_routes = routes(parts)
    slots = jnp.array([[0, 1, 2, 3], [1, 2, 3, 0], [2, 1, 0, 3], [3, 2, 1, 0]], jnp.int32)[z]

    def swap(value):
        return lax.ppermute(value, "core", SWAP)

    inputs_wide = inputs.astype(f32)
    scaled_first, inverse_first, normed_own = norm_forward(inputs_wide, attention_gain)
    first = lax.ppermute(normed_own, LINE, gather[0])
    second = lax.ppermute(first, LINE, gather[1])
    third = lax.ppermute(jnp.where(outer_chip, normed_own, second), LINE, gather[2])
    normed = [jnp.where(owner, piece, swap(piece)) for piece in (normed_own, first, second, third)]

    packed = jnp.concatenate([query_weight, key_weight, value_weight], axis=1)
    one, two = (lax.ppermute(packed, LINE, route) for route in weight_routes)
    mine = jnp.concatenate([jnp.where(lower, one, two), jnp.where(lower, two, one)], axis=0)
    attention_full = lax.all_gather(mine, "plane", axis=0, tiled=True)
    table = lax.ppermute(bias_table, LINE, weight_routes[0])
    block_row = jnp.where(owner, block_index, swap(block_index))[0]

    pad = jnp.zeros((each, 256 - columns), bf16)
    packed_rest = jnp.concatenate([inner_weight, outer_weight.T, output_weight.T, pad], axis=1)
    own_rest = lax.all_gather(packed_rest, EVERY, axis=0).reshape(parts, planes, each, -1)
    other_rest = swap(own_rest)

    rows, onehot = bias_rows(table, position_bucket)
    bias = bias_tiles(rows, length)
    end, full, most, least, clear = spans(block_row)
    group_ref = group.reshape(1)

    pieces = [
        dot(attention_full, piece, ((0,), (1,))).astype(bf16).reshape(3 * heads, size, -1)
        for piece in normed
    ]
    ot, lse = attend_forward(pieces, bias, end, full, most, slots, group_ref)
    mixes = [
        lax.ppermute(ot[r].reshape(columns, -1), LINE, rounds[r]) for r in range(parts)
    ]
    place = jnp.stack([(z - r) % parts for r in range(parts)] + [core]).astype(jnp.int32)
    aligned = each % 16 == 0
    if aligned:
        outs = middle(place, mixes, inputs, cotangent, feedforward_gain, own_rest, other_rest)
        layer_output, grad_hidden, feedforward_part, *gots, keep, send = outs
    else:
        low, high = jnp.where(core == 0, own_rest, other_rest), jnp.where(core == 0, other_rest, own_rest)
        both = jnp.stack([low, high], axis=2).reshape(parts, 2, width // 2, -1)
        lone = place.at[parts].set(0)
        outs = middle(lone, mixes, inputs, cotangent, feedforward_gain, both[:, :1], both[:, 1:])
        layer_output, grad_hidden, feedforward_part, *gots, keep, send = outs
        grads = jnp.concatenate([keep, send], axis=1).reshape(parts, planes, 2, each, -1)
        keep, send = (
            lax.dynamic_index_in_dim(grads, at, 2, False) for at in (core, 1 - core)
        )
    rest = (keep + swap(send)).reshape(parts * planes, each, -1)
    rest_share = lax.psum_scatter(rest, EVERY, scatter_dimension=0).astype(f32) * factor

    gots = [lax.ppermute(got, LINE, back(rounds[r])) for r, got in enumerate(gots)]
    gots = [got.reshape(heads, size, -1) for got in gots]
    dqkv, bands = attend_backward(
        pieces, gots, ot, lse, bias, end, least, clear, slots, group_ref
    )
    dqkv = dqkv.reshape(parts, 3 * columns, length // parts)

    def normed_part(i):
        part = dot(dqkv[i], attention_full, ((0,), (1,))).astype(bf16)
        return part + swap(part)

    third, second, first, own = (normed_part(i) for i in (3, 2, 1, 0))
    none = jnp.zeros_like(own)
    got = lax.ppermute(third, LINE, back(gather[2]))
    own = jnp.where(owner, jnp.where(outer_chip, own + got, own), none)
    second = jnp.where(outer_chip, second, second + got)
    got = lax.ppermute(second, LINE, back(gather[1]))
    first = jnp.where(owner, first, none) + got
    got = lax.ppermute(first, LINE, back(gather[0]))
    grad_first = (own + got).astype(f32)
    input_grad = (
        grad_hidden + norm_backward(grad_first, scaled_first, inverse_first, attention_gain)
    ).astype(bf16)

    attention_grads = sum(dot(normed[i], dqkv[i], ((0,), (1,))) for i in range(parts))
    attention_part = (
        jnp.sum(attention_grads * attention_full.astype(f32), axis=1) / attention_gain
    )
    shared = lax.psum_scatter(
        attention_grads.astype(bf16), "plane", scatter_dimension=0, tiled=True
    )
    low, high = shared[:each], shared[each:]
    attention_share = (
        lax.ppermute(jnp.where(lower, low, high), LINE, back(weight_routes[0]))
        + lax.ppermute(jnp.where(lower, high, low), LINE, back(weight_routes[1]))
    ).astype(f32) * factor

    table_local = table_part(bands, onehot, length)
    buckets = table_local.shape[0]
    table_whole = lax.dynamic_update_slice(
        jnp.zeros((buckets, H), f32), table_local, (jnp.zeros((), jnp.int32), group * heads)
    )
    small = jnp.concatenate(
        [attention_part, feedforward_part.reshape(width), table_whole.reshape(buckets * H)]
    )
    for axis, count in (("core", 2), ("tensor", parts), ("plane", planes)):
        step = 1
        while step < count:
            small = small + lax.ppermute(small, axis, [(i, i ^ step) for i in range(count)])
            step *= 2
    small = small * factor

    return (
        layer_output,
        input_grad,
        small[:width],
        small[width : 2 * width],
        attention_share[:, :columns],
        attention_share[:, columns : 2 * columns],
        attention_share[:, 2 * columns :],
        rest_share[:, 2 * hidden_units : 2 * hidden_units + columns].T,
        rest_share[:, :hidden_units],
        rest_share[:, hidden_units : 2 * hidden_units].T,
        small[2 * width :].reshape(buckets, H),
    )


def solution(mesh):
    groups, parts = mesh.devices.shape
    fine = Mesh(mesh.devices.reshape(groups // 2, 2, parts), ("plane", "core", "tensor"))
    dp = ("plane", "core")
    tokens = P(("plane", "core", "tensor"), None)
    by_rows = P(dp, "tensor")
    by_columns = P("tensor", dp)
    placed = (
        tokens, P(), P(), by_rows, by_rows, by_rows, by_columns, by_rows, by_columns,
        P(None, "tensor"), P(dp, None), P(), tokens,
    )
    results = (
        tokens, tokens, P(), P(), by_rows, by_rows, by_rows, by_columns, by_rows, by_columns, P(),
    )
    return jax.shard_map(body, mesh=fine, in_specs=placed, out_specs=results, check_vma=False)
```

```python
import math

import jax
import jax.numpy as jnp
from jax import lax
from jax.experimental import pallas as pl
from jax.experimental.pallas import tpu as pltpu
from jax.sharding import Mesh, PartitionSpec as P

H = 12
EPSILON = 1e-06
MASKED = -1e30
TILE = 256
AHEAD = 2
BLOCKS = 8
VMEM_LIMIT = 60 * 1024 * 1024
f32, bf16 = jnp.float32, jnp.bfloat16


def dot(left, right, contract=((1,), (0,))):
    return lax.dot_general(left, right, (contract, ((), ())), preferred_element_type=f32)


def norm_forward(values, gain):
    inverse = lax.rsqrt(jnp.mean(values * values, axis=-1, keepdims=True) + EPSILON)
    scaled = values * inverse
    return scaled, inverse, (scaled * gain).astype(bf16)


def norm_backward(grad_normed, scaled, inverse, gain):
    grad_scaled = grad_normed * gain
    return inverse * (
        grad_scaled - scaled * jnp.mean(grad_scaled * scaled, axis=-1, keepdims=True)
    )


def gelu_parts(values):
    cumulative = 0.5 * (1.0 + lax.erf(values * (1.0 / math.sqrt(2.0))))
    density = jnp.exp(-0.5 * values * values) * (1.0 / math.sqrt(2.0 * math.pi))
    return values * cumulative, cumulative + values * density


def whole(shape):
    return pl.BlockSpec(shape, lambda *_: (0,) * len(shape), pipeline_mode=pl.Buffered(1))


def params():
    return pltpu.CompilerParams(vmem_limit_bytes=VMEM_LIMIT)


def bias_rows(bias_table, position_bucket):
    bucket = jnp.concatenate([position_bucket, jnp.zeros((1,), jnp.int32)])[::-1]
    names = jnp.arange(bias_table.shape[0], dtype=jnp.int32)
    onehot = (bucket[None, :] == names[:, None]).astype(f32)
    rows = lax.dot_general(
        bias_table, onehot, (((0,), (0,)), ((), ())), precision=lax.Precision.HIGHEST
    )
    return rows[:, None, :], onehot


def bias_kernel(row_ref, out_ref):
    tiles = out_ref.shape[1]

    def one(place, _):
        start = pl.multiple_of((tiles - 1 - place) * TILE, TILE)
        piece = row_ref[0, :, pl.ds(start, 2 * TILE)]
        spread = jnp.broadcast_to(piece, (TILE, 2 * TILE))
        out_ref[0, place] = pltpu.roll(spread, 0, 1, stride=1, stride_axis=0)[:, TILE:]
        return 0

    lax.fori_loop(0, tiles, one, 0)


def bias_tiles(rows, length):
    heads = rows.shape[0]
    count = length // TILE
    rows = rows[:, :, (count - 1 - AHEAD) * TILE :]
    tiles = count + AHEAD
    return pl.pallas_call(
        bias_kernel,
        grid=(heads,),
        in_specs=[pl.BlockSpec((1, 1, rows.shape[2]), lambda h: (h, 0, 0))],
        out_specs=pl.BlockSpec((1, tiles, TILE, TILE), lambda h: (h, 0, 0, 0)),
        out_shape=jax.ShapeDtypeStruct((heads, tiles, TILE, TILE), f32),
        compiler_params=params(),
        name="bias_tiles",
    )(rows)


def table_part(bands, onehot, length):
    heads, tiles = bands.shape[:2]
    pieces = bands[:, ::-1, 0, :]
    pad = jnp.zeros((heads, 1, TILE), f32)
    line = jnp.concatenate([pieces[:, :, :TILE], pad], 1) + jnp.concatenate(
        [pad, pieces[:, :, TILE:]], 1
    )
    line = line.reshape(heads, (tiles + 1) * TILE)
    base = (length // TILE - 1 - AHEAD) * TILE
    return lax.dot_general(
        onehot[:, base : base + line.shape[1]],
        line,
        (((1,), (1,)), ((), ())),
        precision=lax.Precision.HIGHEST,
    )


def spans(block_row):
    length = block_row.shape[0]
    names = jnp.arange(BLOCKS, dtype=jnp.int32)[:, None]
    upto = jnp.sum(block_row[None, :] <= names, axis=1, dtype=jnp.int32)
    end = jnp.sum(jnp.where(block_row[None, :] == names, upto[:, None], 0), axis=0, dtype=jnp.int32)
    by_tile = end.reshape(length // TILE, TILE)
    full = by_tile[:, 0] // TILE
    most = (by_tile[:, TILE - 1] + TILE - 1) // TILE
    places = jnp.arange(length // TILE, dtype=jnp.int32)[:, None]
    least = jnp.sum(most[None, :] <= places, axis=1, dtype=jnp.int32)
    clear = jnp.sum(full[None, :] <= places, axis=1, dtype=jnp.int32)
    return end.reshape(1, length), full, most, least, clear


def forward_kernel(full_ref, most_ref, slot_ref, group_ref, *refs):
    parts = slot_ref.shape[0]
    pieces = refs[:parts]
    bias_ref, end_ref, ot_ref, lse_ref, qt_ref, k_ref, vt_ref, acc_ref, stat_ref = refs[parts:]
    heads, size, length = qt_ref.shape
    count = length // TILE
    each = count // parts
    query = pl.program_id(0)

    @pl.when(query == 0)
    def _():
        for i, piece in enumerate(pieces):
            places = pl.ds(pl.multiple_of(slot_ref[i] * (length // parts), TILE), length // parts)
            for h in range(heads):
                qt_ref[h, :, places] = piece[h]
                k_ref[h, places, :] = piece[heads + h].T
                vt_ref[h, :, places] = piece[2 * heads + h]

    own = pl.ds(pl.multiple_of(query * TILE, TILE), TILE)
    acc_ref[...] = jnp.zeros_like(acc_ref)
    stat_ref[0] = jnp.full(stat_ref.shape[1:], -jnp.inf, f32)
    stat_ref[1] = jnp.zeros(stat_ref.shape[1:], f32)

    def step(key, masked):
        start = pl.multiple_of(key * TILE, TILE)
        if masked:
            keep = lax.broadcasted_iota(jnp.int32, (TILE, TILE), 0) + start < end_ref[...]
        for h in range(heads):
            scores = dot(k_ref[h, pl.ds(start, TILE), :], qt_ref[h, :, own])
            scores = scores + bias_ref[h, key - query + count - 1]
            if masked:
                scores = jnp.where(keep, scores, MASKED)
            old = stat_ref[0, h]
            new = jnp.maximum(old, jnp.max(scores, axis=0, keepdims=True))
            weights = jnp.exp(scores - new)
            scale = jnp.exp(old - new)
            stat_ref[0, h] = new
            stat_ref[1, h] = stat_ref[1, h] * scale + jnp.sum(weights, axis=0, keepdims=True)
            acc_ref[h] = acc_ref[h] * scale + dot(
                vt_ref[h, :, pl.ds(start, TILE)], weights.astype(bf16)
            )

    def full_step(key, _):
        step(key, False)
        return 0

    def edge_step(key, _):
        step(key, True)
        return 0

    lax.fori_loop(0, full_ref[query], full_step, 0)
    lax.fori_loop(full_ref[query], most_ref[query], edge_step, 0)
    turn = lax.rem(query // each - group_ref[0] + parts, parts)
    inner = pl.ds(pl.multiple_of(lax.rem(query, each) * TILE, TILE), TILE)
    for h in range(heads):
        total = stat_ref[1, h]
        ot_ref[turn, h, :, inner] = (acc_ref[h] * (1.0 / total)).astype(bf16)
        lse_ref[h] = stat_ref[0, h] + jnp.log(total)


def attend_forward(pieces, bias, end, full, most, slots, group):
    parts = len(pieces)
    triple, size, part_length = pieces[0].shape
    heads, length = triple // 3, parts * part_length
    count = length // TILE
    smem = pl.BlockSpec(memory_space=pltpu.SMEM)
    return pl.pallas_call(
        forward_kernel,
        grid=(count,),
        in_specs=[smem] * 4
        + [whole(piece.shape) for piece in pieces]
        + [whole(bias.shape), pl.BlockSpec((1, TILE), lambda i: (0, i))],
        out_specs=[
            whole((parts, heads, size, part_length)),
            pl.BlockSpec((heads, 1, TILE), lambda i: (0, 0, i)),
        ],
        out_shape=[
            jax.ShapeDtypeStruct((parts, heads, size, part_length), bf16),
            jax.ShapeDtypeStruct((heads, 1, length), f32),
        ],
        scratch_shapes=[
            pltpu.VMEM((heads, size, length), bf16),
            pltpu.VMEM((heads, length, size), bf16),
            pltpu.VMEM((heads, size, length), bf16),
            pltpu.VMEM((heads, size, TILE), f32),
            pltpu.VMEM((2, heads, 1, TILE), f32),
        ],
        compiler_params=params(),
        name="attend_forward",
    )(full, most, slots, group, *pieces, bias, end)


def backward_kernel(least_ref, clear_ref, slot_ref, group_ref, *refs):
    parts = slot_ref.shape[0]
    pieces, grads = refs[:parts], refs[parts : 2 * parts]
    (
        ot_ref, lse_ref, bias_ref, end_ref, out_ref, band_out_ref,
        qt_ref, kt_ref, vt_ref, got_ref, q_ref, go_ref,
        dqt_acc, dk_acc, dv_acc, delta_ref, band_ref,
    ) = refs[2 * parts :]
    heads, size, length = qt_ref.shape
    count = length // TILE
    each = count // parts
    part_length = length // parts
    key = pl.program_id(0)
    key_cols = pl.ds(pl.multiple_of(key * TILE, TILE), TILE)

    @pl.when(key == 0)
    def _():
        dqt_acc[...] = jnp.zeros_like(dqt_acc)
        band_ref[...] = jnp.zeros_like(band_ref)
        for i, piece in enumerate(pieces):
            places = pl.ds(pl.multiple_of(slot_ref[i] * part_length, TILE), part_length)
            for h in range(heads):
                qt_ref[h, :, places] = piece[h]
                q_ref[h, places, :] = piece[h].T
                kt_ref[h, :, places] = piece[heads + h]
                vt_ref[h, :, places] = piece[2 * heads + h]
        for turn, grad_piece in enumerate(grads):
            part = lax.rem(group_ref[0] + turn, parts)
            places = pl.ds(pl.multiple_of(part * part_length, TILE), part_length)
            for h in range(heads):
                grad = grad_piece[h]
                got_ref[h, :, places] = grad
                go_ref[h, places, :] = grad.T
                delta_ref[h, :, places] = jnp.sum(
                    ot_ref[turn, h].astype(f32) * grad.astype(f32), axis=0, keepdims=True
                )

    dk_acc[...] = jnp.zeros_like(dk_acc)
    dv_acc[...] = jnp.zeros_like(dv_acc)
    kt = [kt_ref[h, :, key_cols] for h in range(heads)]
    k = [tile.T for tile in kt]
    v = [vt_ref[h, :, key_cols].T for h in range(heads)]

    def step(query, masked):
        cols = pl.ds(pl.multiple_of(query * TILE, TILE), TILE)
        if masked:
            keep = lax.broadcasted_iota(jnp.int32, (TILE, TILE), 0) + key * TILE < end_ref[:, cols]
        place = key - query + count - 1
        for h in range(heads):
            scores = dot(k[h], qt_ref[h, :, cols])
            scores = scores + bias_ref[h, place]
            if masked:
                scores = jnp.where(keep, scores, MASKED)
            weights = jnp.exp(scores - lse_ref[h, :, cols])
            grad_weights = dot(v[h], got_ref[h, :, cols])
            grad_scores = weights * (grad_weights - delta_ref[h, :, cols])
            rounded = grad_scores.astype(bf16)
            band_ref[h, place] += grad_scores
            dv_acc[h] += dot(weights.astype(bf16), go_ref[h, cols, :])
            dk_acc[h] += dot(rounded, q_ref[h, cols, :])
            dqt_acc[h, :, cols] += dot(kt[h], rounded)

    def edge_step(query, _):
        step(query, True)
        return 0

    def full_step(query, _):
        step(query, False)
        return 0

    lax.fori_loop(least_ref[key], clear_ref[key], edge_step, 0)
    lax.fori_loop(clear_ref[key], count, full_step, 0)
    slot = jnp.int32(0)
    for i in range(parts):
        slot = jnp.where(slot_ref[i] == key // each, i, slot)
    inner = pl.ds(pl.multiple_of(lax.rem(key, each) * TILE, TILE), TILE)
    for h in range(heads):
        out_ref[slot, heads + h, :, inner] = dk_acc[h].T.astype(bf16)
        out_ref[slot, 2 * heads + h, :, inner] = dv_acc[h].T.astype(bf16)

    @pl.when(key == count - 1)
    def _():
        for i in range(parts):
            places = pl.ds(pl.multiple_of(slot_ref[i] * part_length, TILE), part_length)
            for h in range(heads):
                out_ref[i, h] = dqt_acc[h, :, places].astype(bf16)

        def one(place, _):
            for h in range(heads):
                band = band_ref[h, place]
                zero = jnp.zeros((TILE // 2, TILE // 2), f32)
                upper, lower = band[: TILE // 2], band[TILE // 2 :]
                lines = jnp.concatenate([zero, zero, upper], axis=1) + jnp.concatenate(
                    [zero, lower, zero], axis=1
                )
                half = TILE // 4
                while half >= 8:
                    lines = lines[:half] + pltpu.roll(lines[half:], 2 * TILE - half, 1)
                    half //= 2
                total = lines[0:1]
                for row in range(1, 8):
                    total = total + pltpu.roll(lines[row : row + 1], 2 * TILE - row, 1)
                band_out_ref[h, place] = total
            return 0

        lax.fori_loop(0, band_ref.shape[1], one, 0)


def attend_backward(pieces, grads, ot, lse, bias, end, least, clear, slots, group):
    parts = len(pieces)
    triple, size, part_length = pieces[0].shape
    heads, length = triple // 3, parts * part_length
    count = length // TILE
    tiles = bias.shape[1]
    smem = pl.BlockSpec(memory_space=pltpu.SMEM)
    operands = (*pieces, *grads, ot, lse, bias, end)
    outs = [((parts, triple, size, part_length), bf16), ((heads, tiles, 1, 2 * TILE), f32)]
    by_columns = pltpu.VMEM((heads, size, length), bf16)
    by_rows = pltpu.VMEM((heads, length, size), bf16)
    return pl.pallas_call(
        backward_kernel,
        grid=(count,),
        in_specs=[smem] * 4 + [whole(a.shape) for a in operands],
        out_specs=[whole(shape) for shape, _ in outs],
        out_shape=[jax.ShapeDtypeStruct(shape, kind) for shape, kind in outs],
        scratch_shapes=[by_columns] * 4
        + [by_rows] * 2
        + [
            pltpu.VMEM((heads, size, length), f32),
            pltpu.VMEM((heads, TILE, size), f32),
            pltpu.VMEM((heads, TILE, size), f32),
            pltpu.VMEM((heads, 1, length), f32),
            pltpu.VMEM((heads, tiles, TILE, TILE), f32),
        ],
        compiler_params=params(),
        name="attend_backward",
    )(least, clear, slots, group, *operands)


def middle_kernel(turn_ref, *refs):
    parts = turn_ref.shape[0]
    mixes = refs[:parts]
    x_ref, g_ref, gain_ref, weight_ref, out_ref, gh_ref, gain_grad_ref = refs[parts : parts + 7]
    gots = refs[parts + 7 : 2 * parts + 7]
    grads_ref, w_ref, grad_ref, second_ref, acc_ref, back_ref, load_sem, store_sem = refs[
        2 * parts + 7 :
    ]
    width = x_ref.shape[1]
    columns = mixes[0].shape[0]
    feed = weight_ref.shape[3] - 256
    hidden_units = feed // 2
    late, early = pl.ds(feed, 256), pl.ds(0, feed)

    def load(z, which, cols):
        return pltpu.make_async_copy(
            weight_ref.at[:, z, :, cols], w_ref.at[z, :, :, cols], load_sem.at[z, which]
        )

    def store(z, which, cols):
        return pltpu.make_async_copy(
            grad_ref.at[z, :, :, cols], grads_ref.at[:, z, :, cols], store_sem.at[z, which]
        )

    for z in range(parts):
        load(z, 0, late).start()
    for z in range(parts):
        load(z, 1, early).start()
    for z in range(parts):
        load(z, 0, late).wait()

    def output_rows(turn):
        return w_ref[turn_ref[turn], :, :, feed : feed + columns].reshape(width, columns)

    hidden = x_ref[...].astype(f32)
    for turn in range(parts):
        hidden = hidden + dot(mixes[turn][...], output_rows(turn), ((0,), (1,)))
    inverse = lax.rsqrt(jnp.mean(hidden * hidden, axis=-1, keepdims=True) + EPSILON)
    second_ref[...] = (hidden * inverse * gain_ref[...]).astype(bf16)
    acc_ref[...] = hidden
    back_ref[...] = jnp.zeros_like(back_ref)
    gh_ref[...] = hidden * inverse

    def hidden_part(z, _):
        load(z, 1, early).wait()
        inner = w_ref[z, :, :, :hidden_units].reshape(width, hidden_units)
        outer = w_ref[z, :, :, hidden_units:feed].reshape(width, hidden_units)
        second = second_ref[...]
        grad = g_ref[...]
        grad_active = dot(grad, outer).astype(bf16).astype(f32)
        active, slope = gelu_parts(dot(second, inner))
        active = active.astype(bf16)
        grad_units = (grad_active * slope).astype(bf16)
        acc_ref[...] += dot(active, outer, ((1,), (1,)))
        back_ref[...] += dot(grad_units, inner, ((1,), (1,)))
        shape = (*grad_ref.shape[1:3], hidden_units)
        grad_ref[z, :, :, :hidden_units] = (
            dot(second, grad_units, ((0,), (0,))).astype(bf16).reshape(shape)
        )
        grad_ref[z, :, :, hidden_units:feed] = (
            dot(grad, active, ((0,), (0,))).astype(bf16).reshape(shape)
        )
        store(z, 1, early).start()
        return 0

    lax.fori_loop(0, parts, hidden_part, 0)
    out_ref[...] = acc_ref[...].astype(bf16)
    scaled = gh_ref[...]
    grad_second = back_ref[...]
    gain_grad_ref[...] = jnp.sum(grad_second * scaled, axis=0, keepdims=True)
    grad_scaled = grad_second * gain_ref[...]
    grad_hidden = g_ref[...].astype(f32) + inverse * (
        grad_scaled - scaled * jnp.mean(grad_scaled * scaled, axis=-1, keepdims=True)
    )
    gh_ref[...] = grad_hidden
    rounded = grad_hidden.astype(bf16)
    for turn in range(parts):
        gots[turn][...] = dot(output_rows(turn), rounded, ((0,), (1,))).astype(bf16)
        grads = dot(rounded, mixes[turn][...], ((0,), (1,))).astype(bf16)
        grad_ref[turn_ref[turn], :, :, feed : feed + columns] = grads.reshape(
            *grad_ref.shape[1:3], columns
        )
        grad_ref[turn_ref[turn], :, :, feed + columns :] = jnp.zeros(
            (*grad_ref.shape[1:3], 256 - columns), bf16
        )
    for z in range(parts):
        store(z, 0, late).start()
    for z in range(parts):
        store(z, 0, late).wait()
        store(z, 1, early).wait()


def middle(turns, mixes, inputs, cotangent, gain, weights):
    rows, width = inputs.shape
    owners, parts, each, columns = weights.shape
    smem = pl.BlockSpec(memory_space=pltpu.SMEM)
    hbm = pl.BlockSpec(memory_space=pl.ANY)
    held = pltpu.VMEM((parts, owners, each, columns), bf16)
    dense = [*mixes, inputs, cotangent, gain.reshape(1, width)]
    outs = [
        jax.ShapeDtypeStruct((rows, width), bf16),
        jax.ShapeDtypeStruct((rows, width), f32),
        jax.ShapeDtypeStruct((1, width), f32),
        *[jax.ShapeDtypeStruct(mix.shape, bf16) for mix in mixes],
    ]
    return pl.pallas_call(
        middle_kernel,
        in_specs=[smem] + [whole(a.shape) for a in dense] + [hbm],
        out_specs=[whole(a.shape) for a in outs] + [hbm],
        out_shape=outs + [jax.ShapeDtypeStruct(weights.shape, bf16)],
        scratch_shapes=[
            held,
            held,
            pltpu.VMEM((rows, width), bf16),
            pltpu.VMEM((rows, width), f32),
            pltpu.VMEM((rows, width), f32),
            pltpu.SemaphoreType.DMA((parts, 2)),
            pltpu.SemaphoreType.DMA((parts, 2)),
        ],
        compiler_params=params(),
        name="middle",
    )(turns, *dense, weights)


def flat(pairs, parts):
    return [(c * parts + z, d * parts + y) for (c, z), (d, y) in pairs]


def routes(parts):
    half = parts // 2
    devices = [(c, z) for c in range(2) for z in range(parts)]

    def group(c, z):
        return (z % half) * 2 + c

    gather = [
        flat([((0, z), (0, z - 1)) for z in (1, 2, 3)] + [((1, z), (1, z + 1)) for z in (0, 1, 2)], parts),
        flat([((0, z), (0, z - 1)) for z in (1, 2)] + [((1, z), (1, z + 1)) for z in (1, 2)], parts),
        flat([((0, 1), (0, 0)), ((0, 0), (0, 1)), ((1, 2), (1, 3)), ((1, 3), (1, 2))], parts),
    ]
    rounds = [
        flat([((c, z), (z // half, (group(c, z) + r) % parts)) for c, z in devices], parts)
        for r in range(parts)
    ]
    weights = [
        flat([((z // half ^ flip, group(c, z)), (c, z)) for c, z in devices], parts)
        for flip in range(2)
    ]
    return gather, rounds, weights


def back(pairs):
    return [(target, source) for source, target in pairs]


SWAP = [(0, 1), (1, 0)]
LINE = ("core", "tensor")


def after(value, *earlier):
    return lax.optimization_barrier((value, *earlier))[0]


def across(value, step):
    return lax.ppermute(value, "plane", [(i, i ^ step) for i in range(lax.axis_size("plane"))])


def planes_gathered(low, high):
    planes = lax.axis_size("plane")
    if planes != 4:
        return lax.all_gather(jnp.stack([low, high]), "plane", axis=0)
    low_x, high_y = across(low, 1), across(high, 2)
    low_y, high_x = across(low, 2), across(high, 1)
    low_xy, high_xy = across(low_x, 2), across(high_y, 1)
    pairs = jnp.stack(
        [jnp.stack(pair) for pair in ((low, high), (low_x, high_x), (low_y, high_y), (low_xy, high_xy))]
    )
    return pairs[jnp.arange(planes) ^ lax.axis_index("plane")]


def body(
    inputs,
    attention_gain,
    feedforward_gain,
    query_weight,
    key_weight,
    value_weight,
    output_weight,
    inner_weight,
    outer_weight,
    bias_table,
    block_index,
    position_bucket,
    cotangent,
):
    length = block_index.shape[1]
    parts = lax.axis_size("tensor")
    planes = lax.axis_size("plane")
    factor = 1.0 / math.sqrt(block_index.shape[0] * length * planes * 2)
    heads = bias_table.shape[1]
    width = inputs.shape[1]
    size = query_weight.shape[1] // heads
    columns = heads * size
    each = query_weight.shape[0]
    hidden_units = inner_weight.shape[1]
    core, z = lax.axis_index("core"), lax.axis_index("tensor")
    half = parts // 2
    lower = z < half
    owner = core == z // half
    outer_chip = (z == 0) | (z == parts - 1)
    group = (z % half) * 2 + core
    gather, rounds, weight_routes = routes(parts)
    slots = jnp.array([[0, 1, 2, 3], [1, 2, 3, 0], [2, 1, 0, 3], [3, 2, 1, 0]], jnp.int32)[z]

    def swap(value):
        return lax.ppermute(value, "core", SWAP)

    pad = jnp.zeros((each, 256 - columns), bf16)
    packed_rest = jnp.concatenate([inner_weight, outer_weight.T, output_weight.T, pad], axis=1)
    line_rest = lax.all_gather(packed_rest, "tensor", axis=0)

    inputs_wide = inputs.astype(f32)
    scaled_first, inverse_first, normed_own = norm_forward(inputs_wide, attention_gain)
    packed = jnp.concatenate([query_weight, key_weight, value_weight], axis=1)
    first = lax.ppermute(normed_own, LINE, gather[0])
    one, two = (lax.ppermute(packed, LINE, route) for route in weight_routes)
    table = lax.ppermute(bias_table, LINE, weight_routes[0])
    block_row = jnp.where(owner, block_index, swap(block_index))[0]
    first, one, two, table, block_row = lax.optimization_barrier((first, one, two, table, block_row))
    second = lax.ppermute(first, LINE, gather[1])
    attention_full = planes_gathered(
        jnp.where(lower, one, two), jnp.where(lower, two, one)
    ).reshape(width, 3 * columns)
    second, attention_full = lax.optimization_barrier((second, attention_full))
    third = lax.ppermute(jnp.where(outer_chip, normed_own, second), LINE, gather[2])
    normed = [jnp.where(owner, piece, swap(piece)) for piece in (normed_own, first, second, third)]
    all_rest = lax.all_gather(after(line_rest, second), ("plane", "core"), axis=0)

    rows, onehot = bias_rows(table, position_bucket)
    bias = bias_tiles(rows, length)
    end, full, most, least, clear = spans(block_row)
    group_ref = group.reshape(1)

    pieces = [
        dot(attention_full, piece, ((0,), (1,))).astype(bf16).reshape(3 * heads, size, -1)
        for piece in normed
    ]
    ot, lse = attend_forward(pieces, bias, end, full, most, slots, group_ref)
    mixes = [lax.ppermute(ot[r].reshape(columns, -1), LINE, rounds[r]) for r in range(parts)]
    turns = jnp.stack([(z - r) % parts for r in range(parts)]).astype(jnp.int32)
    if each % 16:
        all_rest = jnp.swapaxes(all_rest, 0, 1).reshape(1, parts, width, -1)
    layer_output, grad_hidden, feedforward_part, *gots, grads = middle(
        turns, mixes, inputs, cotangent, feedforward_gain, all_rest
    )
    if each % 16:
        grads = jnp.swapaxes(grads.reshape(parts, planes * 2, each, -1), 0, 1)
    gots = [lax.ppermute(got, LINE, back(rounds[r])) for r, got in enumerate(gots)]
    gots = [got.reshape(heads, size, -1) for got in gots]

    rest = lax.psum_scatter(grads, ("plane", "core"), scatter_dimension=0)
    rest = lax.psum_scatter(rest, "tensor", scatter_dimension=0)
    rest_share = rest.astype(f32) * factor

    dqkv, bands = attend_backward(pieces, gots, ot, lse, bias, end, least, clear, slots, group_ref)
    dqkv = dqkv.reshape(parts, 3 * columns, length // parts)

    def normed_part(i):
        part = dot(dqkv[i], attention_full, ((0,), (1,))).astype(bf16)
        return part + swap(part)

    third, second, first, own = (normed_part(i) for i in (3, 2, 1, 0))

    attention_grads = sum(dot(normed[i], dqkv[i], ((0,), (1,))) for i in range(parts))
    attention_part = (
        jnp.sum(attention_grads * attention_full.astype(f32), axis=1) / attention_gain
    )
    attention_grads = attention_grads.astype(bf16).reshape(planes, 2, each, 3 * columns)

    table_local = table_part(bands, onehot, length)
    buckets = table_local.shape[0]
    table_whole = lax.dynamic_update_slice(
        jnp.zeros((buckets, H), f32), table_local, (jnp.zeros((), jnp.int32), group * heads)
    )
    small = jnp.concatenate(
        [attention_part, feedforward_part.reshape(width), table_whole.reshape(buckets * H)]
    )

    def small_step(small, axis, step):
        count = lax.axis_size(axis)
        return small + lax.ppermute(small, axis, [(i, i ^ step) for i in range(count)])

    none = jnp.zeros_like(own)
    got = lax.ppermute(third, LINE, back(gather[2]))
    if planes == 4:
        relative = attention_grads[jnp.arange(planes) ^ lax.axis_index("plane")]
        low, high = relative[:, 0], relative[:, 1]
        low, high = low[0::2] + across(low[1::2], 1), high[:2] + across(high[2:], 2)
    small = small_step(small, "core", 1)
    small = small_step(small, "tensor", 1)
    if planes == 4:
        got, low, high, small = lax.optimization_barrier((got, low, high, small))
    own = jnp.where(owner, jnp.where(outer_chip, own + got, own), none)
    second = jnp.where(outer_chip, second, second + got)
    got = lax.ppermute(second, LINE, back(gather[1]))
    if planes == 4:
        low, high = low[0] + across(low[1], 2), high[0] + across(high[1], 1)
    else:
        shared = lax.psum_scatter(attention_grads, "plane", scatter_dimension=0)
        low, high = shared[0], shared[1]
    small = small_step(small, "tensor", 2)
    small = small_step(small, "plane", 1)
    got, low, high, small = lax.optimization_barrier((got, low, high, small))
    first = jnp.where(owner, first, none) + got
    got = lax.ppermute(first, LINE, back(gather[0]))
    attention_share = (
        lax.ppermute(jnp.where(lower, low, high), LINE, back(weight_routes[0]))
        + lax.ppermute(jnp.where(lower, high, low), LINE, back(weight_routes[1]))
    ).astype(f32) * factor
    step = 2
    while step < planes:
        small = small_step(small, "plane", step)
        step *= 2
    small = small * factor
    grad_first = (own + got).astype(f32)
    input_grad = (
        grad_hidden + norm_backward(grad_first, scaled_first, inverse_first, attention_gain)
    ).astype(bf16)

    return (
        layer_output,
        input_grad,
        small[:width],
        small[width : 2 * width],
        attention_share[:, :columns],
        attention_share[:, columns : 2 * columns],
        attention_share[:, 2 * columns :],
        rest_share[:, 2 * hidden_units : 2 * hidden_units + columns].T,
        rest_share[:, :hidden_units],
        rest_share[:, hidden_units : 2 * hidden_units].T,
        small[2 * width :].reshape(buckets, H),
    )


def solution(mesh):
    groups, parts = mesh.devices.shape
    fine = Mesh(mesh.devices.reshape(groups // 2, 2, parts), ("plane", "core", "tensor"))
    dp = ("plane", "core")
    tokens = P(("plane", "core", "tensor"), None)
    by_rows = P(dp, "tensor")
    by_columns = P("tensor", dp)
    placed = (
        tokens, P(), P(), by_rows, by_rows, by_rows, by_columns, by_rows, by_columns,
        P(None, "tensor"), P(dp, None), P(), tokens,
    )
    results = (
        tokens, tokens, P(), P(), by_rows, by_rows, by_rows, by_columns, by_rows, by_columns, P(),
    )
    return jax.shard_map(body, mesh=fine, in_specs=placed, out_specs=results, check_vma=False)
```

```python
import math

import jax
import jax.numpy as jnp
from jax import lax
from jax.experimental import pallas as pl
from jax.experimental.pallas import tpu as pltpu
from jax.sharding import Mesh, PartitionSpec as P

H = 12
EPSILON = 1e-06
MASKED = -1e30
TILE = 256
AHEAD = 2
BLOCKS = 8
VMEM_LIMIT = 60 * 1024 * 1024
f32, bf16 = jnp.float32, jnp.bfloat16


def dot(left, right, contract=((1,), (0,))):
    return lax.dot_general(left, right, (contract, ((), ())), preferred_element_type=f32)


def norm_forward(values, gain):
    inverse = lax.rsqrt(jnp.mean(values * values, axis=-1, keepdims=True) + EPSILON)
    scaled = values * inverse
    return scaled, inverse, (scaled * gain).astype(bf16)


def norm_backward(grad_normed, scaled, inverse, gain):
    grad_scaled = grad_normed * gain
    return inverse * (
        grad_scaled - scaled * jnp.mean(grad_scaled * scaled, axis=-1, keepdims=True)
    )


def gelu_parts(values):
    cumulative = 0.5 * (1.0 + lax.erf(values * (1.0 / math.sqrt(2.0))))
    density = jnp.exp(-0.5 * values * values) * (1.0 / math.sqrt(2.0 * math.pi))
    return values * cumulative, cumulative + values * density


def whole(shape):
    return pl.BlockSpec(shape, lambda *_: (0,) * len(shape), pipeline_mode=pl.Buffered(1))


def params():
    return pltpu.CompilerParams(vmem_limit_bytes=VMEM_LIMIT)


def cost(microseconds):
    return pl.CostEstimate(flops=microseconds * 10**9, bytes_accessed=0, transcendentals=0)


def bias_rows(bias_table, position_bucket):
    length = (position_bucket.shape[0] + 1) // 2
    bucket = jnp.concatenate([position_bucket, jnp.zeros((1,), jnp.int32)])[::-1]
    bucket = bucket[(length // TILE - 1 - AHEAD) * TILE :]
    names = jnp.arange(bias_table.shape[0], dtype=jnp.int32)
    onehot = (bucket[None, :] == names[:, None]).astype(f32)
    rows = lax.dot_general(
        bias_table, onehot, (((0,), (0,)), ((), ())), precision=lax.Precision.HIGHEST
    )
    return rows[:, None, :], bucket[None, :]


def bias_kernel(row_ref, out_ref):
    tiles = out_ref.shape[1]

    def one(place, _):
        start = pl.multiple_of((tiles - 1 - place) * TILE, TILE)
        piece = row_ref[0, :, pl.ds(start, 2 * TILE)]
        spread = jnp.broadcast_to(piece, (TILE, 2 * TILE))
        out_ref[0, place] = pltpu.roll(spread, 0, 1, stride=1, stride_axis=0)[:, TILE:]
        return 0

    lax.fori_loop(0, tiles, one, 0)


def bias_tiles(rows, length):
    heads = rows.shape[0]
    tiles = length // TILE + AHEAD
    return pl.pallas_call(
        bias_kernel,
        grid=(heads,),
        in_specs=[pl.BlockSpec((1, 1, rows.shape[2]), lambda h: (h, 0, 0))],
        out_specs=pl.BlockSpec((1, tiles, TILE, TILE), lambda h: (h, 0, 0, 0)),
        out_shape=jax.ShapeDtypeStruct((heads, tiles, TILE, TILE), f32),
        compiler_params=params(),
        cost_estimate=cost(6),
        name="bias_tiles",
    )(rows)


def spans(block_row):
    length = block_row.shape[0]
    names = jnp.arange(BLOCKS, dtype=jnp.int32)[:, None]
    upto = jnp.sum(block_row[None, :] <= names, axis=1, dtype=jnp.int32)
    end = jnp.sum(jnp.where(block_row[None, :] == names, upto[:, None], 0), axis=0, dtype=jnp.int32)
    by_tile = end.reshape(length // TILE, TILE)
    full = by_tile[:, 0] // TILE
    most = (by_tile[:, TILE - 1] + TILE - 1) // TILE
    places = jnp.arange(length // TILE, dtype=jnp.int32)[:, None]
    least = jnp.sum(most[None, :] <= places, axis=1, dtype=jnp.int32)
    clear = jnp.sum(full[None, :] <= places, axis=1, dtype=jnp.int32)
    return end.reshape(1, length), full, most, least, clear


def forward_kernel(full_ref, most_ref, slot_ref, group_ref, place_ref, *refs):
    parts, rows_in = slot_ref.shape[0], place_ref.shape[0]
    pieces, weights = refs[:parts], refs[parts : parts + rows_in]
    gain_ref, bias_ref, end_ref = refs[parts + rows_in : parts + rows_in + 3]
    rest = refs[parts + rows_in + 3 :]
    ots = rest[:parts]
    (
        lse_ref, qkv_ref, normed_ref, weight_ref,
        qt_ref, k_ref, vt_ref, bias_held, scores_ref, rows_held, bias_sem,
    ) = rest[parts:]
    heads, size, length = qt_ref.shape
    count = length // TILE
    each = count // parts
    part_length = length // parts
    query = pl.program_id(0)
    load = pltpu.make_async_copy(bias_ref, bias_held, bias_sem)

    @pl.when(query == 0)
    def _():
        load.start()
        for i, piece in enumerate(weights):
            rows = piece.shape[0]
            rows_held[pl.ds(pl.multiple_of(place_ref[i] * rows, rows), rows), :] = piece[...]
        by_columns = rows_held[...].T
        weight_ref[...] = by_columns
        for i, piece in enumerate(pieces):
            tokens = piece[...].astype(f32)
            inverse = lax.rsqrt(jnp.mean(tokens * tokens, axis=-1, keepdims=True) + EPSILON)
            normed = (tokens * inverse * gain_ref[...]).astype(bf16)
            normed_ref[i] = normed
            qkv = dot(by_columns, normed, ((1,), (1,))).astype(bf16)
            qkv = qkv.reshape(3 * heads, size, part_length)
            qkv_ref[i] = qkv
            places = pl.ds(pl.multiple_of(slot_ref[i] * part_length, TILE), part_length)
            for h in range(heads):
                qt_ref[h, :, places] = qkv[h]
                k_ref[h, places, :] = qkv[heads + h].T
                vt_ref[h, :, places] = qkv[2 * heads + h]
        load.wait()

    own = pl.ds(pl.multiple_of(query * TILE, TILE), TILE)
    queries = [qt_ref[h, :, own] for h in range(heads)]
    last = most_ref[query] - 1

    def scores(key):
        rows = pl.ds(pl.multiple_of(key * TILE, TILE), TILE)
        place = key - query + count - 1
        return [
            dot(k_ref[h, rows, :], queries[h]) + bias_held[h, place] for h in range(heads)
        ]

    def step(key, state, masked):
        slot = lax.rem(key, 2)
        ahead = scores(jnp.minimum(key + 1, last))
        current = [scores_ref[slot, h] for h in range(heads)]
        start = pl.multiple_of(key * TILE, TILE)
        if masked:
            keep = lax.broadcasted_iota(jnp.int32, (TILE, TILE), 0) + start < end_ref[...]
            current = [jnp.where(keep, tile, MASKED) for tile in current]
        tops = [
            jnp.maximum(state[h][0], jnp.max(current[h], axis=0, keepdims=True))
            for h in range(heads)
        ]
        weights = [jnp.exp(current[h] - tops[h]) for h in range(heads)]
        result = []
        for h in range(heads):
            top, total, mix = state[h]
            scale = jnp.exp(top - tops[h])
            total = total * scale + jnp.sum(weights[h], axis=0, keepdims=True)
            mix = mix * scale + dot(vt_ref[h, :, pl.ds(start, TILE)], weights[h].astype(bf16))
            result.append((tops[h], total, mix))
        for h in range(heads):
            scores_ref[1 - slot, h] = ahead[h]
        return tuple(result)

    for h, tile in enumerate(scores(0)):
        scores_ref[0, h] = tile
    state = tuple(
        (jnp.full((1, TILE), -jnp.inf, f32), jnp.zeros((1, TILE), f32), jnp.zeros((size, TILE), f32))
        for _ in range(heads)
    )
    state = lax.fori_loop(0, full_ref[query], lambda key, s: step(key, s, False), state)
    state = lax.fori_loop(full_ref[query], most_ref[query], lambda key, s: step(key, s, True), state)
    turn = lax.rem(query // each - group_ref[0] + parts, parts)
    inner = pl.ds(pl.multiple_of(lax.rem(query, each) * TILE, TILE), TILE)
    mixes = [(mix * (1.0 / total)).astype(bf16) for _, total, mix in state]
    for h, (top, total, _) in enumerate(state):
        lse_ref[h] = top + jnp.log(total)
    for r in range(parts):

        @pl.when(turn == r)
        def _():
            for h in range(heads):
                ots[r][h * size : (h + 1) * size, inner] = mixes[h]


def attend_forward(pieces, weights, places, gain, bias, end, full, most, slots, group):
    parts = len(pieces)
    part_length, width = pieces[0].shape
    columns = weights[0].shape[1]
    heads = bias.shape[0]
    size = columns // (3 * heads)
    length = parts * part_length
    smem = pl.BlockSpec(memory_space=pltpu.SMEM)
    outs = [
        *[jax.ShapeDtypeStruct((heads * size, part_length), bf16)] * parts,
        jax.ShapeDtypeStruct((heads, 1, length), f32),
        jax.ShapeDtypeStruct((parts, 3 * heads, size, part_length), bf16),
        jax.ShapeDtypeStruct((parts, part_length, width), bf16),
        jax.ShapeDtypeStruct((columns, width), bf16),
    ]
    out_specs = [whole(a.shape) for a in outs]
    out_specs[parts] = pl.BlockSpec((heads, 1, TILE), lambda i: (0, 0, i))
    return pl.pallas_call(
        forward_kernel,
        grid=(length // TILE,),
        in_specs=[smem] * 5
        + [whole(a.shape) for a in (*pieces, *weights)]
        + [
            whole((1, width)),
            pl.BlockSpec(memory_space=pl.ANY),
            pl.BlockSpec((1, TILE), lambda i: (0, i)),
        ],
        out_specs=out_specs,
        out_shape=outs,
        scratch_shapes=[
            pltpu.VMEM((heads, size, length), bf16),
            pltpu.VMEM((heads, length, size), bf16),
            pltpu.VMEM((heads, size, length), bf16),
            pltpu.VMEM(bias.shape, f32),
            pltpu.VMEM((2, heads, TILE, TILE), f32),
            pltpu.VMEM((width, columns), bf16),
            pltpu.SemaphoreType.DMA,
        ],
        compiler_params=params(),
        cost_estimate=cost(30),
        name="attend_forward",
    )(full, most, slots, group, places, *pieces, *weights, gain.reshape(1, width), bias, end)


def backward_kernel(least_ref, clear_ref, slot_ref, group_ref, place_ref, *refs):
    parts = slot_ref.shape[0]
    grads, ots = refs[:parts], refs[parts : 2 * parts]
    (
        qkv_ref, lse_ref, end_ref, normed_ref, weight_ref, gain_ref, feed_gain_ref, bucket_ref, bias_ref,
    ) = refs[2 * parts : 2 * parts + 9]
    outs = refs[2 * parts + 9 : 3 * parts + 9]
    small_ref = refs[3 * parts + 9]
    scratch = 16
    share_refs = refs[3 * parts + 10 : len(refs) - scratch]
    (
        qt_ref, kt_ref, vt_ref, got_ref, q_ref, go_ref, dqkv_ref,
        dqt_acc, dk_acc, dv_acc, delta_ref, band_ref, bias_held, sum_ref, line_ref, bias_sem,
    ) = refs[len(refs) - scratch :]
    heads, size, length = qt_ref.shape
    columns = heads * size
    count = length // TILE
    each = count // parts
    part_length = length // parts
    key = pl.program_id(0)
    key_cols = pl.ds(pl.multiple_of(key * TILE, TILE), TILE)
    load = pltpu.make_async_copy(bias_ref, bias_held, bias_sem)
    every = range(heads)

    @pl.when(key == 0)
    def _():
        load.start()
        dqt_acc[...] = jnp.zeros_like(dqt_acc)
        band_ref[...] = jnp.zeros_like(band_ref)
        for i in range(parts):
            places = pl.ds(pl.multiple_of(slot_ref[i] * part_length, TILE), part_length)
            for h in every:
                qt_ref[h, :, places] = qkv_ref[i, h]
                q_ref[h, places, :] = qkv_ref[i, h].T
                kt_ref[h, :, places] = qkv_ref[i, heads + h]
                vt_ref[h, :, places] = qkv_ref[i, 2 * heads + h]
        for turn in range(parts):
            part = lax.rem(group_ref[0] + turn, parts)
            places = pl.ds(pl.multiple_of(part * part_length, TILE), part_length)
            for h in every:
                rows = slice(h * size, (h + 1) * size)
                grad = grads[turn][rows, :]
                got_ref[h, :, places] = grad
                go_ref[h, places, :] = grad.T
                delta_ref[h, :, places] = jnp.sum(
                    ots[turn][rows, :].astype(f32) * grad.astype(f32), axis=0, keepdims=True
                )
        load.wait()

    dk_acc[...] = jnp.zeros_like(dk_acc)
    dv_acc[...] = jnp.zeros_like(dv_acc)
    kt = [kt_ref[h, :, key_cols] for h in every]
    k = [tile.T for tile in kt]
    v = [vt_ref[h, :, key_cols].T for h in every]

    def step(query, masked):
        cols = pl.ds(pl.multiple_of(query * TILE, TILE), TILE)
        place = key - query + count - 1
        scores = [dot(k[h], qt_ref[h, :, cols]) + bias_held[h, place] for h in every]
        if masked:
            keep = lax.broadcasted_iota(jnp.int32, (TILE, TILE), 0) + key * TILE < end_ref[:, cols]
            scores = [jnp.where(keep, tile, MASKED) for tile in scores]
        grad_weights = [dot(v[h], got_ref[h, :, cols]) for h in every]
        weights = [jnp.exp(scores[h] - lse_ref[h, :, cols]) for h in every]
        grad_scores = [weights[h] * (grad_weights[h] - delta_ref[h, :, cols]) for h in every]
        for h in every:
            band_ref[h, place] += grad_scores[h]
        rounded = [tile.astype(bf16) for tile in grad_scores]
        weights = [tile.astype(bf16) for tile in weights]
        for h in every:
            dv_acc[h] += dot(weights[h], go_ref[h, cols, :])
        for h in every:
            dk_acc[h] += dot(rounded[h], q_ref[h, cols, :])
        for h in every:
            dqt_acc[h, :, cols] += dot(kt[h], rounded[h])

    def edge_step(query, _):
        step(query, True)
        return 0

    def full_step(query, _):
        step(query, False)
        return 0

    lax.fori_loop(least_ref[key], clear_ref[key], edge_step, 0)
    lax.fori_loop(clear_ref[key], count, full_step, 0)
    slot = jnp.int32(0)
    for i in range(parts):
        slot = jnp.where(slot_ref[i] == key // each, i, slot)
    inner = pl.ds(pl.multiple_of(lax.rem(key, each) * TILE, TILE), TILE)
    for h in every:
        dqkv_ref[slot, columns + h * size : columns + (h + 1) * size, inner] = dk_acc[h].T.astype(bf16)
        dqkv_ref[slot, 2 * columns + h * size : 2 * columns + (h + 1) * size, inner] = (
            dv_acc[h].T.astype(bf16)
        )

    @pl.when(key == count - 1)
    def _():
        for i in range(parts):
            places = pl.ds(pl.multiple_of(slot_ref[i] * part_length, TILE), part_length)
            for h in every:
                dqkv_ref[i, h * size : (h + 1) * size, :] = dqt_acc[h, :, places].astype(bf16)
        weight = weight_ref[...]
        for i in range(parts):
            outs[i][...] = dot(dqkv_ref[i], weight, ((0,), (0,))).astype(bf16)
        total = dot(dqkv_ref[0], normed_ref[0])
        for i in range(1, parts):
            total = total + dot(dqkv_ref[i], normed_ref[i])
        sum_ref[...] = total.T
        place = 0
        for share in share_refs:
            for i in range(share.shape[0]):
                rows = share.shape[1]
                at = pl.ds(pl.multiple_of(place_ref[place] * rows, rows), rows)
                share[i] = sum_ref[at, :].astype(bf16)
                place += 1

        small_ref[...] = jnp.zeros_like(small_ref)
        gain_grad = jnp.sum(total * weight.astype(f32), axis=0, keepdims=True) / gain_ref[...]
        lanes = small_ref.shape[1]
        each_gain = weight.shape[1] // lanes
        for row in range(each_gain):
            cut = slice(row * lanes, (row + 1) * lanes)
            small_ref[row : row + 1, :] = gain_grad[:, cut]
            small_ref[each_gain + row : each_gain + row + 1, :] = feed_gain_ref[:, cut]

        line_ref[...] = jnp.zeros_like(line_ref)
        tiles = band_ref.shape[1]

        def one(pair, _):
            bands = [(place, h) for place in (2 * pair, 2 * pair + 1) for h in every]
            zero = jnp.zeros((TILE // 2, TILE // 2), f32)
            lines = []
            for place, h in bands:
                upper, lower = band_ref[h, place, : TILE // 2], band_ref[h, place, TILE // 2 :]
                lines.append(
                    jnp.concatenate([zero, zero, upper], axis=1)
                    + jnp.concatenate([zero, lower, zero], axis=1)
                )
            half = TILE // 4
            while half >= 1:
                turned = [pltpu.roll(line[half:], 2 * TILE - half, 1) for line in lines]
                lines = [line[:half] + turn for line, turn in zip(lines, turned)]
                half //= 2
            for (place, h), line in zip(bands, lines):
                start = pl.multiple_of((tiles - 1 - place) * TILE, TILE)
                line_ref[h : h + 1, pl.ds(start, 2 * TILE)] += line
            return 0

        lax.fori_loop(0, tiles // 2, one, 0)
        line = line_ref[0:8, :]
        terms = []
        for _ in range(3):
            term = line.astype(bf16)
            terms.append(term)
            line = line - term.astype(f32)
        names = lax.broadcasted_iota(jnp.int32, (lanes, line_ref.shape[1]), 0)
        onehot = jnp.where(lax.rem(names, lanes // 4) == bucket_ref[...], 1.0, 0.0).astype(bf16)
        sums = [dot(term, onehot, ((1,), (1,))) for term in terms]
        sums = sums[0] + sums[1] + sums[2]
        lane = lax.broadcasted_iota(jnp.int32, (1, lanes), 1)
        table = jnp.zeros((1, lanes), f32)
        for h in every:
            mine = (lane >= h * (lanes // 4)) & (lane < (h + 1) * (lanes // 4))
            table = jnp.where(mine, sums[h : h + 1], table)
        small_ref[pl.ds(2 * each_gain + group_ref[0], 1), :] = table


def attend_backward(
    grads, ots, qkv, lse, end, normed, weight, gain, feed_gain_grad, bucket, bias,
    least, clear, slots, group, places, shares,
):
    parts, triple, size, part_length = qkv.shape
    heads, length = triple // 3, parts * part_length
    columns, width = weight.shape
    tiles = bias.shape[1]
    smem = pl.BlockSpec(memory_space=pltpu.SMEM)
    dense = [*grads, *ots, qkv, lse, end, normed, weight, gain.reshape(1, width), feed_gain_grad, bucket]
    small = jax.ShapeDtypeStruct((2 * (width // 128) + parts, 128), f32)
    outs = [jax.ShapeDtypeStruct((part_length, width), bf16)] * parts + [small]
    outs += [jax.ShapeDtypeStruct((number, rows, columns), bf16) for number, rows in shares]
    by_columns = pltpu.VMEM((heads, size, length), bf16)
    by_rows = pltpu.VMEM((heads, length, size), bf16)
    return pl.pallas_call(
        backward_kernel,
        grid=(length // TILE,),
        in_specs=[smem] * 5
        + [whole(a.shape) for a in dense]
        + [pl.BlockSpec(memory_space=pl.ANY)],
        out_specs=[whole(a.shape) for a in outs],
        out_shape=outs,
        scratch_shapes=[by_columns] * 4
        + [by_rows] * 2
        + [
            pltpu.VMEM((parts, columns, part_length), bf16),
            pltpu.VMEM((heads, size, length), f32),
            pltpu.VMEM((heads, TILE, size), f32),
            pltpu.VMEM((heads, TILE, size), f32),
            pltpu.VMEM((heads, 1, length), f32),
            pltpu.VMEM((heads, tiles, TILE, TILE), f32),
            pltpu.VMEM(bias.shape, f32),
            pltpu.VMEM((width, columns), f32),
            pltpu.VMEM((8, bucket.shape[1]), f32),
            pltpu.SemaphoreType.DMA,
        ],
        compiler_params=params(),
        cost_estimate=cost(50),
        name="attend_backward",
    )(least, clear, slots, group, places, *dense, bias)


def middle_kernel(turn_ref, *refs):
    parts = turn_ref.shape[0]
    mixes = refs[:parts]
    x_ref, g_ref, gain_ref, weight_ref, out_ref, gh_ref, gain_grad_ref = refs[parts : parts + 7]
    gots = refs[parts + 7 : 2 * parts + 7]
    grads_ref, w_ref, grad_ref, second_ref, acc_ref, back_ref, load_sem, store_sem = refs[
        2 * parts + 7 :
    ]
    width = x_ref.shape[1]
    columns = mixes[0].shape[0]
    feed = weight_ref.shape[3] - 256
    hidden_units = feed // 2
    late, early = pl.ds(feed, 256), pl.ds(0, feed)

    def load(z, which, cols):
        return pltpu.make_async_copy(
            weight_ref.at[:, z, :, cols], w_ref.at[z, :, :, cols], load_sem.at[z, which]
        )

    def store(z, which, cols):
        return pltpu.make_async_copy(
            grad_ref.at[z, :, :, cols], grads_ref.at[:, z, :, cols], store_sem.at[z, which]
        )

    for z in range(parts):
        load(z, 0, late).start()
    for z in range(parts):
        load(z, 1, early).start()
    for z in range(parts):
        load(z, 0, late).wait()

    def output_rows(turn):
        return w_ref[turn_ref[turn], :, :, feed : feed + columns].reshape(width, columns)

    hidden = x_ref[...].astype(f32)
    for turn in range(parts):
        hidden = hidden + dot(mixes[turn][...], output_rows(turn), ((0,), (1,)))
    inverse = lax.rsqrt(jnp.mean(hidden * hidden, axis=-1, keepdims=True) + EPSILON)
    second_ref[...] = (hidden * inverse * gain_ref[...]).astype(bf16)
    acc_ref[...] = hidden
    back_ref[...] = jnp.zeros_like(back_ref)
    gh_ref[...] = hidden * inverse

    def hidden_part(z, _):
        load(z, 1, early).wait()
        inner = w_ref[z, :, :, :hidden_units].reshape(width, hidden_units)
        outer = w_ref[z, :, :, hidden_units:feed].reshape(width, hidden_units)
        second = second_ref[...]
        grad = g_ref[...]
        grad_active = dot(grad, outer).astype(bf16).astype(f32)
        active, slope = gelu_parts(dot(second, inner))
        active = active.astype(bf16)
        grad_units = (grad_active * slope).astype(bf16)
        acc_ref[...] += dot(active, outer, ((1,), (1,)))
        back_ref[...] += dot(grad_units, inner, ((1,), (1,)))
        shape = (*grad_ref.shape[1:3], hidden_units)
        grad_ref[z, :, :, :hidden_units] = (
            dot(second, grad_units, ((0,), (0,))).astype(bf16).reshape(shape)
        )
        grad_ref[z, :, :, hidden_units:feed] = (
            dot(grad, active, ((0,), (0,))).astype(bf16).reshape(shape)
        )
        store(z, 1, early).start()
        return 0

    lax.fori_loop(0, parts, hidden_part, 0)
    out_ref[...] = acc_ref[...].astype(bf16)
    scaled = gh_ref[...]
    grad_second = back_ref[...]
    gain_grad_ref[...] = jnp.sum(grad_second * scaled, axis=0, keepdims=True)
    grad_scaled = grad_second * gain_ref[...]
    grad_hidden = g_ref[...].astype(f32) + inverse * (
        grad_scaled - scaled * jnp.mean(grad_scaled * scaled, axis=-1, keepdims=True)
    )
    gh_ref[...] = grad_hidden
    rounded = grad_hidden.astype(bf16)
    for turn in range(parts):
        gots[turn][...] = dot(output_rows(turn), rounded, ((0,), (1,))).astype(bf16)
        grads = dot(rounded, mixes[turn][...], ((0,), (1,))).astype(bf16)
        grad_ref[turn_ref[turn], :, :, feed : feed + columns] = grads.reshape(
            *grad_ref.shape[1:3], columns
        )
        grad_ref[turn_ref[turn], :, :, feed + columns :] = jnp.zeros(
            (*grad_ref.shape[1:3], 256 - columns), bf16
        )
    for z in range(parts):
        store(z, 0, late).start()
    for z in range(parts):
        store(z, 0, late).wait()
        store(z, 1, early).wait()


def middle(turns, mixes, inputs, cotangent, gain, weights):
    rows, width = inputs.shape
    owners, parts, each, columns = weights.shape
    smem = pl.BlockSpec(memory_space=pltpu.SMEM)
    hbm = pl.BlockSpec(memory_space=pl.ANY)
    held = pltpu.VMEM((parts, owners, each, columns), bf16)
    dense = [*mixes, inputs, cotangent, gain.reshape(1, width)]
    outs = [
        jax.ShapeDtypeStruct((rows, width), bf16),
        jax.ShapeDtypeStruct((rows, width), f32),
        jax.ShapeDtypeStruct((1, width), f32),
        *[jax.ShapeDtypeStruct(mix.shape, bf16) for mix in mixes],
    ]
    return pl.pallas_call(
        middle_kernel,
        in_specs=[smem] + [whole(a.shape) for a in dense] + [hbm],
        out_specs=[whole(a.shape) for a in outs] + [hbm],
        out_shape=outs + [jax.ShapeDtypeStruct(weights.shape, bf16)],
        scratch_shapes=[
            held,
            held,
            pltpu.VMEM((rows, width), bf16),
            pltpu.VMEM((rows, width), f32),
            pltpu.VMEM((rows, width), f32),
            pltpu.SemaphoreType.DMA((parts, 2)),
            pltpu.SemaphoreType.DMA((parts, 2)),
        ],
        compiler_params=params(),
        cost_estimate=cost(25),
        name="middle",
    )(turns, *dense, weights)


def flat(pairs, parts):
    return [(c * parts + z, d * parts + y) for (c, z), (d, y) in pairs]


def routes(parts):
    half = parts // 2
    devices = [(c, z) for c in range(2) for z in range(parts)]

    def group(c, z):
        return (z % half) * 2 + c

    gather = [
        flat([((0, z), (0, z - 1)) for z in (1, 2, 3)] + [((1, z), (1, z + 1)) for z in (0, 1, 2)], parts),
        flat([((0, z), (0, z - 1)) for z in (1, 2)] + [((1, z), (1, z + 1)) for z in (1, 2)], parts),
        flat([((0, 1), (0, 0)), ((0, 0), (0, 1)), ((1, 2), (1, 3)), ((1, 3), (1, 2))], parts),
    ]
    rounds = [
        flat([((c, z), (z // half, (group(c, z) + r) % parts)) for c, z in devices], parts)
        for r in range(parts)
    ]
    weights = [
        flat([((z // half ^ flip, group(c, z)), (c, z)) for c, z in devices], parts)
        for flip in range(2)
    ]
    return gather, rounds, weights


def back(pairs):
    return [(target, source) for source, target in pairs]


SWAP = [(0, 1), (1, 0)]
LINE = ("core", "tensor")


def after(value, *earlier):
    return lax.optimization_barrier((value, *earlier))[0]


def across(value, step):
    return lax.ppermute(value, "plane", [(i, i ^ step) for i in range(lax.axis_size("plane"))])


def body(
    inputs,
    attention_gain,
    feedforward_gain,
    query_weight,
    key_weight,
    value_weight,
    output_weight,
    inner_weight,
    outer_weight,
    bias_table,
    block_index,
    position_bucket,
    cotangent,
):
    length = block_index.shape[1]
    parts = lax.axis_size("tensor")
    planes = lax.axis_size("plane")
    factor = 1.0 / math.sqrt(block_index.shape[0] * length * planes * 2)
    heads = bias_table.shape[1]
    buckets = bias_table.shape[0]
    width = inputs.shape[1]
    size = query_weight.shape[1] // heads
    columns = heads * size
    each = query_weight.shape[0]
    hidden_units = inner_weight.shape[1]
    core, z, plane = lax.axis_index("core"), lax.axis_index("tensor"), lax.axis_index("plane")
    half = parts // 2
    lower = z < half
    owner = core == z // half
    outer_chip = (z == 0) | (z == parts - 1)
    group = (z % half) * 2 + core
    group_ref = group.reshape(1)
    square = planes == 4 and each % 16 == 0
    gather, rounds, weight_routes = routes(parts)
    slots = jnp.array([[0, 1, 2, 3], [1, 2, 3, 0], [2, 1, 0, 3], [3, 2, 1, 0]], jnp.int32)[z]

    def swap(value):
        return lax.ppermute(value, "core", SWAP)

    pad = jnp.zeros((each, 256 - columns), bf16)
    packed_rest = jnp.concatenate([inner_weight, outer_weight.T, output_weight.T, pad], axis=1)
    line_rest = lax.all_gather(packed_rest, "tensor", axis=0)

    packed = jnp.concatenate([query_weight, key_weight, value_weight], axis=1)
    first = lax.ppermute(inputs, LINE, gather[0])
    one, two = (lax.ppermute(packed, LINE, route) for route in weight_routes)
    table = lax.ppermute(bias_table, LINE, weight_routes[0])
    block_row = jnp.where(owner, block_index, swap(block_index))[0]
    first, one, two, table, block_row = lax.optimization_barrier((first, one, two, table, block_row))
    second = lax.ppermute(first, LINE, gather[1])
    low, high = jnp.where(lower, one, two), jnp.where(lower, two, one)
    if square:
        low_x, high_y = across(low, 1), across(high, 2)
        low_y, high_x = across(low, 2), across(high, 1)
        low_xy, high_xy = across(low_x, 2), across(high_y, 1)
        weights = [low, high, low_x, high_x, low_y, high_y, low_xy, high_xy]
        order = plane ^ jnp.arange(planes, dtype=jnp.int32)
        places = jnp.stack([order * 2, order * 2 + 1], axis=1).reshape(-1)
    else:
        both = lax.all_gather(jnp.stack([low, high]), "plane", axis=0)
        weights = [both.reshape(width, 3 * columns)]
        places = jnp.zeros((1,), jnp.int32)
    rows, bucket = bias_rows(table, position_bucket)
    bias = bias_tiles(rows, length)
    second, bias, *weights = lax.optimization_barrier((second, bias, *weights))
    third = lax.ppermute(jnp.where(outer_chip, inputs, second), LINE, gather[2])
    pieces = [jnp.where(owner, piece, swap(piece)) for piece in (inputs, first, second, third)]
    all_rest = lax.all_gather(after(line_rest, second), ("plane", "core"), axis=0)

    end, full, most, least, clear = spans(block_row)

    *ots, lse, qkv, normed, weight = attend_forward(
        pieces, weights, places, attention_gain, bias, end, full, most, slots, group_ref
    )
    mixes = [lax.ppermute(ot, LINE, rounds[r]) for r, ot in enumerate(ots)]
    turns = jnp.stack([(z - r) % parts for r in range(parts)]).astype(jnp.int32)
    if each % 16:
        all_rest = jnp.swapaxes(all_rest, 0, 1).reshape(1, parts, width, -1)
    layer_output, grad_hidden, feedforward_part, *gots, grads = middle(
        turns, mixes, inputs, cotangent, feedforward_gain, all_rest
    )
    if each % 16:
        grads = jnp.swapaxes(grads.reshape(parts, planes * 2, each, -1), 0, 1)
    gots = [lax.ppermute(got, LINE, back(rounds[r])) for r, got in enumerate(gots)]

    rest = lax.psum_scatter(grads, ("plane", "core"), scatter_dimension=0)

    if square:
        order = plane ^ jnp.array([1, 3, 0, 2, 2, 3, 0, 1], jnp.int32)
        places = order * 2 + jnp.array([0, 0, 0, 0, 1, 1, 1, 1], jnp.int32)
        shares = [(2, each)] * 4
    else:
        places, shares = jnp.zeros((1,), jnp.int32), [(1, width)]
    back_outs = attend_backward(
        gots, ots, qkv, lse, end, normed, weight, attention_gain, feedforward_part, bucket, bias,
        least, clear, slots, group_ref, places, shares,
    )

    def small_step(small, axis, step):
        count = lax.axis_size(axis)
        return small + lax.ppermute(small, axis, [(i, i ^ step) for i in range(count)])

    own, first, second, third, small, *weight_grads = back_outs
    third = third + swap(third)
    got = lax.ppermute(third, LINE, back(gather[2]))
    own, first, second = (part + swap(part) for part in (own, first, second))
    none = jnp.zeros_like(own)
    if square:
        low_send, low, high_send, high = weight_grads
        low, high = low + across(low_send, 1), high + across(high_send, 2)
    else:
        attention_grads = weight_grads[0].reshape(planes, 2, each, 3 * columns)
        low = high = attention_grads
    small = small_step(small, "core", 1)
    small = small_step(small, "tensor", 1)
    got, low, high, small, rest = lax.optimization_barrier((got, low, high, small, rest))
    rest = lax.psum_scatter(rest, "tensor", scatter_dimension=0)
    own = jnp.where(owner, jnp.where(outer_chip, own + got, own), none)
    second = jnp.where(outer_chip, second, second + got)
    got = lax.ppermute(second, LINE, back(gather[1]))
    if square:
        low, high = low[0] + across(low[1], 2), high[0] + across(high[1], 1)
    else:
        shared = lax.psum_scatter(low, "plane", scatter_dimension=0)
        low, high = shared[0], shared[1]
    small = small_step(small, "tensor", 2)
    small = small_step(small, "plane", 1)
    got, low, high, small = lax.optimization_barrier((got, low, high, small))
    first = jnp.where(owner, first, none) + got
    got = lax.ppermute(first, LINE, back(gather[0]))
    attention_share = (
        lax.ppermute(jnp.where(lower, low, high), LINE, back(weight_routes[0]))
        + lax.ppermute(jnp.where(lower, high, low), LINE, back(weight_routes[1]))
    ).astype(f32) * factor
    step = 2
    while step < planes:
        small = small_step(small, "plane", step)
        step *= 2
    small = small * factor
    rest_share = rest.astype(f32) * factor
    grad_first = (own + got).astype(f32)
    scaled_first, inverse_first, _ = norm_forward(inputs.astype(f32), attention_gain)
    input_grad = (
        grad_hidden + norm_backward(grad_first, scaled_first, inverse_first, attention_gain)
    ).astype(bf16)
    gain_rows = width // 128
    table_grad = small[2 * gain_rows :, : heads * 32].reshape(parts * heads, 32)[:, :buckets].T

    return (
        layer_output,
        input_grad,
        small[:gain_rows].reshape(width),
        small[gain_rows : 2 * gain_rows].reshape(width),
        attention_share[:, :columns],
        attention_share[:, columns : 2 * columns],
        attention_share[:, 2 * columns :],
        rest_share[:, 2 * hidden_units : 2 * hidden_units + columns].T,
        rest_share[:, :hidden_units],
        rest_share[:, hidden_units : 2 * hidden_units].T,
        table_grad,
    )


def solution(mesh):
    groups, parts = mesh.devices.shape
    fine = Mesh(mesh.devices.reshape(groups // 2, 2, parts), ("plane", "core", "tensor"))
    dp = ("plane", "core")
    tokens = P(("plane", "core", "tensor"), None)
    by_rows = P(dp, "tensor")
    by_columns = P("tensor", dp)
    placed = (
        tokens, P(), P(), by_rows, by_rows, by_rows, by_columns, by_rows, by_columns,
        P(None, "tensor"), P(dp, None), P(), tokens,
    )
    results = (
        tokens, tokens, P(), P(), by_rows, by_rows, by_rows, by_columns, by_rows, by_columns, P(),
    )
    return jax.shard_map(body, mesh=fine, in_specs=placed, out_specs=results, check_vma=False)
```

```python
import math

import jax
import jax.numpy as jnp
from jax import lax
from jax.experimental import pallas as pl
from jax.experimental.pallas import tpu as pltpu
from jax.sharding import Mesh, PartitionSpec as P

H = 12
EPSILON = 1e-06
MASKED = -1e30
TILE = 256
AHEAD = 2
BLOCKS = 8
VMEM_LIMIT = 60 * 1024 * 1024
f32, bf16 = jnp.float32, jnp.bfloat16


def dot(left, right, contract=((1,), (0,))):
    return lax.dot_general(left, right, (contract, ((), ())), preferred_element_type=f32)


def norm_forward(values, gain):
    inverse = lax.rsqrt(jnp.mean(values * values, axis=-1, keepdims=True) + EPSILON)
    scaled = values * inverse
    return scaled, inverse, (scaled * gain).astype(bf16)


def norm_backward(grad_normed, scaled, inverse, gain):
    grad_scaled = grad_normed * gain
    return inverse * (
        grad_scaled - scaled * jnp.mean(grad_scaled * scaled, axis=-1, keepdims=True)
    )


def gelu_parts(values):
    cumulative = 0.5 * (1.0 + lax.erf(values * (1.0 / math.sqrt(2.0))))
    density = jnp.exp(-0.5 * values * values) * (1.0 / math.sqrt(2.0 * math.pi))
    return values * cumulative, cumulative + values * density


def whole(shape):
    return pl.BlockSpec(shape, lambda *_: (0,) * len(shape), pipeline_mode=pl.Buffered(1))


def params():
    return pltpu.CompilerParams(vmem_limit_bytes=VMEM_LIMIT)


def cost(microseconds):
    return pl.CostEstimate(flops=microseconds * 10**9, bytes_accessed=0, transcendentals=0)


def bias_rows(bias_table, position_bucket):
    length = (position_bucket.shape[0] + 1) // 2
    bucket = jnp.concatenate([position_bucket, jnp.zeros((1,), jnp.int32)])[::-1]
    bucket = bucket[(length // TILE - 1 - AHEAD) * TILE :]
    names = jnp.arange(bias_table.shape[0], dtype=jnp.int32)
    onehot = (bucket[None, :] == names[:, None]).astype(f32)
    rows = lax.dot_general(
        bias_table, onehot, (((0,), (0,)), ((), ())), precision=lax.Precision.HIGHEST
    )
    return rows[:, None, :], bucket[None, :]


def bias_kernel(row_ref, out_ref):
    tiles = out_ref.shape[1]

    def one(place, _):
        start = pl.multiple_of((tiles - 1 - place) * TILE, TILE)
        piece = row_ref[0, :, pl.ds(start, 2 * TILE)]
        spread = jnp.broadcast_to(piece, (TILE, 2 * TILE))
        out_ref[0, place] = pltpu.roll(spread, 0, 1, stride=1, stride_axis=0)[:, TILE:]
        return 0

    lax.fori_loop(0, tiles, one, 0)


def bias_tiles(rows, length):
    heads = rows.shape[0]
    tiles = length // TILE + AHEAD
    return pl.pallas_call(
        bias_kernel,
        grid=(heads,),
        in_specs=[pl.BlockSpec((1, 1, rows.shape[2]), lambda h: (h, 0, 0))],
        out_specs=pl.BlockSpec((1, tiles, TILE, TILE), lambda h: (h, 0, 0, 0)),
        out_shape=jax.ShapeDtypeStruct((heads, tiles, TILE, TILE), f32),
        compiler_params=params(),
        cost_estimate=cost(6),
        name="bias_tiles",
    )(rows)


def spans(block_row):
    length = block_row.shape[0]
    names = jnp.arange(BLOCKS, dtype=jnp.int32)[:, None]
    upto = jnp.sum(block_row[None, :] <= names, axis=1, dtype=jnp.int32)
    end = jnp.sum(jnp.where(block_row[None, :] == names, upto[:, None], 0), axis=0, dtype=jnp.int32)
    by_tile = end.reshape(length // TILE, TILE)
    full = by_tile[:, 0] // TILE
    most = (by_tile[:, TILE - 1] + TILE - 1) // TILE
    places = jnp.arange(length // TILE, dtype=jnp.int32)[:, None]
    least = jnp.sum(most[None, :] <= places, axis=1, dtype=jnp.int32)
    clear = jnp.sum(full[None, :] <= places, axis=1, dtype=jnp.int32)
    return end.reshape(1, length), full, most, least, clear


def forward_kernel(full_ref, most_ref, slot_ref, group_ref, place_ref, *refs):
    parts, rows_in = slot_ref.shape[0], place_ref.shape[0]
    pieces, weights = refs[:parts], refs[parts : parts + rows_in]
    gain_ref, bias_ref, end_ref = refs[parts + rows_in : parts + rows_in + 3]
    rest = refs[parts + rows_in + 3 :]
    ots = rest[:parts]
    (
        lse_ref, qkv_ref, normed_ref, weight_ref, own_ref,
        qt_ref, k_ref, vt_ref, bias_held, scores_ref, rows_held, bias_sem,
    ) = rest[parts:]
    heads, size, length = qt_ref.shape
    count = length // TILE
    each = count // parts
    part_length = length // parts
    query = pl.program_id(0)
    load = pltpu.make_async_copy(bias_ref, bias_held, bias_sem)

    @pl.when(query == 0)
    def _():
        load.start()
        for i, piece in enumerate(weights):
            rows = piece.shape[0]
            rows_held[pl.ds(pl.multiple_of(place_ref[i] * rows, rows), rows), :] = piece[...]
        by_columns = rows_held[...].T
        weight_ref[...] = by_columns
        for i, piece in enumerate(pieces):
            @pl.when(slot_ref[i] == group_ref[0])
            def _():
                own_ref[...] = piece[...]

            tokens = piece[...].astype(f32)
            inverse = lax.rsqrt(jnp.mean(tokens * tokens, axis=-1, keepdims=True) + EPSILON)
            normed = (tokens * inverse * gain_ref[...]).astype(bf16)
            normed_ref[i] = normed
            qkv = dot(by_columns, normed, ((1,), (1,))).astype(bf16)
            qkv = qkv.reshape(3 * heads, size, part_length)
            qkv_ref[i] = qkv
            places = pl.ds(pl.multiple_of(slot_ref[i] * part_length, TILE), part_length)
            for h in range(heads):
                qt_ref[h, :, places] = qkv[h]
                k_ref[h, places, :] = qkv[heads + h].T
                vt_ref[h, :, places] = qkv[2 * heads + h]
        load.wait()

    own = pl.ds(pl.multiple_of(query * TILE, TILE), TILE)
    queries = [qt_ref[h, :, own] for h in range(heads)]
    last = most_ref[query] - 1

    def scores(key):
        rows = pl.ds(pl.multiple_of(key * TILE, TILE), TILE)
        place = key - query + count - 1
        return [
            dot(k_ref[h, rows, :], queries[h]) + bias_held[h, place] for h in range(heads)
        ]

    def step(key, state, masked):
        slot = lax.rem(key, 2)
        ahead = scores(jnp.minimum(key + 1, last))
        current = [scores_ref[slot, h] for h in range(heads)]
        start = pl.multiple_of(key * TILE, TILE)
        if masked:
            keep = lax.broadcasted_iota(jnp.int32, (TILE, TILE), 0) + start < end_ref[...]
            current = [jnp.where(keep, tile, MASKED) for tile in current]
        tops = [
            jnp.maximum(state[h][0], jnp.max(current[h], axis=0, keepdims=True))
            for h in range(heads)
        ]
        weights = [jnp.exp(current[h] - tops[h]) for h in range(heads)]
        result = []
        for h in range(heads):
            top, total, mix = state[h]
            scale = jnp.exp(top - tops[h])
            total = total * scale + jnp.sum(weights[h], axis=0, keepdims=True)
            mix = mix * scale + dot(vt_ref[h, :, pl.ds(start, TILE)], weights[h].astype(bf16))
            result.append((tops[h], total, mix))
        for h in range(heads):
            scores_ref[1 - slot, h] = ahead[h]
        return tuple(result)

    for h, tile in enumerate(scores(0)):
        scores_ref[0, h] = tile
    state = tuple(
        (jnp.full((1, TILE), -jnp.inf, f32), jnp.zeros((1, TILE), f32), jnp.zeros((size, TILE), f32))
        for _ in range(heads)
    )
    state = lax.fori_loop(0, full_ref[query], lambda key, s: step(key, s, False), state)
    state = lax.fori_loop(full_ref[query], most_ref[query], lambda key, s: step(key, s, True), state)
    turn = (query // each) ^ group_ref[0]
    inner = pl.ds(pl.multiple_of(lax.rem(query, each) * TILE, TILE), TILE)
    mixes = [(mix * (1.0 / total)).astype(bf16) for _, total, mix in state]
    for h, (top, total, _) in enumerate(state):
        lse_ref[h] = top + jnp.log(total)
    for r in range(parts):

        @pl.when(turn == r)
        def _():
            for h in range(heads):
                ots[r][h * size : (h + 1) * size, inner] = mixes[h]


def attend_forward(pieces, weights, places, gain, bias, end, full, most, slots, group):
    parts = len(pieces)
    part_length, width = pieces[0].shape
    columns = weights[0].shape[1]
    heads = bias.shape[0]
    size = columns // (3 * heads)
    length = parts * part_length
    smem = pl.BlockSpec(memory_space=pltpu.SMEM)
    outs = [
        *[jax.ShapeDtypeStruct((heads * size, part_length), bf16)] * parts,
        jax.ShapeDtypeStruct((heads, 1, length), f32),
        jax.ShapeDtypeStruct((parts, 3 * heads, size, part_length), bf16),
        jax.ShapeDtypeStruct((parts, part_length, width), bf16),
        jax.ShapeDtypeStruct((columns, width), bf16),
        jax.ShapeDtypeStruct((part_length, width), bf16),
    ]
    out_specs = [whole(a.shape) for a in outs]
    out_specs[parts] = pl.BlockSpec((heads, 1, TILE), lambda i: (0, 0, i))
    return pl.pallas_call(
        forward_kernel,
        grid=(length // TILE,),
        in_specs=[smem] * 5
        + [whole(a.shape) for a in (*pieces, *weights)]
        + [
            whole((1, width)),
            pl.BlockSpec(memory_space=pl.ANY),
            pl.BlockSpec((1, TILE), lambda i: (0, i)),
        ],
        out_specs=out_specs,
        out_shape=outs,
        scratch_shapes=[
            pltpu.VMEM((heads, size, length), bf16),
            pltpu.VMEM((heads, length, size), bf16),
            pltpu.VMEM((heads, size, length), bf16),
            pltpu.VMEM(bias.shape, f32),
            pltpu.VMEM((2, heads, TILE, TILE), f32),
            pltpu.VMEM((width, columns), bf16),
            pltpu.SemaphoreType.DMA,
        ],
        compiler_params=params(),
        cost_estimate=cost(30),
        name="attend_forward",
    )(full, most, slots, group, places, *pieces, *weights, gain.reshape(1, width), bias, end)


def backward_kernel(least_ref, clear_ref, slot_ref, group_ref, place_ref, *refs):
    parts = slot_ref.shape[0]
    grads, ots = refs[:parts], refs[parts : 2 * parts]
    (
        qkv_ref, lse_ref, end_ref, normed_ref, weight_ref, gain_ref, feed_gain_ref, bucket_ref, bias_ref,
    ) = refs[2 * parts : 2 * parts + 9]
    outs = refs[2 * parts + 9 : 3 * parts + 9]
    small_ref = refs[3 * parts + 9]
    scratch = 16
    share_refs = refs[3 * parts + 10 : len(refs) - scratch]
    (
        qt_ref, kt_ref, vt_ref, got_ref, q_ref, go_ref, dqkv_ref,
        dqt_acc, dk_acc, dv_acc, delta_ref, band_ref, bias_held, sum_ref, line_ref, bias_sem,
    ) = refs[len(refs) - scratch :]
    heads, size, length = qt_ref.shape
    columns = heads * size
    count = length // TILE
    each = count // parts
    part_length = length // parts
    key = pl.program_id(0)
    key_cols = pl.ds(pl.multiple_of(key * TILE, TILE), TILE)
    load = pltpu.make_async_copy(bias_ref, bias_held, bias_sem)
    every = range(heads)

    @pl.when(key == 0)
    def _():
        load.start()
        dqt_acc[...] = jnp.zeros_like(dqt_acc)
        band_ref[...] = jnp.zeros_like(band_ref)
        for i in range(parts):
            places = pl.ds(pl.multiple_of(slot_ref[i] * part_length, TILE), part_length)
            for h in every:
                qt_ref[h, :, places] = qkv_ref[i, h]
                q_ref[h, places, :] = qkv_ref[i, h].T
                kt_ref[h, :, places] = qkv_ref[i, heads + h]
                vt_ref[h, :, places] = qkv_ref[i, 2 * heads + h]
        for turn in range(parts):
            part = group_ref[0] ^ turn
            places = pl.ds(pl.multiple_of(part * part_length, TILE), part_length)
            for h in every:
                rows = slice(h * size, (h + 1) * size)
                grad = grads[turn][rows, :]
                got_ref[h, :, places] = grad
                go_ref[h, places, :] = grad.T
                delta_ref[h, :, places] = jnp.sum(
                    ots[turn][rows, :].astype(f32) * grad.astype(f32), axis=0, keepdims=True
                )
        load.wait()

    dk_acc[...] = jnp.zeros_like(dk_acc)
    dv_acc[...] = jnp.zeros_like(dv_acc)
    kt = [kt_ref[h, :, key_cols] for h in every]
    k = [tile.T for tile in kt]
    v = [vt_ref[h, :, key_cols].T for h in every]

    def step(query, masked):
        cols = pl.ds(pl.multiple_of(query * TILE, TILE), TILE)
        place = key - query + count - 1
        scores = [dot(k[h], qt_ref[h, :, cols]) + bias_held[h, place] for h in every]
        if masked:
            keep = lax.broadcasted_iota(jnp.int32, (TILE, TILE), 0) + key * TILE < end_ref[:, cols]
            scores = [jnp.where(keep, tile, MASKED) for tile in scores]
        grad_weights = [dot(v[h], got_ref[h, :, cols]) for h in every]
        weights = [jnp.exp(scores[h] - lse_ref[h, :, cols]) for h in every]
        grad_scores = [weights[h] * (grad_weights[h] - delta_ref[h, :, cols]) for h in every]
        for h in every:
            band_ref[h, place] += grad_scores[h]
        rounded = [tile.astype(bf16) for tile in grad_scores]
        weights = [tile.astype(bf16) for tile in weights]
        for h in every:
            dv_acc[h] += dot(weights[h], go_ref[h, cols, :])
        for h in every:
            dk_acc[h] += dot(rounded[h], q_ref[h, cols, :])
        for h in every:
            dqt_acc[h, :, cols] += dot(kt[h], rounded[h])

    def edge_step(query, _):
        step(query, True)
        return 0

    def full_step(query, _):
        step(query, False)
        return 0

    lax.fori_loop(least_ref[key], clear_ref[key], edge_step, 0)
    lax.fori_loop(clear_ref[key], count, full_step, 0)
    slot = jnp.int32(0)
    for i in range(parts):
        slot = jnp.where(slot_ref[i] == key // each, i, slot)
    inner = pl.ds(pl.multiple_of(lax.rem(key, each) * TILE, TILE), TILE)
    for h in every:
        dqkv_ref[slot, columns + h * size : columns + (h + 1) * size, inner] = dk_acc[h].T.astype(bf16)
        dqkv_ref[slot, 2 * columns + h * size : 2 * columns + (h + 1) * size, inner] = (
            dv_acc[h].T.astype(bf16)
        )

    @pl.when(key == count - 1)
    def _():
        for i in range(parts):
            places = pl.ds(pl.multiple_of(slot_ref[i] * part_length, TILE), part_length)
            for h in every:
                dqkv_ref[i, h * size : (h + 1) * size, :] = dqt_acc[h, :, places].astype(bf16)
        weight = weight_ref[...]
        for i in range(parts):
            outs[i][...] = dot(dqkv_ref[i], weight, ((0,), (0,))).astype(bf16)
        total = dot(dqkv_ref[0], normed_ref[0])
        for i in range(1, parts):
            total = total + dot(dqkv_ref[i], normed_ref[i])
        sum_ref[...] = total.T
        place = 0
        for share in share_refs:
            for i in range(share.shape[0]):
                rows = share.shape[1]
                at = pl.ds(pl.multiple_of(place_ref[place] * rows, rows), rows)
                share[i] = sum_ref[at, :].astype(bf16)
                place += 1

        small_ref[...] = jnp.zeros_like(small_ref)
        gain_grad = jnp.sum(total * weight.astype(f32), axis=0, keepdims=True) / gain_ref[...]
        lanes = small_ref.shape[1]
        each_gain = weight.shape[1] // lanes
        for row in range(each_gain):
            cut = slice(row * lanes, (row + 1) * lanes)
            small_ref[row : row + 1, :] = gain_grad[:, cut]
            small_ref[each_gain + row : each_gain + row + 1, :] = feed_gain_ref[:, cut]

        line_ref[...] = jnp.zeros_like(line_ref)
        tiles = band_ref.shape[1]

        def one(pair, _):
            bands = [(place, h) for place in (2 * pair, 2 * pair + 1) for h in every]
            zero = jnp.zeros((TILE // 2, TILE // 2), f32)
            lines = []
            for place, h in bands:
                upper, lower = band_ref[h, place, : TILE // 2], band_ref[h, place, TILE // 2 :]
                lines.append(
                    jnp.concatenate([zero, zero, upper], axis=1)
                    + jnp.concatenate([zero, lower, zero], axis=1)
                )
            half = TILE // 4
            while half >= 1:
                turned = [pltpu.roll(line[half:], 2 * TILE - half, 1) for line in lines]
                lines = [line[:half] + turn for line, turn in zip(lines, turned)]
                half //= 2
            for (place, h), line in zip(bands, lines):
                start = pl.multiple_of((tiles - 1 - place) * TILE, TILE)
                line_ref[h : h + 1, pl.ds(start, 2 * TILE)] += line
            return 0

        lax.fori_loop(0, tiles // 2, one, 0)
        line = line_ref[0:8, :]
        terms = []
        for _ in range(3):
            term = line.astype(bf16)
            terms.append(term)
            line = line - term.astype(f32)
        names = lax.broadcasted_iota(jnp.int32, (lanes, line_ref.shape[1]), 0)
        onehot = jnp.where(lax.rem(names, lanes // 4) == bucket_ref[...], 1.0, 0.0).astype(bf16)
        sums = [dot(term, onehot, ((1,), (1,))) for term in terms]
        sums = sums[0] + sums[1] + sums[2]
        lane = lax.broadcasted_iota(jnp.int32, (1, lanes), 1)
        table = jnp.zeros((1, lanes), f32)
        for h in every:
            mine = (lane >= h * (lanes // 4)) & (lane < (h + 1) * (lanes // 4))
            table = jnp.where(mine, sums[h : h + 1], table)
        small_ref[pl.ds(2 * each_gain + group_ref[0], 1), :] = table


def attend_backward(
    grads, ots, qkv, lse, end, normed, weight, gain, feed_gain_grad, bucket, bias,
    least, clear, slots, group, places, shares,
):
    parts, triple, size, part_length = qkv.shape
    heads, length = triple // 3, parts * part_length
    columns, width = weight.shape
    tiles = bias.shape[1]
    smem = pl.BlockSpec(memory_space=pltpu.SMEM)
    dense = [*grads, *ots, qkv, lse, end, normed, weight, gain.reshape(1, width), feed_gain_grad, bucket]
    small = jax.ShapeDtypeStruct((2 * (width // 128) + parts, 128), f32)
    outs = [jax.ShapeDtypeStruct((part_length, width), bf16)] * parts + [small]
    outs += [jax.ShapeDtypeStruct((number, rows, columns), bf16) for number, rows in shares]
    by_columns = pltpu.VMEM((heads, size, length), bf16)
    by_rows = pltpu.VMEM((heads, length, size), bf16)
    return pl.pallas_call(
        backward_kernel,
        grid=(length // TILE,),
        in_specs=[smem] * 5
        + [whole(a.shape) for a in dense]
        + [pl.BlockSpec(memory_space=pl.ANY)],
        out_specs=[whole(a.shape) for a in outs],
        out_shape=outs,
        scratch_shapes=[by_columns] * 4
        + [by_rows] * 2
        + [
            pltpu.VMEM((parts, columns, part_length), bf16),
            pltpu.VMEM((heads, size, length), f32),
            pltpu.VMEM((heads, TILE, size), f32),
            pltpu.VMEM((heads, TILE, size), f32),
            pltpu.VMEM((heads, 1, length), f32),
            pltpu.VMEM((heads, tiles, TILE, TILE), f32),
            pltpu.VMEM(bias.shape, f32),
            pltpu.VMEM((width, columns), f32),
            pltpu.VMEM((8, bucket.shape[1]), f32),
            pltpu.SemaphoreType.DMA,
        ],
        compiler_params=params(),
        cost_estimate=cost(50),
        name="attend_backward",
    )(least, clear, slots, group, places, *dense, bias)


def middle_kernel(turn_ref, *refs):
    parts = turn_ref.shape[0]
    mixes = refs[:parts]
    x_ref, g_ref, gain_ref, weight_ref, out_ref, gain_grad_ref = refs[parts : parts + 6]
    gots = refs[parts + 6 : 2 * parts + 6]
    (
        grads_ref, w_ref, grad_ref, second_ref, acc_ref, back_ref, gh_ref, load_sem, store_sem,
    ) = refs[2 * parts + 6 :]
    width = x_ref.shape[1]
    columns = mixes[0].shape[0]
    feed = weight_ref.shape[3] - 256
    hidden_units = feed // 2
    late, early = pl.ds(feed, 256), pl.ds(0, feed)

    def load(z, which, cols):
        return pltpu.make_async_copy(
            weight_ref.at[:, z, :, cols], w_ref.at[z, :, :, cols], load_sem.at[z, which]
        )

    def store(z, which, cols):
        return pltpu.make_async_copy(
            grad_ref.at[z, :, :, cols], grads_ref.at[:, z, :, cols], store_sem.at[z, which]
        )

    for z in range(parts):
        load(z, 0, late).start()
    for z in range(parts):
        load(z, 1, early).start()
    for z in range(parts):
        load(z, 0, late).wait()

    def output_rows(turn):
        return w_ref[turn_ref[turn], :, :, feed : feed + columns].reshape(width, columns)

    hidden = x_ref[...].astype(f32)
    for turn in range(parts):
        hidden = hidden + dot(mixes[turn][...], output_rows(turn), ((0,), (1,)))
    inverse = lax.rsqrt(jnp.mean(hidden * hidden, axis=-1, keepdims=True) + EPSILON)
    second_ref[...] = (hidden * inverse * gain_ref[...]).astype(bf16)
    acc_ref[...] = hidden
    back_ref[...] = jnp.zeros_like(back_ref)
    gh_ref[...] = hidden * inverse

    def hidden_part(z, _):
        load(z, 1, early).wait()
        inner = w_ref[z, :, :, :hidden_units].reshape(width, hidden_units)
        outer = w_ref[z, :, :, hidden_units:feed].reshape(width, hidden_units)
        second = second_ref[...]
        grad = g_ref[...]
        grad_active = dot(grad, outer).astype(bf16).astype(f32)
        active, slope = gelu_parts(dot(second, inner))
        active = active.astype(bf16)
        grad_units = (grad_active * slope).astype(bf16)
        acc_ref[...] += dot(active, outer, ((1,), (1,)))
        back_ref[...] += dot(grad_units, inner, ((1,), (1,)))
        shape = (*grad_ref.shape[1:3], hidden_units)
        grad_ref[z, :, :, :hidden_units] = (
            dot(second, grad_units, ((0,), (0,))).astype(bf16).reshape(shape)
        )
        grad_ref[z, :, :, hidden_units:feed] = (
            dot(grad, active, ((0,), (0,))).astype(bf16).reshape(shape)
        )
        store(z, 1, early).start()
        return 0

    lax.fori_loop(0, parts, hidden_part, 0)
    out_ref[0] = acc_ref[...].astype(bf16)
    scaled = gh_ref[...]
    grad_second = back_ref[...]
    gain_grad_ref[...] = jnp.sum(grad_second * scaled, axis=0, keepdims=True)
    grad_scaled = grad_second * gain_ref[...]
    grad_hidden = g_ref[...].astype(f32) + inverse * (
        grad_scaled - scaled * jnp.mean(grad_scaled * scaled, axis=-1, keepdims=True)
    )
    rounded = grad_hidden.astype(bf16)
    out_ref[1] = rounded
    for turn in range(parts):
        gots[turn][...] = dot(output_rows(turn), rounded, ((0,), (1,))).astype(bf16)
        grads = dot(rounded, mixes[turn][...], ((0,), (1,))).astype(bf16)
        grad_ref[turn_ref[turn], :, :, feed : feed + columns] = grads.reshape(
            *grad_ref.shape[1:3], columns
        )
        grad_ref[turn_ref[turn], :, :, feed + columns :] = jnp.zeros(
            (*grad_ref.shape[1:3], 256 - columns), bf16
        )
    for z in range(parts):
        store(z, 0, late).start()
    for z in range(parts):
        store(z, 0, late).wait()
        store(z, 1, early).wait()


def middle(turns, mixes, inputs, cotangent, gain, weights):
    rows, width = inputs.shape
    owners, parts, each, columns = weights.shape
    smem = pl.BlockSpec(memory_space=pltpu.SMEM)
    hbm = pl.BlockSpec(memory_space=pl.ANY)
    held = pltpu.VMEM((parts, owners, each, columns), bf16)
    dense = [*mixes, inputs, cotangent, gain.reshape(1, width)]
    outs = [
        jax.ShapeDtypeStruct((2, rows, width), bf16),
        jax.ShapeDtypeStruct((1, width), f32),
        *[jax.ShapeDtypeStruct(mix.shape, bf16) for mix in mixes],
    ]
    return pl.pallas_call(
        middle_kernel,
        in_specs=[smem] + [whole(a.shape) for a in dense] + [hbm],
        out_specs=[whole(a.shape) for a in outs] + [hbm],
        out_shape=outs + [jax.ShapeDtypeStruct(weights.shape, bf16)],
        scratch_shapes=[
            held,
            held,
            pltpu.VMEM((rows, width), bf16),
            pltpu.VMEM((rows, width), f32),
            pltpu.VMEM((rows, width), f32),
            pltpu.VMEM((rows, width), f32),
            pltpu.SemaphoreType.DMA((parts, 2)),
            pltpu.SemaphoreType.DMA((parts, 2)),
        ],
        compiler_params=params(),
        name="middle",
    )(turns, *dense, weights)


def flat(pairs, parts):
    return [(c * parts + z, d * parts + y) for (c, z), (d, y) in pairs]


def routes(parts):
    half = parts // 2
    devices = [(c, z) for c in range(2) for z in range(parts)]

    def group(c, z):
        return (z % half) * 2 + c

    gather = [
        flat([((0, z), (0, z - 1)) for z in (1, 2, 3)] + [((1, z), (1, z + 1)) for z in (0, 1, 2)], parts),
        flat([((0, z), (0, z - 1)) for z in (1, 2)] + [((1, z), (1, z + 1)) for z in (1, 2)], parts),
        flat([((0, 1), (0, 0)), ((0, 0), (0, 1)), ((1, 2), (1, 3)), ((1, 3), (1, 2))], parts),
    ]
    rounds = [
        flat([((c, z), (c ^ (r % half), z ^ (r // half))) for c, z in devices], parts)
        for r in range(parts)
    ]
    owners = flat([((c, z), (z // half, group(c, z))) for c, z in devices], parts)
    weights = [
        flat([((z // half ^ flip, group(c, z)), (c, z)) for c, z in devices], parts)
        for flip in range(2)
    ]
    return gather, rounds, owners, weights


def back(pairs):
    return [(target, source) for source, target in pairs]


SWAP = [(0, 1), (1, 0)]
LINE = ("core", "tensor")


def after(value, *earlier):
    return lax.optimization_barrier((value, *earlier))[0]


def across(value, step):
    return lax.ppermute(value, "plane", [(i, i ^ step) for i in range(lax.axis_size("plane"))])


def body(
    inputs,
    attention_gain,
    feedforward_gain,
    query_weight,
    key_weight,
    value_weight,
    output_weight,
    inner_weight,
    outer_weight,
    bias_table,
    block_index,
    position_bucket,
    cotangent,
):
    length = block_index.shape[1]
    parts = lax.axis_size("tensor")
    planes = lax.axis_size("plane")
    factor = 1.0 / math.sqrt(block_index.shape[0] * length * planes * 2)
    heads = bias_table.shape[1]
    buckets = bias_table.shape[0]
    width = inputs.shape[1]
    size = query_weight.shape[1] // heads
    columns = heads * size
    each = query_weight.shape[0]
    hidden_units = inner_weight.shape[1]
    core, z, plane = lax.axis_index("core"), lax.axis_index("tensor"), lax.axis_index("plane")
    half = parts // 2
    lower = z < half
    owner = core == z // half
    outer_chip = (z == 0) | (z == parts - 1)
    group = (z % half) * 2 + core
    group_ref = group.reshape(1)
    square = planes == 4 and each % 16 == 0
    gather, rounds, owners, weight_routes = routes(parts)
    slots = jnp.array([[0, 1, 2, 3], [1, 2, 3, 0], [2, 1, 0, 3], [3, 2, 1, 0]], jnp.int32)[z]

    def swap(value):
        return lax.ppermute(value, "core", SWAP)

    pad = jnp.zeros((each, 256 - columns), bf16)
    packed_rest = jnp.concatenate([inner_weight, outer_weight.T, output_weight.T, pad], axis=1)

    packed = jnp.concatenate([query_weight, key_weight, value_weight], axis=1)
    first = lax.ppermute(inputs, LINE, gather[0])
    table = lax.ppermute(bias_table, LINE, weight_routes[0])
    block_row = jnp.where(owner, block_index, swap(block_index))[0]
    first, table, block_row, packed, packed_rest = lax.optimization_barrier(
        (first, table, block_row, packed, packed_rest)
    )
    one, two = (lax.ppermute(packed, LINE, route) for route in weight_routes)
    line_rest = lax.all_gather(packed_rest, "tensor", axis=0)
    second = lax.ppermute(first, LINE, gather[1])
    rows, bucket = bias_rows(table, position_bucket)
    bias = bias_tiles(rows, length)
    one, two = after((one, two), bias)
    low, high = jnp.where(lower, one, two), jnp.where(lower, two, one)
    if square:
        low_x, high_y = across(low, 1), across(high, 2)
        low_y, high_x = across(low, 2), across(high, 1)
        low_xy, high_xy = across(low_x, 2), across(high_y, 1)
        weights = [low, high, low_x, high_x, low_y, high_y, low_xy, high_xy]
        order = plane ^ jnp.arange(planes, dtype=jnp.int32)
        places = jnp.stack([order * 2, order * 2 + 1], axis=1).reshape(-1)
    else:
        both = lax.all_gather(jnp.stack([low, high]), "plane", axis=0)
        weights = [both.reshape(width, 3 * columns)]
        places = jnp.zeros((1,), jnp.int32)
    second, *weights = lax.optimization_barrier((second, *weights))
    third = lax.ppermute(jnp.where(outer_chip, inputs, second), LINE, gather[2])
    pieces = [jnp.where(owner, piece, swap(piece)) for piece in (inputs, first, second, third)]
    all_rest = lax.all_gather(after(line_rest, second), ("plane", "core"), axis=0)

    end, full, most, least, clear = spans(block_row)

    grad = lax.ppermute(after(cotangent, third), LINE, back(owners))
    *ots, lse, qkv, normed, weight, own_tokens = attend_forward(
        pieces, weights, places, attention_gain, bias, end, full, most, slots, group_ref
    )
    mixes = [ots[0]] + [lax.ppermute(ots[r], LINE, rounds[r]) for r in range(1, parts)]
    turns = (group ^ jnp.arange(parts)).astype(jnp.int32)
    if each % 16:
        all_rest = jnp.swapaxes(all_rest, 0, 1).reshape(1, parts, width, -1)
    results, feedforward_part, *gots, grads = middle(
        turns, mixes, own_tokens, grad, feedforward_gain, all_rest
    )
    if each % 16:
        grads = jnp.swapaxes(grads.reshape(parts, planes * 2, each, -1), 0, 1)
    gots = [gots[0]] + [lax.ppermute(gots[r], LINE, rounds[r]) for r in range(1, parts)]
    gots, results = lax.optimization_barrier((gots, results))
    results = lax.ppermute(results, LINE, owners)
    layer_output, grad_hidden = results[0], results[1].astype(f32)

    rest = lax.psum_scatter(grads, ("plane", "core"), scatter_dimension=0)

    if square:
        order = plane ^ jnp.array([1, 3, 0, 2, 2, 3, 0, 1], jnp.int32)
        places = order * 2 + jnp.array([0, 0, 0, 0, 1, 1, 1, 1], jnp.int32)
        shares = [(2, each)] * 4
    else:
        places, shares = jnp.zeros((1,), jnp.int32), [(1, width)]
    back_outs = attend_backward(
        gots, ots, qkv, lse, end, normed, weight, attention_gain, feedforward_part, bucket, bias,
        least, clear, slots, group_ref, places, shares,
    )

    def small_step(small, axis, step):
        count = lax.axis_size(axis)
        return small + lax.ppermute(small, axis, [(i, i ^ step) for i in range(count)])

    own, first, second, third, small, *weight_grads = back_outs
    third = third + swap(third)
    got = lax.ppermute(third, LINE, back(gather[2]))
    own, first, second = (part + swap(part) for part in (own, first, second))
    none = jnp.zeros_like(own)
    if square:
        low_send, low, high_send, high = weight_grads
        low, high = low + across(low_send, 1), high + across(high_send, 2)
    else:
        attention_grads = weight_grads[0].reshape(planes, 2, each, 3 * columns)
        low = high = attention_grads
    small = small_step(small, "core", 1)
    small = small_step(small, "tensor", 1)
    got, low, high, small, rest = lax.optimization_barrier((got, low, high, small, rest))
    rest = lax.psum_scatter(rest, "tensor", scatter_dimension=0)
    own = jnp.where(owner, jnp.where(outer_chip, own + got, own), none)
    second = jnp.where(outer_chip, second, second + got)
    got = lax.ppermute(second, LINE, back(gather[1]))
    if square:
        low, high = low[0] + across(low[1], 2), high[0] + across(high[1], 1)
    else:
        shared = lax.psum_scatter(low, "plane", scatter_dimension=0)
        low, high = shared[0], shared[1]
    small = small_step(small, "tensor", 2)
    small = small_step(small, "plane", 1)
    got, low, high, small = lax.optimization_barrier((got, low, high, small))
    first = jnp.where(owner, first, none) + got
    got = lax.ppermute(first, LINE, back(gather[0]))
    attention_share = (
        lax.ppermute(jnp.where(lower, low, high), LINE, back(weight_routes[0]))
        + lax.ppermute(jnp.where(lower, high, low), LINE, back(weight_routes[1]))
    ).astype(f32) * factor
    step = 2
    while step < planes:
        small = small_step(small, "plane", step)
        step *= 2
    small = small * factor
    rest_share = rest.astype(f32) * factor
    grad_first = (own + got).astype(f32)
    scaled_first, inverse_first, _ = norm_forward(inputs.astype(f32), attention_gain)
    input_grad = (
        grad_hidden + norm_backward(grad_first, scaled_first, inverse_first, attention_gain)
    ).astype(bf16)
    gain_rows = width // 128
    table_grad = small[2 * gain_rows :, : heads * 32].reshape(parts * heads, 32)[:, :buckets].T

    return (
        layer_output,
        input_grad,
        small[:gain_rows].reshape(width),
        small[gain_rows : 2 * gain_rows].reshape(width),
        attention_share[:, :columns],
        attention_share[:, columns : 2 * columns],
        attention_share[:, 2 * columns :],
        rest_share[:, 2 * hidden_units : 2 * hidden_units + columns].T,
        rest_share[:, :hidden_units],
        rest_share[:, hidden_units : 2 * hidden_units].T,
        table_grad,
    )


def solution(mesh):
    groups, parts = mesh.devices.shape
    fine = Mesh(mesh.devices.reshape(groups // 2, 2, parts), ("plane", "core", "tensor"))
    dp = ("plane", "core")
    tokens = P(("plane", "core", "tensor"), None)
    by_rows = P(dp, "tensor")
    by_columns = P("tensor", dp)
    placed = (
        tokens, P(), P(), by_rows, by_rows, by_rows, by_columns, by_rows, by_columns,
        P(None, "tensor"), P(dp, None), P(), tokens,
    )
    results = (
        tokens, tokens, P(), P(), by_rows, by_rows, by_rows, by_columns, by_rows, by_columns, P(),
    )
    return jax.shard_map(body, mesh=fine, in_specs=placed, out_specs=results, check_vma=False)
```

```python
import math

import jax
import jax.numpy as jnp
from jax import lax
from jax.experimental import pallas as pl
from jax.experimental.pallas import tpu as pltpu
from jax.sharding import Mesh, PartitionSpec as P

H = 12
EPSILON = 1e-06
MASKED = -1e30
TILE = 256
AHEAD = 2
BLOCKS = 8
VMEM_LIMIT = 60 * 1024 * 1024
f32, bf16 = jnp.float32, jnp.bfloat16


def dot(left, right, contract=((1,), (0,))):
    return lax.dot_general(left, right, (contract, ((), ())), preferred_element_type=f32)


def norm_forward(values, gain):
    inverse = lax.rsqrt(jnp.mean(values * values, axis=-1, keepdims=True) + EPSILON)
    scaled = values * inverse
    return scaled, inverse, (scaled * gain).astype(bf16)


def norm_backward(grad_normed, scaled, inverse, gain):
    grad_scaled = grad_normed * gain
    return inverse * (
        grad_scaled - scaled * jnp.mean(grad_scaled * scaled, axis=-1, keepdims=True)
    )


def gelu_parts(values):
    cumulative = 0.5 * (1.0 + lax.erf(values * (1.0 / math.sqrt(2.0))))
    density = jnp.exp(-0.5 * values * values) * (1.0 / math.sqrt(2.0 * math.pi))
    return values * cumulative, cumulative + values * density


def whole(shape):
    return pl.BlockSpec(shape, lambda *_: (0,) * len(shape), pipeline_mode=pl.Buffered(1))


def params():
    return pltpu.CompilerParams(vmem_limit_bytes=VMEM_LIMIT)


def cost(microseconds):
    return pl.CostEstimate(flops=microseconds * 10**9, bytes_accessed=0, transcendentals=0)


def bias_rows(bias_table, position_bucket):
    length = (position_bucket.shape[0] + 1) // 2
    bucket = jnp.concatenate([position_bucket, jnp.zeros((1,), jnp.int32)])[::-1]
    bucket = bucket[(length // TILE - 1 - AHEAD) * TILE :]
    names = jnp.arange(bias_table.shape[0], dtype=jnp.int32)
    onehot = (bucket[None, :] == names[:, None]).astype(f32)
    rows = lax.dot_general(
        bias_table, onehot, (((0,), (0,)), ((), ())), precision=lax.Precision.HIGHEST
    )
    return rows[:, None, :], bucket[None, :]


def bias_kernel(row_ref, out_ref):
    tiles = out_ref.shape[1]

    def one(place, _):
        start = pl.multiple_of((tiles - 1 - place) * TILE, TILE)
        piece = row_ref[0, :, pl.ds(start, 2 * TILE)]
        spread = jnp.broadcast_to(piece, (TILE, 2 * TILE))
        out_ref[0, place] = pltpu.roll(spread, 0, 1, stride=1, stride_axis=0)[:, TILE:]
        return 0

    lax.fori_loop(0, tiles, one, 0)


def bias_tiles(rows, length):
    heads = rows.shape[0]
    tiles = length // TILE + AHEAD
    return pl.pallas_call(
        bias_kernel,
        grid=(heads,),
        in_specs=[pl.BlockSpec((1, 1, rows.shape[2]), lambda h: (h, 0, 0))],
        out_specs=pl.BlockSpec((1, tiles, TILE, TILE), lambda h: (h, 0, 0, 0)),
        out_shape=jax.ShapeDtypeStruct((heads, tiles, TILE, TILE), f32),
        compiler_params=params(),
        cost_estimate=cost(6),
        name="bias_tiles",
    )(rows)


def spans(block_row):
    length = block_row.shape[0]
    names = jnp.arange(BLOCKS, dtype=jnp.int32)[:, None]
    upto = jnp.sum(block_row[None, :] <= names, axis=1, dtype=jnp.int32)
    end = jnp.sum(jnp.where(block_row[None, :] == names, upto[:, None], 0), axis=0, dtype=jnp.int32)
    by_tile = end.reshape(length // TILE, TILE)
    full = by_tile[:, 0] // TILE
    most = (by_tile[:, TILE - 1] + TILE - 1) // TILE
    places = jnp.arange(length // TILE, dtype=jnp.int32)[:, None]
    least = jnp.sum(most[None, :] <= places, axis=1, dtype=jnp.int32)
    clear = jnp.sum(full[None, :] <= places, axis=1, dtype=jnp.int32)
    return end.reshape(1, length), full, most, least, clear


def token_parts(piece, gain, by_columns, heads):
    tokens = piece.astype(f32)
    inverse = lax.rsqrt(jnp.mean(tokens * tokens, axis=-1, keepdims=True) + EPSILON)
    normed = (tokens * inverse * gain).astype(bf16)
    qkv = dot(by_columns, normed, ((1,), (1,))).astype(bf16)
    return normed, qkv.reshape(3 * heads, -1, normed.shape[0])


def attend_tiles(query, first, clear, last, state, end, queries, k_ref, vt_ref, bias_held, scores_ref):
    heads = len(queries)
    count = k_ref.shape[1] // TILE

    def scores(key):
        rows = pl.ds(pl.multiple_of(key * TILE, TILE), TILE)
        place = jnp.minimum(key - query + count - 1, bias_held.shape[1] - 1)
        return [dot(k_ref[h, rows, :], queries[h]) + bias_held[h, place] for h in range(heads)]

    def step(key, state, masked):
        slot = lax.rem(key, 2)
        ahead = scores(jnp.minimum(key + 1, last - 1))
        current = [scores_ref[slot, h] for h in range(heads)]
        start = pl.multiple_of(key * TILE, TILE)
        if masked:
            keep = lax.broadcasted_iota(jnp.int32, (TILE, TILE), 0) + start < end
            current = [jnp.where(keep, tile, MASKED) for tile in current]
        tops = [
            jnp.maximum(state[h][0], jnp.max(current[h], axis=0, keepdims=True))
            for h in range(heads)
        ]
        weights = [jnp.exp(current[h] - tops[h]) for h in range(heads)]
        result = []
        for h in range(heads):
            top, total, mix = state[h]
            scale = jnp.exp(top - tops[h])
            total = total * scale + jnp.sum(weights[h], axis=0, keepdims=True)
            mix = mix * scale + dot(vt_ref[h, :, pl.ds(start, TILE)], weights[h].astype(bf16))
            result.append((tops[h], total, mix))
        for h in range(heads):
            scores_ref[1 - slot, h] = ahead[h]
        return tuple(result)

    begin = jnp.minimum(first, count - 1)
    for h, tile in enumerate(scores(begin)):
        scores_ref[lax.rem(begin, 2), h] = tile
    clear = jnp.clip(clear, first, jnp.maximum(first, last))
    state = lax.fori_loop(first, clear, lambda key, s: step(key, s, False), state)
    return lax.fori_loop(clear, last, lambda key, s: step(key, s, True), state)


def empty_state(heads, size):
    return tuple(
        (jnp.full((1, TILE), MASKED, f32), jnp.zeros((1, TILE), f32), jnp.zeros((size, TILE), f32))
        for _ in range(heads)
    )


def early_kernel(full_ref, most_ref, slot_ref, group_ref, range_ref, place_ref, *refs):
    known, rows_in = slot_ref.shape[0] - 1, place_ref.shape[0]
    pieces, weights = refs[:known], refs[known : known + rows_in]
    (
        gain_ref, end_ref, bias_ref,
        qkv_ref, normed_ref, weight_ref, own_ref, top_ref, total_ref, mix_ref,
        qt_ref, k_ref, vt_ref, bias_held, scores_ref, rows_held, bias_sem,
    ) = refs[known + rows_in :]
    heads, size, length = qt_ref.shape
    part_length = length // (known + 1)
    turn = pl.program_id(0)
    load = pltpu.make_async_copy(bias_ref, bias_held, bias_sem)

    @pl.when(turn == 0)
    def _():
        load.start()
        for i, piece in enumerate(weights):
            rows = piece.shape[0]
            rows_held[pl.ds(pl.multiple_of(place_ref[i] * rows, rows), rows), :] = piece[...]
        by_columns = rows_held[...].T
        weight_ref[...] = by_columns
        for i, piece in enumerate(pieces):

            @pl.when(slot_ref[i] == group_ref[0])
            def _():
                own_ref[...] = piece[...]

            normed, qkv = token_parts(piece[...], gain_ref[...], by_columns, heads)
            normed_ref[i] = normed
            qkv_ref[i] = qkv
            places = pl.ds(pl.multiple_of(slot_ref[i] * part_length, TILE), part_length)
            for h in range(heads):
                qt_ref[h, :, places] = qkv[h]
                k_ref[h, places, :] = qkv[heads + h].T
                vt_ref[h, :, places] = qkv[2 * heads + h]
        load.wait()

    low, high = range_ref[0], range_ref[1]
    query = low + turn
    own = pl.ds(pl.multiple_of(query * TILE, TILE), TILE)
    state = attend_tiles(
        query, low, full_ref[query], jnp.minimum(most_ref[query], high), empty_state(heads, size),
        end_ref[:, own], [qt_ref[h, :, own] for h in range(heads)],
        k_ref, vt_ref, bias_held, scores_ref,
    )
    for h, (top, total, mix) in enumerate(state):
        top_ref[h, :, own] = top
        total_ref[h, :, own] = total
        mix_ref[h, :, own] = mix


def late_kernel(full_ref, most_ref, slot_ref, group_ref, range_ref, *refs):
    parts = slot_ref.shape[0]
    (
        piece_ref, weight_ref, gain_ref, end_ref, before_ref, top_ref, total_ref, mix_ref, bias_ref,
    ) = refs[:9]
    ots = refs[9 : 9 + parts]
    (
        lse_ref, qkv_ref, normed_ref,
        qt_ref, k_ref, vt_ref, bias_held, scores_ref, held_ref, bias_sem,
    ) = refs[9 + parts :]
    heads, size, length = qt_ref.shape
    count = length // TILE
    each = count // parts
    part_length = length // parts
    query = pl.program_id(0)
    load = pltpu.make_async_copy(bias_ref, bias_held, bias_sem)

    @pl.when(query == 0)
    def _():
        load.start()
        normed, qkv = token_parts(piece_ref[...], gain_ref[...], weight_ref[...], heads)
        normed_ref[0] = normed
        qkv_ref[0] = qkv
        for i in range(parts):
            source = before_ref.at[i] if i < parts - 1 else qkv_ref.at[0]
            places = pl.ds(pl.multiple_of(slot_ref[i] * part_length, TILE), part_length)
            for h in range(heads):
                qt_ref[h, :, places] = source[h]
                k_ref[h, places, :] = source[heads + h].T
                vt_ref[h, :, places] = source[2 * heads + h]
        load.wait()

    low, high = range_ref[0], range_ref[1]
    own = pl.ds(pl.multiple_of(query * TILE, TILE), TILE)
    begun = (query >= low) & (query < high)
    for h in range(heads):
        held_ref[h, 0:1, :] = jnp.where(begun, top_ref[h, :, own], MASKED)
        held_ref[h, 1:2, :] = jnp.where(begun, total_ref[h, :, own], 0.0)
        held_ref[h, 8:, :] = jnp.where(begun, mix_ref[h, :, own], 0.0)
    state = tuple(
        (held_ref[h, 0:1, :], held_ref[h, 1:2, :], held_ref[h, 8:, :]) for h in range(heads)
    )
    most = most_ref[query]
    first = jnp.where(begun & (low == 0), high, 0)
    last = jnp.where(begun & (low > 0), jnp.minimum(low, most), most)
    state = attend_tiles(
        query, first, full_ref[query], last, state,
        end_ref[:, own], [qt_ref[h, :, own] for h in range(heads)],
        k_ref, vt_ref, bias_held, scores_ref,
    )
    turn = (query // each) ^ group_ref[0]
    inner = pl.ds(pl.multiple_of(lax.rem(query, each) * TILE, TILE), TILE)
    mixes = [(mix * (1.0 / total)).astype(bf16) for _, total, mix in state]
    for h, (top, total, _) in enumerate(state):
        lse_ref[h] = top + jnp.log(total)
    for r in range(parts):

        @pl.when(turn == r)
        def _():
            for h in range(heads):
                ots[r][h * size : (h + 1) * size, inner] = mixes[h]


def shape(*dims, kind=bf16):
    return jax.ShapeDtypeStruct(dims, kind)


def sequence_held(heads, size, length, bias):
    return [
        pltpu.VMEM((heads, size, length), bf16),
        pltpu.VMEM((heads, length, size), bf16),
        pltpu.VMEM((heads, size, length), bf16),
        pltpu.VMEM(bias.shape, f32),
        pltpu.VMEM((2, heads, TILE, TILE), f32),
    ]


def attend_early(pieces, weights, places, gain, bias, end, full, most, slots, group, known):
    parts = len(pieces) + 1
    part_length, width = pieces[0].shape
    columns = weights[0].shape[1]
    heads = bias.shape[0]
    size = columns // (3 * heads)
    length = parts * part_length
    smem = pl.BlockSpec(memory_space=pltpu.SMEM)
    hbm = pl.BlockSpec(memory_space=pl.ANY)
    outs = [
        shape(parts - 1, 3 * heads, size, part_length),
        shape(parts - 1, part_length, width),
        shape(columns, width),
        shape(part_length, width),
        shape(heads, 1, length, kind=f32),
        shape(heads, 1, length, kind=f32),
        shape(heads, size, length, kind=f32),
    ]
    dense = (*pieces, *weights, gain, end)
    return pl.pallas_call(
        early_kernel,
        grid=((parts - 1) * part_length // TILE,),
        in_specs=[smem] * 6 + [whole(a.shape) for a in dense] + [hbm],
        out_specs=[whole(a.shape) for a in outs],
        out_shape=outs,
        scratch_shapes=sequence_held(heads, size, length, bias)
        + [pltpu.VMEM((width, columns), bf16), pltpu.SemaphoreType.DMA],
        compiler_params=params(),
        cost_estimate=cost(20),
        name="attend_early",
    )(full, most, slots, group, known, places, *dense, bias)


def attend_late(piece, weight, gain, bias, end, full, most, slots, group, known, qkv, state):
    part_length, width = piece.shape
    parts, heads = qkv.shape[0] + 1, bias.shape[0]
    size = qkv.shape[2]
    length = parts * part_length
    smem = pl.BlockSpec(memory_space=pltpu.SMEM)
    hbm = pl.BlockSpec(memory_space=pl.ANY)
    outs = [
        *[shape(heads * size, part_length)] * parts,
        shape(heads, 1, length, kind=f32),
        shape(1, 3 * heads, size, part_length),
        shape(1, part_length, width),
    ]
    out_specs = [whole(a.shape) for a in outs]
    out_specs[parts] = pl.BlockSpec((heads, 1, TILE), lambda i: (0, 0, i))
    dense = (piece, weight, gain, end, qkv, *state)
    return pl.pallas_call(
        late_kernel,
        grid=(length // TILE,),
        in_specs=[smem] * 5 + [whole(a.shape) for a in dense] + [hbm],
        out_specs=out_specs,
        out_shape=outs,
        scratch_shapes=sequence_held(heads, size, length, bias)
        + [pltpu.VMEM((heads, size + 8, TILE), f32), pltpu.SemaphoreType.DMA],
        compiler_params=params(),
        cost_estimate=cost(15),
        name="attend_late",
    )(full, most, slots, group, known, *dense, bias)

def backward_kernel(least_ref, clear_ref, slot_ref, group_ref, *refs):
    parts = slot_ref.shape[0]
    grads, ots = refs[:parts], refs[parts : 2 * parts]
    (
        qkv_early, qkv_late, lse_ref, end_ref, weight_ref, bias_ref,
    ) = refs[2 * parts : 2 * parts + 6]
    outs = refs[2 * parts + 6 : 3 * parts + 6]
    qkv_ref = [qkv_early.at[i] for i in range(parts - 1)] + [qkv_late.at[0]]
    (
        dqkv_ref, band_out,
        qt_ref, kt_ref, vt_ref, got_ref,
        dqt_acc, dk_acc, dv_acc, delta_ref, band_ref, bias_held, bias_sem, band_sem,
    ) = refs[3 * parts + 6 :]
    heads, size, length = qt_ref.shape
    columns = heads * size
    count = length // TILE
    each = count // parts
    part_length = length // parts
    key = pl.program_id(0)
    key_cols = pl.ds(pl.multiple_of(key * TILE, TILE), TILE)
    load = pltpu.make_async_copy(bias_ref, bias_held, bias_sem)
    store = pltpu.make_async_copy(band_ref, band_out, band_sem)
    every = range(heads)

    @pl.when(key == 0)
    def _():
        load.start()
        dqt_acc[...] = jnp.zeros_like(dqt_acc)
        band_ref[...] = jnp.zeros_like(band_ref)
        for i in range(parts):
            places = pl.ds(pl.multiple_of(slot_ref[i] * part_length, TILE), part_length)
            for h in every:
                qt_ref[h, :, places] = qkv_ref[i][h]
                kt_ref[h, :, places] = qkv_ref[i][heads + h]
                vt_ref[h, :, places] = qkv_ref[i][2 * heads + h]
        for turn in range(parts):
            part = group_ref[0] ^ turn
            places = pl.ds(pl.multiple_of(part * part_length, TILE), part_length)
            for h in every:
                rows = slice(h * size, (h + 1) * size)
                grad = grads[turn][rows, :]
                got_ref[h, :, places] = grad
                delta_ref[h, :, places] = jnp.sum(
                    ots[turn][rows, :].astype(f32) * grad.astype(f32), axis=0, keepdims=True
                )
        load.wait()

    dk_acc[...] = jnp.zeros_like(dk_acc)
    dv_acc[...] = jnp.zeros_like(dv_acc)
    kt = [kt_ref[h, :, key_cols] for h in every]
    k = [tile.T for tile in kt]
    v = [vt_ref[h, :, key_cols].T for h in every]

    def step(query, masked):
        cols = pl.ds(pl.multiple_of(query * TILE, TILE), TILE)
        place = key - query + count - 1
        scores = [dot(k[h], qt_ref[h, :, cols]) + bias_held[h, place] for h in every]
        if masked:
            keep = lax.broadcasted_iota(jnp.int32, (TILE, TILE), 0) + key * TILE < end_ref[:, cols]
            scores = [jnp.where(keep, tile, MASKED) for tile in scores]
        grad_weights = [dot(v[h], got_ref[h, :, cols]) for h in every]
        weights = [jnp.exp(scores[h] - lse_ref[h, :, cols]) for h in every]
        grad_scores = [weights[h] * (grad_weights[h] - delta_ref[h, :, cols]) for h in every]
        for h in every:
            band_ref[h, place] += grad_scores[h]
        rounded = [tile.astype(bf16) for tile in grad_scores]
        weights = [tile.astype(bf16) for tile in weights]
        for h in every:
            dv_acc[h] += dot(got_ref[h, :, cols], weights[h], ((1,), (1,)))
        for h in every:
            dk_acc[h] += dot(qt_ref[h, :, cols], rounded[h], ((1,), (1,)))
        for h in every:
            dqt_acc[h, :, cols] += dot(kt[h], rounded[h])

    def edge_step(query, _):
        step(query, True)
        return 0

    def full_step(query, _):
        step(query, False)
        return 0

    lax.fori_loop(least_ref[key], clear_ref[key], edge_step, 0)
    lax.fori_loop(clear_ref[key], count, full_step, 0)
    slot = jnp.int32(0)
    for i in range(parts):
        slot = jnp.where(slot_ref[i] == key // each, i, slot)
    inner = pl.ds(pl.multiple_of(lax.rem(key, each) * TILE, TILE), TILE)
    for h in every:
        dqkv_ref[slot, columns + h * size : columns + (h + 1) * size, inner] = dk_acc[h].astype(bf16)
        dqkv_ref[slot, 2 * columns + h * size : 2 * columns + (h + 1) * size, inner] = (
            dv_acc[h].astype(bf16)
        )

    @pl.when(key == count - 1)
    def _():
        for i in range(parts):
            places = pl.ds(pl.multiple_of(slot_ref[i] * part_length, TILE), part_length)
            for h in every:
                dqkv_ref[i, h * size : (h + 1) * size, :] = dqt_acc[h, :, places].astype(bf16)
        store.start()
        weight = weight_ref[...]
        for i in reversed(range(parts)):
            outs[i][...] = dot(dqkv_ref[i], weight, ((0,), (0,))).astype(bf16)
        store.wait()


def sums_kernel(group_ref, place_ref, *refs):
    (
        dqkv_ref, normed_early, normed_late, weight_ref, gain_ref, feed_gain_ref, bucket_ref, band_in, small_ref,
    ) = refs[:9]
    share_refs = refs[9:-4]
    band_ref, sum_ref, line_ref, band_sem = refs[-4:]
    load = pltpu.make_async_copy(band_in, band_ref, band_sem)
    load.start()
    parts = dqkv_ref.shape[0]
    every = range(band_ref.shape[0])
    normed_ref = [normed_early.at[i] for i in range(parts - 1)] + [normed_late.at[0]]
    weight = weight_ref[...]
    total = dot(dqkv_ref[0], normed_ref[0][...])
    for i in range(1, parts):
        total = total + dot(dqkv_ref[i], normed_ref[i][...])
    sum_ref[...] = total.T
    place = 0
    for share in share_refs:
        for i in range(share.shape[0]):
            rows = share.shape[1]
            at = pl.ds(pl.multiple_of(place_ref[place] * rows, rows), rows)
            share[i] = sum_ref[at, :].astype(bf16)
            place += 1

    small_ref[...] = jnp.zeros_like(small_ref)
    gain_grad = jnp.sum(total * weight.astype(f32), axis=0, keepdims=True) / gain_ref[...]
    lanes = small_ref.shape[1]
    each_gain = weight.shape[1] // lanes
    for row in range(each_gain):
        cut = slice(row * lanes, (row + 1) * lanes)
        small_ref[row : row + 1, :] = gain_grad[:, cut]
        small_ref[each_gain + row : each_gain + row + 1, :] = feed_gain_ref[:, cut]

    line_ref[...] = jnp.zeros_like(line_ref)
    load.wait()
    tiles = band_ref.shape[1]

    def one(pair, _):
        bands = [(place, h) for place in (2 * pair, 2 * pair + 1) for h in every]
        zero = jnp.zeros((TILE // 2, TILE // 2), f32)
        lines = []
        for place, h in bands:
            upper, lower = band_ref[h, place, : TILE // 2], band_ref[h, place, TILE // 2 :]
            lines.append(
                jnp.concatenate([zero, zero, upper], axis=1)
                + jnp.concatenate([zero, lower, zero], axis=1)
            )
        half = TILE // 4
        while half >= 1:
            turned = [pltpu.roll(line[half:], 2 * TILE - half, 1) for line in lines]
            lines = [line[:half] + turn for line, turn in zip(lines, turned)]
            half //= 2
        for (place, h), line in zip(bands, lines):
            start = pl.multiple_of((tiles - 1 - place) * TILE, TILE)
            line_ref[h : h + 1, pl.ds(start, 2 * TILE)] += line
        return 0

    lax.fori_loop(0, tiles // 2, one, 0)
    line = line_ref[0:8, :]
    terms = []
    for _ in range(3):
        term = line.astype(bf16)
        terms.append(term)
        line = line - term.astype(f32)
    names = lax.broadcasted_iota(jnp.int32, (lanes, line_ref.shape[1]), 0)
    onehot = jnp.where(lax.rem(names, lanes // 4) == bucket_ref[...], 1.0, 0.0).astype(bf16)
    sums = [dot(term, onehot, ((1,), (1,))) for term in terms]
    sums = sums[0] + sums[1] + sums[2]
    lane = lax.broadcasted_iota(jnp.int32, (1, lanes), 1)
    table = jnp.zeros((1, lanes), f32)
    for h in every:
        mine = (lane >= h * (lanes // 4)) & (lane < (h + 1) * (lanes // 4))
        table = jnp.where(mine, sums[h : h + 1], table)
    small_ref[pl.ds(2 * each_gain + group_ref[0], 1), :] = table


def attend_backward(grads, ots, qkv, lse, end, weight, bias, least, clear, slots, group):
    parts = len(grads)
    _, triple, size, part_length = qkv[0].shape
    heads, length = triple // 3, parts * part_length
    columns, width = weight.shape
    smem = pl.BlockSpec(memory_space=pltpu.SMEM)
    hbm = pl.BlockSpec(memory_space=pl.ANY)
    dense = [*grads, *ots, *qkv, lse, end, weight]
    outs = [shape(part_length, width)] * parts + [shape(parts, columns, part_length)]
    by_columns = pltpu.VMEM((heads, size, length), bf16)
    return pl.pallas_call(
        backward_kernel,
        grid=(length // TILE,),
        in_specs=[smem] * 4 + [whole(a.shape) for a in dense] + [hbm],
        out_specs=[whole(a.shape) for a in outs] + [hbm],
        out_shape=outs + [shape(*bias.shape, kind=f32)],
        scratch_shapes=[by_columns] * 4
        + [
            pltpu.VMEM((heads, size, length), f32),
            pltpu.VMEM((heads, size, TILE), f32),
            pltpu.VMEM((heads, size, TILE), f32),
            pltpu.VMEM((heads, 1, length), f32),
            pltpu.VMEM(bias.shape, f32),
            pltpu.VMEM(bias.shape, f32),
            pltpu.SemaphoreType.DMA,
            pltpu.SemaphoreType.DMA,
        ],
        compiler_params=params(),
        cost_estimate=cost(45),
        name="attend_backward",
    )(least, clear, slots, group, *dense, bias)


def attend_sums(dqkv, normed, weight, gain, feed_gain_grad, bucket, bands, group, places, shares):
    parts, columns, _ = dqkv.shape
    width = weight.shape[1]
    smem = pl.BlockSpec(memory_space=pltpu.SMEM)
    dense = [dqkv, *normed, weight, gain.reshape(1, width), feed_gain_grad, bucket]
    outs = [shape(2 * (width // 128) + parts, 128, kind=f32)]
    outs += [shape(number, rows, columns) for number, rows in shares]
    return pl.pallas_call(
        sums_kernel,
        in_specs=[smem] * 2
        + [whole(a.shape) for a in dense]
        + [pl.BlockSpec(memory_space=pl.ANY)],
        out_specs=[whole(a.shape) for a in outs],
        out_shape=outs,
        scratch_shapes=[
            pltpu.VMEM(bands.shape, f32),
            pltpu.VMEM((width, columns), f32),
            pltpu.VMEM((8, bucket.shape[1]), f32),
            pltpu.SemaphoreType.DMA,
        ],
        compiler_params=params(),
        cost_estimate=cost(12),
        name="attend_sums",
    )(group, places, *dense, bands)


def middle_kernel(turn_ref, *refs):
    parts = turn_ref.shape[0]
    mixes = refs[:parts]
    x_ref, g_ref, gain_ref, weight_ref, out_ref, gain_grad_ref = refs[parts : parts + 6]
    gots = refs[parts + 6 : 2 * parts + 6]
    (
        grads_ref, w_ref, grad_ref, second_ref, acc_ref, back_ref, gh_ref, load_sem, store_sem,
    ) = refs[2 * parts + 6 :]
    width = x_ref.shape[1]
    columns = mixes[0].shape[0]
    feed = weight_ref.shape[3] - 256
    hidden_units = feed // 2
    late, early = pl.ds(feed, 256), pl.ds(0, feed)

    def load(z, which, cols):
        return pltpu.make_async_copy(
            weight_ref.at[:, z, :, cols], w_ref.at[z, :, :, cols], load_sem.at[z, which]
        )

    def store(z, which, cols):
        return pltpu.make_async_copy(
            grad_ref.at[z, :, :, cols], grads_ref.at[:, z, :, cols], store_sem.at[z, which]
        )

    for z in range(parts):
        load(z, 0, late).start()
    for z in range(parts):
        load(z, 1, early).start()
    for z in range(parts):
        load(z, 0, late).wait()

    def output_rows(turn):
        return w_ref[turn_ref[turn], :, :, feed : feed + columns].reshape(width, columns)

    hidden = x_ref[...].astype(f32)
    for turn in range(parts):
        hidden = hidden + dot(mixes[turn][...], output_rows(turn), ((0,), (1,)))
    inverse = lax.rsqrt(jnp.mean(hidden * hidden, axis=-1, keepdims=True) + EPSILON)
    second_ref[...] = (hidden * inverse * gain_ref[...]).astype(bf16)
    acc_ref[...] = hidden
    back_ref[...] = jnp.zeros_like(back_ref)
    gh_ref[...] = hidden * inverse

    def hidden_part(z, _):
        load(z, 1, early).wait()
        inner = w_ref[z, :, :, :hidden_units].reshape(width, hidden_units)
        outer = w_ref[z, :, :, hidden_units:feed].reshape(width, hidden_units)
        second = second_ref[...]
        grad = g_ref[...]
        units = dot(second, inner)
        grad_active = dot(grad, outer).astype(bf16).astype(f32)
        active, slope = gelu_parts(units)
        active = active.astype(bf16)
        grad_units = (grad_active * slope).astype(bf16)
        acc_ref[...] += dot(active, outer, ((1,), (1,)))
        back_ref[...] += dot(grad_units, inner, ((1,), (1,)))
        shape = (*grad_ref.shape[1:3], hidden_units)
        grad_ref[z, :, :, :hidden_units] = (
            dot(second, grad_units, ((0,), (0,))).astype(bf16).reshape(shape)
        )
        grad_ref[z, :, :, hidden_units:feed] = (
            dot(grad, active, ((0,), (0,))).astype(bf16).reshape(shape)
        )
        store(z, 1, early).start()
        return 0

    lax.fori_loop(0, parts, hidden_part, 0)
    out_ref[0] = acc_ref[...].astype(bf16)
    scaled = gh_ref[...]
    grad_second = back_ref[...]
    gain_grad_ref[...] = jnp.sum(grad_second * scaled, axis=0, keepdims=True)
    grad_scaled = grad_second * gain_ref[...]
    grad_hidden = g_ref[...].astype(f32) + inverse * (
        grad_scaled - scaled * jnp.mean(grad_scaled * scaled, axis=-1, keepdims=True)
    )
    rounded = grad_hidden.astype(bf16)
    out_ref[1] = rounded
    for turn in range(parts):
        gots[turn][...] = dot(output_rows(turn), rounded, ((0,), (1,))).astype(bf16)
        grads = dot(rounded, mixes[turn][...], ((0,), (1,))).astype(bf16)
        grad_ref[turn_ref[turn], :, :, feed : feed + columns] = grads.reshape(
            *grad_ref.shape[1:3], columns
        )
        grad_ref[turn_ref[turn], :, :, feed + columns :] = jnp.zeros(
            (*grad_ref.shape[1:3], 256 - columns), bf16
        )
    for z in range(parts):
        store(z, 0, late).start()
    for z in range(parts):
        store(z, 0, late).wait()
        store(z, 1, early).wait()


def middle(turns, mixes, inputs, cotangent, gain, weights):
    rows, width = inputs.shape
    owners, parts, each, columns = weights.shape
    smem = pl.BlockSpec(memory_space=pltpu.SMEM)
    hbm = pl.BlockSpec(memory_space=pl.ANY)
    held = pltpu.VMEM((parts, owners, each, columns), bf16)
    dense = [*mixes, inputs, cotangent, gain.reshape(1, width)]
    outs = [
        jax.ShapeDtypeStruct((2, rows, width), bf16),
        jax.ShapeDtypeStruct((1, width), f32),
        *[jax.ShapeDtypeStruct(mix.shape, bf16) for mix in mixes],
    ]
    return pl.pallas_call(
        middle_kernel,
        in_specs=[smem] + [whole(a.shape) for a in dense] + [hbm],
        out_specs=[whole(a.shape) for a in outs] + [hbm],
        out_shape=outs + [jax.ShapeDtypeStruct(weights.shape, bf16)],
        scratch_shapes=[
            held,
            held,
            pltpu.VMEM((rows, width), bf16),
            pltpu.VMEM((rows, width), f32),
            pltpu.VMEM((rows, width), f32),
            pltpu.VMEM((rows, width), f32),
            pltpu.SemaphoreType.DMA((parts, 2)),
            pltpu.SemaphoreType.DMA((parts, 2)),
        ],
        compiler_params=params(),
        name="middle",
    )(turns, *dense, weights)


def flat(pairs, parts):
    return [(c * parts + z, d * parts + y) for (c, z), (d, y) in pairs]


def routes(parts):
    half = parts // 2
    devices = [(c, z) for c in range(2) for z in range(parts)]

    def group(c, z):
        return (z % half) * 2 + c

    gather = [
        flat([((0, z), (0, z - 1)) for z in (1, 2, 3)] + [((1, z), (1, z + 1)) for z in (0, 1, 2)], parts),
        flat([((0, z), (0, z - 1)) for z in (1, 2)] + [((1, z), (1, z + 1)) for z in (1, 2)], parts),
        flat([((0, 1), (0, 0)), ((0, 0), (0, 1)), ((1, 2), (1, 3)), ((1, 3), (1, 2))], parts),
    ]
    rounds = [
        flat([((c, z), (c ^ (r % half), z ^ (r // half))) for c, z in devices], parts)
        for r in range(parts)
    ]
    owners = flat([((c, z), (z // half, group(c, z))) for c, z in devices], parts)
    weights = [
        flat([((z // half ^ flip, group(c, z)), (c, z)) for c, z in devices], parts)
        for flip in range(2)
    ]
    return gather, rounds, owners, weights


def back(pairs):
    return [(target, source) for source, target in pairs]


SWAP = [(0, 1), (1, 0)]
LINE = ("core", "tensor")


def after(value, *earlier):
    return lax.optimization_barrier((value, *earlier))[0]


def across(value, step):
    return lax.ppermute(value, "plane", [(i, i ^ step) for i in range(lax.axis_size("plane"))])


def body(
    inputs,
    attention_gain,
    feedforward_gain,
    query_weight,
    key_weight,
    value_weight,
    output_weight,
    inner_weight,
    outer_weight,
    bias_table,
    block_index,
    position_bucket,
    cotangent,
):
    length = block_index.shape[1]
    parts = lax.axis_size("tensor")
    planes = lax.axis_size("plane")
    factor = 1.0 / math.sqrt(block_index.shape[0] * length * planes * 2)
    heads = bias_table.shape[1]
    buckets = bias_table.shape[0]
    width = inputs.shape[1]
    size = query_weight.shape[1] // heads
    columns = heads * size
    each = query_weight.shape[0]
    hidden_units = inner_weight.shape[1]
    core, z, plane = lax.axis_index("core"), lax.axis_index("tensor"), lax.axis_index("plane")
    half = parts // 2
    lower = z < half
    owner = core == z // half
    outer_chip = (z == 0) | (z == parts - 1)
    group = (z % half) * 2 + core
    group_ref = group.reshape(1)
    square = planes == 4 and each % 16 == 0
    gather, rounds, owners, weight_routes = routes(parts)
    tiles = length // TILE
    at_start = (z == 0) | (z == half)
    known = jnp.where(at_start, jnp.array([0, tiles - tiles // parts]), jnp.array([tiles // parts, tiles]))
    known = known.astype(jnp.int32)
    slots = jnp.array([[0, 1, 2, 3], [1, 2, 3, 0], [2, 1, 0, 3], [3, 2, 1, 0]], jnp.int32)[z]

    def swap(value):
        return lax.ppermute(value, "core", SWAP)

    pad = jnp.zeros((each, 256 - columns), bf16)
    packed_rest = jnp.concatenate([inner_weight, outer_weight.T, output_weight.T, pad], axis=1)

    packed = jnp.concatenate([query_weight, key_weight, value_weight], axis=1)
    first = lax.ppermute(inputs, LINE, gather[0])
    first, table, block_row, packed, packed_rest = lax.optimization_barrier(
        (first, bias_table, jnp.where(owner, block_index, swap(block_index)), packed, packed_rest)
    )
    table = lax.ppermute(table, LINE, weight_routes[0])
    block_row = block_row[0]
    line_rest = lax.all_gather(packed_rest, "tensor", axis=0)
    one, two = (lax.ppermute(packed, LINE, route) for route in weight_routes)
    second = lax.ppermute(first, LINE, gather[1])
    rows, bucket = bias_rows(table, position_bucket)
    bias = bias_tiles(rows, length)
    one, two = after((one, two), bias)
    low, high = jnp.where(lower, one, two), jnp.where(lower, two, one)
    if square:
        low_x, high_y = across(low, 1), across(high, 2)
        low_y, high_x = across(low, 2), across(high, 1)
        low_xy, high_xy = across(low_x, 2), across(high_y, 1)
        weights = [low, high, low_x, high_x, low_y, high_y, low_xy, high_xy]
        order = plane ^ jnp.arange(planes, dtype=jnp.int32)
        places = jnp.stack([order * 2, order * 2 + 1], axis=1).reshape(-1)
    else:
        both = lax.all_gather(jnp.stack([low, high]), "plane", axis=0)
        weights = [both.reshape(width, 3 * columns)]
        places = jnp.zeros((1,), jnp.int32)
    end, full, most, least, clear = spans(block_row)
    marks = (attention_gain.reshape(1, width), bias, end, full, most, slots, group_ref, known)
    pieces = [jnp.where(owner, piece, swap(piece)) for piece in (inputs, first)]
    second, pieces, weights, places, marks, least, clear = lax.optimization_barrier(
        (second, pieces, weights, places, marks, least, clear)
    )
    third = lax.ppermute(jnp.where(outer_chip, inputs, second), LINE, gather[2])
    pieces = [*pieces, jnp.where(owner, second, swap(second))]
    all_rest = lax.all_gather(after(line_rest, second), ("plane", "core"), axis=0)


    _, bias, end, full, most, slots, group_ref, known = marks
    qkv, normed, weight, own_tokens, *state = attend_early(pieces, weights, places, *marks)
    third, state, cotangent = lax.optimization_barrier((third, state, cotangent))
    grad = lax.ppermute(cotangent, LINE, back(owners))
    third = jnp.where(owner, third, swap(third))
    *ots, lse, late_qkv, late_normed = attend_late(third, weight, *marks, qkv, state)
    qkv, normed = (qkv, late_qkv), (normed, late_normed)
    mixes = [ots[0]] + [lax.ppermute(ots[r], LINE, rounds[r]) for r in range(1, parts)]
    turns = (group ^ jnp.arange(parts)).astype(jnp.int32)
    if each % 16:
        all_rest = jnp.swapaxes(all_rest, 0, 1).reshape(1, parts, width, -1)
    results, feedforward_part, *gots, grads = middle(
        turns, mixes, own_tokens, grad, feedforward_gain, all_rest
    )
    if each % 16:
        grads = jnp.swapaxes(grads.reshape(parts, planes * 2, each, -1), 0, 1)
    gots = [gots[0]] + [lax.ppermute(gots[r], LINE, rounds[r]) for r in range(1, parts)]
    if square:
        order = plane ^ jnp.array([1, 3, 0, 2, 2, 3, 0, 1], jnp.int32)
        places = order * 2 + jnp.array([0, 0, 0, 0, 1, 1, 1, 1], jnp.int32)
        shares = [(2, each)] * 4
    else:
        places, shares = jnp.zeros((1,), jnp.int32), [(1, width)]
    gots, results, places, bucket = lax.optimization_barrier((gots, results, places, bucket))
    results = lax.ppermute(results, LINE, owners)

    rest = lax.psum_scatter(grads, ("plane", "core"), scatter_dimension=0)

    own, first, second, third, dqkv, bands = attend_backward(
        gots, ots, qkv, lse, end, weight, bias, least, clear, slots, group_ref
    )
    third, results = lax.optimization_barrier((third, results))
    layer_output, grad_hidden = results[0], results[1].astype(f32)
    third = third + swap(third)
    got = lax.ppermute(third, LINE, back(gather[2]))
    own, first, second = (part + swap(part) for part in (own, first, second))

    def small_step(small, axis, step):
        count = lax.axis_size(axis)
        return small + lax.ppermute(small, axis, [(i, i ^ step) for i in range(count)])

    dqkv, bands, third = lax.optimization_barrier((dqkv, bands, third))
    small, *weight_grads = attend_sums(
        dqkv, normed, weight, attention_gain, feedforward_part, bucket, bands, group_ref, places, shares
    )
    none = jnp.zeros_like(own)
    got, small, weight_grads, rest = lax.optimization_barrier((got, small, weight_grads, rest))
    rest = lax.psum_scatter(rest, "tensor", scatter_dimension=0)
    own = jnp.where(owner, jnp.where(outer_chip, own + got, own), none)
    second = jnp.where(outer_chip, second, second + got)
    got = lax.ppermute(second, LINE, back(gather[1]))
    if square:
        low_send, low, high_send, high = weight_grads
        low, high = low + across(low_send, 1), high + across(high_send, 2)
    else:
        low = high = weight_grads[0].reshape(planes, 2, each, 3 * columns)
    small = small_step(small, "core", 1)
    small = small_step(small, "tensor", 1)
    got, low, high, small = lax.optimization_barrier((got, low, high, small))
    first = jnp.where(owner, first, none) + got
    got = lax.ppermute(first, LINE, back(gather[0]))
    if square:
        low, high = low[0] + across(low[1], 2), high[0] + across(high[1], 1)
    else:
        shared = lax.psum_scatter(low, "plane", scatter_dimension=0)
        low, high = shared[0], shared[1]
    small = small_step(small, "tensor", 2)
    step = 1
    while step < planes:
        small = small_step(small, "plane", step)
        step *= 2
    attention_share = (
        lax.ppermute(jnp.where(lower, low, high), LINE, back(weight_routes[0]))
        + lax.ppermute(jnp.where(lower, high, low), LINE, back(weight_routes[1]))
    ).astype(f32) * factor
    small = small * factor
    rest_share = rest.astype(f32) * factor
    grad_first = (own + got).astype(f32)
    scaled_first, inverse_first, _ = norm_forward(inputs.astype(f32), attention_gain)
    input_grad = (
        grad_hidden + norm_backward(grad_first, scaled_first, inverse_first, attention_gain)
    ).astype(bf16)
    gain_rows = width // 128
    table_grad = small[2 * gain_rows :, : heads * 32].reshape(parts * heads, 32)[:, :buckets].T

    return (
        layer_output,
        input_grad,
        small[:gain_rows].reshape(width),
        small[gain_rows : 2 * gain_rows].reshape(width),
        attention_share[:, :columns],
        attention_share[:, columns : 2 * columns],
        attention_share[:, 2 * columns :],
        rest_share[:, 2 * hidden_units : 2 * hidden_units + columns].T,
        rest_share[:, :hidden_units],
        rest_share[:, hidden_units : 2 * hidden_units].T,
        table_grad,
    )


def solution(mesh):
    groups, parts = mesh.devices.shape
    fine = Mesh(mesh.devices.reshape(groups // 2, 2, parts), ("plane", "core", "tensor"))
    dp = ("plane", "core")
    tokens = P(("plane", "core", "tensor"), None)
    by_rows = P(dp, "tensor")
    by_columns = P("tensor", dp)
    placed = (
        tokens, P(), P(), by_rows, by_rows, by_rows, by_columns, by_rows, by_columns,
        P(None, "tensor"), P(dp, None), P(), tokens,
    )
    results = (
        tokens, tokens, P(), P(), by_rows, by_rows, by_rows, by_columns, by_rows, by_columns, P(),
    )
    return jax.shard_map(body, mesh=fine, in_specs=placed, out_specs=results, check_vma=False)
```

```python
import math

import jax
import jax.numpy as jnp
from jax import lax
from jax.experimental import pallas as pl
from jax.experimental.pallas import tpu as pltpu
from jax.sharding import Mesh, PartitionSpec as P

H = 12
EPSILON = 1e-06
MASKED = -1e30
LOG2E = 1.4426950408889634
TILE = 256
AHEAD = 2
BLOCKS = 8
VMEM_LIMIT = 60 * 1024 * 1024
f32, bf16 = jnp.float32, jnp.bfloat16


def dot(left, right, contract=((1,), (0,))):
    return lax.dot_general(left, right, (contract, ((), ())), preferred_element_type=f32)


def norm_forward(values, gain):
    inverse = lax.rsqrt(jnp.mean(values * values, axis=-1, keepdims=True) + EPSILON)
    scaled = values * inverse
    return scaled, inverse, (scaled * gain).astype(bf16)


def norm_backward(grad_normed, scaled, inverse, gain):
    grad_scaled = grad_normed * gain
    return inverse * (
        grad_scaled - scaled * jnp.mean(grad_scaled * scaled, axis=-1, keepdims=True)
    )


def gelu_parts(values):
    cumulative = 0.5 * (1.0 + lax.erf(values * (1.0 / math.sqrt(2.0))))
    density = jnp.exp(-0.5 * values * values) * (1.0 / math.sqrt(2.0 * math.pi))
    return values * cumulative, cumulative + values * density


def whole(shape):
    return pl.BlockSpec(shape, lambda *_: (0,) * len(shape), pipeline_mode=pl.Buffered(1))


def params():
    return pltpu.CompilerParams(vmem_limit_bytes=VMEM_LIMIT)


def cost(microseconds):
    return pl.CostEstimate(flops=microseconds * 10**9, bytes_accessed=0, transcendentals=0)


def bias_rows(bias_table, position_bucket):
    length = (position_bucket.shape[0] + 1) // 2
    bucket = jnp.concatenate([position_bucket, jnp.zeros((1,), jnp.int32)])[::-1]
    bucket = bucket[(length // TILE - 1 - AHEAD) * TILE :]
    names = jnp.arange(bias_table.shape[0], dtype=jnp.int32)
    onehot = (bucket[None, :] == names[:, None]).astype(f32)
    rows = lax.dot_general(
        bias_table, onehot, (((0,), (0,)), ((), ())), precision=lax.Precision.HIGHEST
    )
    return rows[:, None, :] * LOG2E, bucket[None, :]


def bias_kernel(row_ref, out_ref):
    tiles = out_ref.shape[1]

    def one(place, _):
        start = pl.multiple_of((tiles - 1 - place) * TILE, TILE)
        piece = row_ref[0, :, pl.ds(start, 2 * TILE)]
        spread = jnp.broadcast_to(piece, (TILE, 2 * TILE))
        out_ref[0, place] = pltpu.roll(spread, 0, 1, stride=1, stride_axis=0)[:, TILE:]
        return 0

    lax.fori_loop(0, tiles, one, 0)


def bias_tiles(rows, length):
    heads = rows.shape[0]
    tiles = length // TILE + AHEAD
    return pl.pallas_call(
        bias_kernel,
        grid=(heads,),
        in_specs=[pl.BlockSpec((1, 1, rows.shape[2]), lambda h: (h, 0, 0))],
        out_specs=pl.BlockSpec((1, tiles, TILE, TILE), lambda h: (h, 0, 0, 0)),
        out_shape=jax.ShapeDtypeStruct((heads, tiles, TILE, TILE), f32),
        compiler_params=params(),
        cost_estimate=cost(6),
        name="bias_tiles",
    )(rows)


def spans(block_row):
    length = block_row.shape[0]
    names = jnp.arange(BLOCKS, dtype=jnp.int32)[:, None]
    upto = jnp.sum(block_row[None, :] <= names, axis=1, dtype=jnp.int32)
    end = jnp.sum(jnp.where(block_row[None, :] == names, upto[:, None], 0), axis=0, dtype=jnp.int32)
    by_tile = end.reshape(length // TILE, TILE)
    full = by_tile[:, 0] // TILE
    most = (by_tile[:, TILE - 1] + TILE - 1) // TILE
    places = jnp.arange(length // TILE, dtype=jnp.int32)[:, None]
    least = jnp.sum(most[None, :] <= places, axis=1, dtype=jnp.int32)
    clear = jnp.sum(full[None, :] <= places, axis=1, dtype=jnp.int32)
    return end.reshape(1, length), full, most, least, clear


def query_pair(queries):
    scaled = queries.astype(f32) * LOG2E
    high = scaled.astype(bf16)
    return jnp.concatenate([high, (scaled - high.astype(f32)).astype(bf16)], axis=0)


def key_pair(keys):
    return jnp.concatenate([keys, keys], axis=0).T


def token_parts(piece, gain, by_columns, heads):
    tokens = piece.astype(f32)
    inverse = lax.rsqrt(jnp.mean(tokens * tokens, axis=-1, keepdims=True) + EPSILON)
    normed = (tokens * inverse * gain).astype(bf16)
    qkv = dot(by_columns, normed, ((1,), (1,))).astype(bf16)
    return normed, qkv.reshape(3 * heads, -1, normed.shape[0])


def attend_tiles(query, first, clear, last, state, end, queries, k_ref, vt_ref, bias_held, scores_ref):
    heads = len(queries)
    count = k_ref.shape[1] // TILE

    def scores(key):
        rows = pl.ds(pl.multiple_of(key * TILE, TILE), TILE)
        place = jnp.minimum(key - query + count - 1, bias_held.shape[1] - 1)
        return [dot(k_ref[h, rows, :], queries[h]) + bias_held[h, place] for h in range(heads)]

    def step(key, state, masked):
        slot = lax.rem(key, 2)
        ahead = scores(jnp.minimum(key + 1, last - 1))
        current = [scores_ref[slot, h] for h in range(heads)]
        start = pl.multiple_of(key * TILE, TILE)
        if masked:
            keep = lax.broadcasted_iota(jnp.int32, (TILE, TILE), 0) + start < end
            current = [jnp.where(keep, tile, MASKED) for tile in current]
        tops = [
            jnp.maximum(state[h][0], jnp.max(current[h], axis=0, keepdims=True))
            for h in range(heads)
        ]
        weights = [jnp.exp2(current[h] - tops[h]) for h in range(heads)]
        result = []
        for h in range(heads):
            top, total, mix = state[h]
            scale = jnp.exp2(top - tops[h])
            total = total * scale + jnp.sum(weights[h], axis=0, keepdims=True)
            mix = mix * scale + dot(vt_ref[h, :, pl.ds(start, TILE)], weights[h].astype(bf16))
            result.append((tops[h], total, mix))
        for h in range(heads):
            scores_ref[1 - slot, h] = ahead[h]
        return tuple(result)

    begin = jnp.minimum(first, count - 1)
    for h, tile in enumerate(scores(begin)):
        scores_ref[lax.rem(begin, 2), h] = tile
    clear = jnp.clip(clear, first, jnp.maximum(first, last))
    state = lax.fori_loop(first, clear, lambda key, s: step(key, s, False), state)
    return lax.fori_loop(clear, last, lambda key, s: step(key, s, True), state)


def empty_state(heads, size):
    return tuple(
        (jnp.full((1, TILE), MASKED, f32), jnp.zeros((1, TILE), f32), jnp.zeros((size, TILE), f32))
        for _ in range(heads)
    )


def early_kernel(full_ref, most_ref, slot_ref, group_ref, range_ref, place_ref, *refs):
    known, rows_in = slot_ref.shape[0] - 1, place_ref.shape[0]
    pieces, weights = refs[:known], refs[known : known + rows_in]
    (
        gain_ref, end_ref, bias_ref,
        qkv_ref, normed_ref, weight_ref, own_ref, top_ref, total_ref, mix_ref,
        qt_ref, k_ref, vt_ref, bias_held, scores_ref, rows_held, bias_sem,
    ) = refs[known + rows_in :]
    heads, size, length = vt_ref.shape
    part_length = length // (known + 1)
    turn = pl.program_id(0)
    load = pltpu.make_async_copy(bias_ref, bias_held, bias_sem)

    @pl.when(turn == 0)
    def _():
        load.start()
        for i, piece in enumerate(weights):
            rows = piece.shape[0]
            rows_held[pl.ds(pl.multiple_of(place_ref[i] * rows, rows), rows), :] = piece[...]
        by_columns = rows_held[...].T
        weight_ref[...] = by_columns
        for i, piece in enumerate(pieces):

            @pl.when(slot_ref[i] == group_ref[0])
            def _():
                own_ref[...] = piece[...]

            normed, qkv = token_parts(piece[...], gain_ref[...], by_columns, heads)
            normed_ref[i] = normed
            qkv_ref[i] = qkv
            places = pl.ds(pl.multiple_of(slot_ref[i] * part_length, TILE), part_length)
            for h in range(heads):
                qt_ref[h, :, places] = query_pair(qkv[h])
                k_ref[h, places, :] = key_pair(qkv[heads + h])
                vt_ref[h, :, places] = qkv[2 * heads + h]
        load.wait()

    low, high = range_ref[0], range_ref[1]
    query = low + turn
    own = pl.ds(pl.multiple_of(query * TILE, TILE), TILE)
    state = attend_tiles(
        query, low, full_ref[query], jnp.minimum(most_ref[query], high), empty_state(heads, size),
        end_ref[:, own], [qt_ref[h, :, own] for h in range(heads)],
        k_ref, vt_ref, bias_held, scores_ref,
    )
    for h, (top, total, mix) in enumerate(state):
        top_ref[h, :, own] = top
        total_ref[h, :, own] = total
        mix_ref[h, :, own] = mix


def late_kernel(full_ref, most_ref, slot_ref, group_ref, range_ref, *refs):
    parts = slot_ref.shape[0]
    (
        piece_ref, weight_ref, gain_ref, end_ref, before_ref, top_ref, total_ref, mix_ref, bias_ref,
    ) = refs[:9]
    ots = refs[9 : 9 + parts]
    (
        lse_ref, qkv_ref, normed_ref,
        qt_ref, k_ref, vt_ref, bias_held, scores_ref, held_ref, bias_sem,
    ) = refs[9 + parts :]
    heads, size, length = vt_ref.shape
    count = length // TILE
    each = count // parts
    part_length = length // parts
    query = pl.program_id(0)
    load = pltpu.make_async_copy(bias_ref, bias_held, bias_sem)

    @pl.when(query == 0)
    def _():
        load.start()
        normed, qkv = token_parts(piece_ref[...], gain_ref[...], weight_ref[...], heads)
        normed_ref[0] = normed
        qkv_ref[0] = qkv
        for i in range(parts):
            source = before_ref.at[i] if i < parts - 1 else qkv_ref.at[0]
            places = pl.ds(pl.multiple_of(slot_ref[i] * part_length, TILE), part_length)
            for h in range(heads):
                qt_ref[h, :, places] = query_pair(source[h])
                k_ref[h, places, :] = key_pair(source[heads + h])
                vt_ref[h, :, places] = source[2 * heads + h]
        load.wait()

    low, high = range_ref[0], range_ref[1]
    own = pl.ds(pl.multiple_of(query * TILE, TILE), TILE)
    begun = (query >= low) & (query < high)
    for h in range(heads):
        held_ref[h, 0:1, :] = jnp.where(begun, top_ref[h, :, own], MASKED)
        held_ref[h, 1:2, :] = jnp.where(begun, total_ref[h, :, own], 0.0)
        held_ref[h, 8:, :] = jnp.where(begun, mix_ref[h, :, own], 0.0)
    state = tuple(
        (held_ref[h, 0:1, :], held_ref[h, 1:2, :], held_ref[h, 8:, :]) for h in range(heads)
    )
    most = most_ref[query]
    first = jnp.where(begun & (low == 0), high, 0)
    last = jnp.where(begun & (low > 0), jnp.minimum(low, most), most)
    state = attend_tiles(
        query, first, full_ref[query], last, state,
        end_ref[:, own], [qt_ref[h, :, own] for h in range(heads)],
        k_ref, vt_ref, bias_held, scores_ref,
    )
    turn = (query // each) ^ group_ref[0]
    inner = pl.ds(pl.multiple_of(lax.rem(query, each) * TILE, TILE), TILE)
    mixes = [(mix * (1.0 / total)).astype(bf16) for _, total, mix in state]
    for h, (top, total, _) in enumerate(state):
        lse_ref[h] = top + jnp.log(total) * LOG2E
    for r in range(parts):

        @pl.when(turn == r)
        def _():
            for h in range(heads):
                ots[r][h * size : (h + 1) * size, inner] = mixes[h]


def shape(*dims, kind=bf16):
    return jax.ShapeDtypeStruct(dims, kind)


def sequence_held(heads, size, length, bias):
    return [
        pltpu.VMEM((heads, 2 * size, length), bf16),
        pltpu.VMEM((heads, length, 2 * size), bf16),
        pltpu.VMEM((heads, size, length), bf16),
        pltpu.VMEM(bias.shape, f32),
        pltpu.VMEM((2, heads, TILE, TILE), f32),
    ]


def attend_early(pieces, weights, places, gain, bias, end, full, most, slots, group, known):
    parts = len(pieces) + 1
    part_length, width = pieces[0].shape
    columns = weights[0].shape[1]
    heads = bias.shape[0]
    size = columns // (3 * heads)
    length = parts * part_length
    smem = pl.BlockSpec(memory_space=pltpu.SMEM)
    hbm = pl.BlockSpec(memory_space=pl.ANY)
    outs = [
        shape(parts - 1, 3 * heads, size, part_length),
        shape(parts - 1, part_length, width),
        shape(columns, width),
        shape(part_length, width),
        shape(heads, 1, length, kind=f32),
        shape(heads, 1, length, kind=f32),
        shape(heads, size, length, kind=f32),
    ]
    dense = (*pieces, *weights, gain, end)
    return pl.pallas_call(
        early_kernel,
        grid=((parts - 1) * part_length // TILE,),
        in_specs=[smem] * 6 + [whole(a.shape) for a in dense] + [hbm],
        out_specs=[whole(a.shape) for a in outs],
        out_shape=outs,
        scratch_shapes=sequence_held(heads, size, length, bias)
        + [pltpu.VMEM((width, columns), bf16), pltpu.SemaphoreType.DMA],
        compiler_params=params(),
        cost_estimate=cost(20),
        name="attend_early",
    )(full, most, slots, group, known, places, *dense, bias)


def attend_late(piece, weight, gain, bias, end, full, most, slots, group, known, qkv, state):
    part_length, width = piece.shape
    parts, heads = qkv.shape[0] + 1, bias.shape[0]
    size = qkv.shape[2]
    length = parts * part_length
    smem = pl.BlockSpec(memory_space=pltpu.SMEM)
    hbm = pl.BlockSpec(memory_space=pl.ANY)
    outs = [
        *[shape(heads * size, part_length)] * parts,
        shape(heads, 1, length, kind=f32),
        shape(1, 3 * heads, size, part_length),
        shape(1, part_length, width),
    ]
    out_specs = [whole(a.shape) for a in outs]
    out_specs[parts] = pl.BlockSpec((heads, 1, TILE), lambda i: (0, 0, i))
    dense = (piece, weight, gain, end, qkv, *state)
    return pl.pallas_call(
        late_kernel,
        grid=(length // TILE,),
        in_specs=[smem] * 5 + [whole(a.shape) for a in dense] + [hbm],
        out_specs=out_specs,
        out_shape=outs,
        scratch_shapes=sequence_held(heads, size, length, bias)
        + [pltpu.VMEM((heads, size + 8, TILE), f32), pltpu.SemaphoreType.DMA],
        compiler_params=params(),
        cost_estimate=cost(15),
        name="attend_late",
    )(full, most, slots, group, known, *dense, bias)

def backward_kernel(least_ref, clear_ref, slot_ref, group_ref, *refs):
    parts = slot_ref.shape[0]
    grads, ots = refs[:parts], refs[parts : 2 * parts]
    (
        qkv_early, qkv_late, lse_ref, end_ref, weight_ref, bias_ref,
    ) = refs[2 * parts : 2 * parts + 6]
    outs = refs[2 * parts + 6 : 3 * parts + 6]
    qkv_ref = [qkv_early.at[i] for i in range(parts - 1)] + [qkv_late.at[0]]
    (
        dqkv_ref, band_out,
        qt_ref, kt_ref, vt_ref, got_ref, pair_ref,
        dqt_acc, dk_acc, dv_acc, delta_ref, band_ref, bias_held, bias_sem, band_sem,
    ) = refs[3 * parts + 6 :]
    heads, size, length = qt_ref.shape
    columns = heads * size
    count = length // TILE
    each = count // parts
    part_length = length // parts
    key = pl.program_id(0)
    key_cols = pl.ds(pl.multiple_of(key * TILE, TILE), TILE)
    load = pltpu.make_async_copy(bias_ref, bias_held, bias_sem)
    store = pltpu.make_async_copy(band_ref, band_out, band_sem)
    every = range(heads)

    @pl.when(key == 0)
    def _():
        load.start()
        dqt_acc[...] = jnp.zeros_like(dqt_acc)
        band_ref[...] = jnp.zeros_like(band_ref)
        for i in range(parts):
            places = pl.ds(pl.multiple_of(slot_ref[i] * part_length, TILE), part_length)
            for h in every:
                qt_ref[h, :, places] = qkv_ref[i][h]
                pair_ref[h, :, places] = query_pair(qkv_ref[i][h])
                kt_ref[h, :, places] = qkv_ref[i][heads + h]
                vt_ref[h, :, places] = qkv_ref[i][2 * heads + h]
        for turn in range(parts):
            part = group_ref[0] ^ turn
            places = pl.ds(pl.multiple_of(part * part_length, TILE), part_length)
            for h in every:
                rows = slice(h * size, (h + 1) * size)
                grad = grads[turn][rows, :]
                got_ref[h, :, places] = grad
                delta_ref[h, :, places] = jnp.sum(
                    ots[turn][rows, :].astype(f32) * grad.astype(f32), axis=0, keepdims=True
                )
        load.wait()

    dk_acc[...] = jnp.zeros_like(dk_acc)
    dv_acc[...] = jnp.zeros_like(dv_acc)
    kt = [kt_ref[h, :, key_cols] for h in every]
    k = [key_pair(tile) for tile in kt]
    v = [vt_ref[h, :, key_cols].T for h in every]

    def step(query, masked):
        cols = pl.ds(pl.multiple_of(query * TILE, TILE), TILE)
        place = key - query + count - 1
        scores = [dot(k[h], pair_ref[h, :, cols]) + bias_held[h, place] for h in every]
        if masked:
            keep = lax.broadcasted_iota(jnp.int32, (TILE, TILE), 0) + key * TILE < end_ref[:, cols]
            scores = [jnp.where(keep, tile, MASKED) for tile in scores]
        grad_weights = [dot(v[h], got_ref[h, :, cols]) for h in every]
        weights = [jnp.exp2(scores[h] - lse_ref[h, :, cols]) for h in every]
        grad_scores = [weights[h] * (grad_weights[h] - delta_ref[h, :, cols]) for h in every]
        for h in every:
            band_ref[h, place] += grad_scores[h]
        rounded = [tile.astype(bf16) for tile in grad_scores]
        weights = [tile.astype(bf16) for tile in weights]
        for h in every:
            dv_acc[h] += dot(got_ref[h, :, cols], weights[h], ((1,), (1,)))
        for h in every:
            dk_acc[h] += dot(qt_ref[h, :, cols], rounded[h], ((1,), (1,)))
        for h in every:
            dqt_acc[h, :, cols] += dot(kt[h], rounded[h])

    def edge_step(query, _):
        step(query, True)
        return 0

    def full_step(query, _):
        step(query, False)
        return 0

    lax.fori_loop(least_ref[key], clear_ref[key], edge_step, 0)
    lax.fori_loop(clear_ref[key], count, full_step, 0)
    slot = jnp.int32(0)
    for i in range(parts):
        slot = jnp.where(slot_ref[i] == key // each, i, slot)
    inner = pl.ds(pl.multiple_of(lax.rem(key, each) * TILE, TILE), TILE)
    for h in every:
        dqkv_ref[slot, columns + h * size : columns + (h + 1) * size, inner] = dk_acc[h].astype(bf16)
        dqkv_ref[slot, 2 * columns + h * size : 2 * columns + (h + 1) * size, inner] = (
            dv_acc[h].astype(bf16)
        )

    @pl.when(key == count - 1)
    def _():
        for i in range(parts):
            places = pl.ds(pl.multiple_of(slot_ref[i] * part_length, TILE), part_length)
            for h in every:
                dqkv_ref[i, h * size : (h + 1) * size, :] = dqt_acc[h, :, places].astype(bf16)
        store.start()
        weight = weight_ref[...]
        for i in reversed(range(parts)):
            outs[i][...] = dot(dqkv_ref[i], weight, ((0,), (0,))).astype(bf16)
        store.wait()


def sums_kernel(group_ref, place_ref, *refs):
    (
        dqkv_ref, normed_early, normed_late, weight_ref, gain_ref, feed_gain_ref, bucket_ref, band_in, small_ref,
    ) = refs[:9]
    share_refs = refs[9:-4]
    band_ref, sum_ref, line_ref, band_sem = refs[-4:]
    load = pltpu.make_async_copy(band_in, band_ref, band_sem)
    load.start()
    parts = dqkv_ref.shape[0]
    every = range(band_ref.shape[0])
    normed_ref = [normed_early.at[i] for i in range(parts - 1)] + [normed_late.at[0]]
    weight = weight_ref[...]
    total = dot(dqkv_ref[0], normed_ref[0][...])
    for i in range(1, parts):
        total = total + dot(dqkv_ref[i], normed_ref[i][...])
    sum_ref[...] = total.T
    place = 0
    for share in share_refs:
        for i in range(share.shape[0]):
            rows = share.shape[1]
            at = pl.ds(pl.multiple_of(place_ref[place] * rows, rows), rows)
            share[i] = sum_ref[at, :].astype(bf16)
            place += 1

    small_ref[...] = jnp.zeros_like(small_ref)
    gain_grad = jnp.sum(total * weight.astype(f32), axis=0, keepdims=True) / gain_ref[...]
    lanes = small_ref.shape[1]
    each_gain = weight.shape[1] // lanes
    for row in range(each_gain):
        cut = slice(row * lanes, (row + 1) * lanes)
        small_ref[row : row + 1, :] = gain_grad[:, cut]
        small_ref[each_gain + row : each_gain + row + 1, :] = feed_gain_ref[:, cut]

    line_ref[...] = jnp.zeros_like(line_ref)
    load.wait()
    tiles = band_ref.shape[1]

    def one(pair, _):
        bands = [(place, h) for place in (2 * pair, 2 * pair + 1) for h in every]
        zero = jnp.zeros((TILE // 2, TILE // 2), f32)
        lines = []
        for place, h in bands:
            upper, lower = band_ref[h, place, : TILE // 2], band_ref[h, place, TILE // 2 :]
            lines.append(
                jnp.concatenate([zero, zero, upper], axis=1)
                + jnp.concatenate([zero, lower, zero], axis=1)
            )
        half = TILE // 4
        while half >= 1:
            turned = [pltpu.roll(line[half:], 2 * TILE - half, 1) for line in lines]
            lines = [line[:half] + turn for line, turn in zip(lines, turned)]
            half //= 2
        for (place, h), line in zip(bands, lines):
            start = pl.multiple_of((tiles - 1 - place) * TILE, TILE)
            line_ref[h : h + 1, pl.ds(start, 2 * TILE)] += line
        return 0

    lax.fori_loop(0, tiles // 2, one, 0)
    line = line_ref[0:8, :]
    terms = []
    for _ in range(3):
        term = line.astype(bf16)
        terms.append(term)
        line = line - term.astype(f32)
    names = lax.broadcasted_iota(jnp.int32, (lanes, line_ref.shape[1]), 0)
    onehot = jnp.where(lax.rem(names, lanes // 4) == bucket_ref[...], 1.0, 0.0).astype(bf16)
    sums = [dot(term, onehot, ((1,), (1,))) for term in terms]
    sums = sums[0] + sums[1] + sums[2]
    lane = lax.broadcasted_iota(jnp.int32, (1, lanes), 1)
    table = jnp.zeros((1, lanes), f32)
    for h in every:
        mine = (lane >= h * (lanes // 4)) & (lane < (h + 1) * (lanes // 4))
        table = jnp.where(mine, sums[h : h + 1], table)
    small_ref[pl.ds(2 * each_gain + group_ref[0], 1), :] = table


def attend_backward(grads, ots, qkv, lse, end, weight, bias, least, clear, slots, group):
    parts = len(grads)
    _, triple, size, part_length = qkv[0].shape
    heads, length = triple // 3, parts * part_length
    columns, width = weight.shape
    smem = pl.BlockSpec(memory_space=pltpu.SMEM)
    hbm = pl.BlockSpec(memory_space=pl.ANY)
    dense = [*grads, *ots, *qkv, lse, end, weight]
    outs = [shape(part_length, width)] * parts + [shape(parts, columns, part_length)]
    by_columns = pltpu.VMEM((heads, size, length), bf16)
    return pl.pallas_call(
        backward_kernel,
        grid=(length // TILE,),
        in_specs=[smem] * 4 + [whole(a.shape) for a in dense] + [hbm],
        out_specs=[whole(a.shape) for a in outs] + [hbm],
        out_shape=outs + [shape(*bias.shape, kind=f32)],
        scratch_shapes=[by_columns] * 4
        + [
            pltpu.VMEM((heads, 2 * size, length), bf16),
            pltpu.VMEM((heads, size, length), f32),
            pltpu.VMEM((heads, size, TILE), f32),
            pltpu.VMEM((heads, size, TILE), f32),
            pltpu.VMEM((heads, 1, length), f32),
            pltpu.VMEM(bias.shape, f32),
            pltpu.VMEM(bias.shape, f32),
            pltpu.SemaphoreType.DMA,
            pltpu.SemaphoreType.DMA,
        ],
        compiler_params=params(),
        cost_estimate=cost(45),
        name="attend_backward",
    )(least, clear, slots, group, *dense, bias)


def attend_sums(dqkv, normed, weight, gain, feed_gain_grad, bucket, bands, group, places, shares):
    parts, columns, _ = dqkv.shape
    width = weight.shape[1]
    smem = pl.BlockSpec(memory_space=pltpu.SMEM)
    dense = [dqkv, *normed, weight, gain.reshape(1, width), feed_gain_grad, bucket]
    outs = [shape(2 * (width // 128) + parts, 128, kind=f32)]
    outs += [shape(number, rows, columns) for number, rows in shares]
    return pl.pallas_call(
        sums_kernel,
        in_specs=[smem] * 2
        + [whole(a.shape) for a in dense]
        + [pl.BlockSpec(memory_space=pl.ANY)],
        out_specs=[whole(a.shape) for a in outs],
        out_shape=outs,
        scratch_shapes=[
            pltpu.VMEM(bands.shape, f32),
            pltpu.VMEM((width, columns), f32),
            pltpu.VMEM((8, bucket.shape[1]), f32),
            pltpu.SemaphoreType.DMA,
        ],
        compiler_params=params(),
        cost_estimate=cost(12),
        name="attend_sums",
    )(group, places, *dense, bands)


def middle_kernel(turn_ref, *refs):
    parts = turn_ref.shape[0]
    mixes = refs[:parts]
    x_ref, g_ref, gain_ref, weight_ref, out_ref, gain_grad_ref = refs[parts : parts + 6]
    gots = refs[parts + 6 : 2 * parts + 6]
    (
        grads_ref, w_ref, grad_ref, second_ref, acc_ref, back_ref, gh_ref, load_sem, store_sem,
    ) = refs[2 * parts + 6 :]
    width = x_ref.shape[1]
    columns = mixes[0].shape[0]
    feed = weight_ref.shape[3] - 256
    hidden_units = feed // 2
    late, early = pl.ds(feed, 256), pl.ds(0, feed)

    def load(z, which, cols):
        return pltpu.make_async_copy(
            weight_ref.at[:, z, :, cols], w_ref.at[z, :, :, cols], load_sem.at[z, which]
        )

    def store(z, which, cols):
        return pltpu.make_async_copy(
            grad_ref.at[z, :, :, cols], grads_ref.at[:, z, :, cols], store_sem.at[z, which]
        )

    for z in range(parts):
        load(z, 0, late).start()
    for z in range(parts):
        load(z, 1, early).start()
    for z in range(parts):
        load(z, 0, late).wait()

    def output_rows(turn):
        return w_ref[turn_ref[turn], :, :, feed : feed + columns].reshape(width, columns)

    hidden = x_ref[...].astype(f32)
    for turn in range(parts):
        hidden = hidden + dot(mixes[turn][...], output_rows(turn), ((0,), (1,)))
    inverse = lax.rsqrt(jnp.mean(hidden * hidden, axis=-1, keepdims=True) + EPSILON)
    second_ref[...] = (hidden * inverse * gain_ref[...]).astype(bf16)
    acc_ref[...] = hidden
    back_ref[...] = jnp.zeros_like(back_ref)
    gh_ref[...] = hidden * inverse

    def hidden_part(z, _):
        load(z, 1, early).wait()
        inner = w_ref[z, :, :, :hidden_units].reshape(width, hidden_units)
        outer = w_ref[z, :, :, hidden_units:feed].reshape(width, hidden_units)
        second = second_ref[...]
        grad = g_ref[...]
        units = dot(second, inner)
        grad_active = dot(grad, outer).astype(bf16).astype(f32)
        active, slope = gelu_parts(units)
        active = active.astype(bf16)
        grad_units = (grad_active * slope).astype(bf16)
        acc_ref[...] += dot(active, outer, ((1,), (1,)))
        back_ref[...] += dot(grad_units, inner, ((1,), (1,)))
        shape = (*grad_ref.shape[1:3], hidden_units)
        grad_ref[z, :, :, :hidden_units] = (
            dot(second, grad_units, ((0,), (0,))).astype(bf16).reshape(shape)
        )
        grad_ref[z, :, :, hidden_units:feed] = (
            dot(grad, active, ((0,), (0,))).astype(bf16).reshape(shape)
        )
        store(z, 1, early).start()
        return 0

    lax.fori_loop(0, parts, hidden_part, 0)
    out_ref[0] = acc_ref[...].astype(bf16)
    scaled = gh_ref[...]
    grad_second = back_ref[...]
    gain_grad_ref[...] = jnp.sum(grad_second * scaled, axis=0, keepdims=True)
    grad_scaled = grad_second * gain_ref[...]
    grad_hidden = g_ref[...].astype(f32) + inverse * (
        grad_scaled - scaled * jnp.mean(grad_scaled * scaled, axis=-1, keepdims=True)
    )
    rounded = grad_hidden.astype(bf16)
    out_ref[1] = rounded
    for turn in range(parts):
        gots[turn][...] = dot(output_rows(turn), rounded, ((0,), (1,))).astype(bf16)
        grads = dot(rounded, mixes[turn][...], ((0,), (1,))).astype(bf16)
        grad_ref[turn_ref[turn], :, :, feed : feed + columns] = grads.reshape(
            *grad_ref.shape[1:3], columns
        )
        grad_ref[turn_ref[turn], :, :, feed + columns :] = jnp.zeros(
            (*grad_ref.shape[1:3], 256 - columns), bf16
        )
    for z in range(parts):
        store(z, 0, late).start()
    for z in range(parts):
        store(z, 0, late).wait()
        store(z, 1, early).wait()


def middle(turns, mixes, inputs, cotangent, gain, weights):
    rows, width = inputs.shape
    owners, parts, each, columns = weights.shape
    smem = pl.BlockSpec(memory_space=pltpu.SMEM)
    hbm = pl.BlockSpec(memory_space=pl.ANY)
    held = pltpu.VMEM((parts, owners, each, columns), bf16)
    dense = [*mixes, inputs, cotangent, gain.reshape(1, width)]
    outs = [
        jax.ShapeDtypeStruct((2, rows, width), bf16),
        jax.ShapeDtypeStruct((1, width), f32),
        *[jax.ShapeDtypeStruct(mix.shape, bf16) for mix in mixes],
    ]
    return pl.pallas_call(
        middle_kernel,
        in_specs=[smem] + [whole(a.shape) for a in dense] + [hbm],
        out_specs=[whole(a.shape) for a in outs] + [hbm],
        out_shape=outs + [jax.ShapeDtypeStruct(weights.shape, bf16)],
        scratch_shapes=[
            held,
            held,
            pltpu.VMEM((rows, width), bf16),
            pltpu.VMEM((rows, width), f32),
            pltpu.VMEM((rows, width), f32),
            pltpu.VMEM((rows, width), f32),
            pltpu.SemaphoreType.DMA((parts, 2)),
            pltpu.SemaphoreType.DMA((parts, 2)),
        ],
        compiler_params=params(),
        name="middle",
    )(turns, *dense, weights)


def flat(pairs, parts):
    return [(c * parts + z, d * parts + y) for (c, z), (d, y) in pairs]


def routes(parts):
    half = parts // 2
    devices = [(c, z) for c in range(2) for z in range(parts)]

    def group(c, z):
        return (z % half) * 2 + c

    gather = [
        flat([((0, z), (0, z - 1)) for z in (1, 2, 3)] + [((1, z), (1, z + 1)) for z in (0, 1, 2)], parts),
        flat([((0, z), (0, z - 1)) for z in (1, 2)] + [((1, z), (1, z + 1)) for z in (1, 2)], parts),
        flat([((0, 1), (0, 0)), ((0, 0), (0, 1)), ((1, 2), (1, 3)), ((1, 3), (1, 2))], parts),
    ]
    rounds = [
        flat([((c, z), (c ^ (r % half), z ^ (r // half))) for c, z in devices], parts)
        for r in range(parts)
    ]
    owners = flat([((c, z), (z // half, group(c, z))) for c, z in devices], parts)
    weights = [
        flat([((z // half ^ flip, group(c, z)), (c, z)) for c, z in devices], parts)
        for flip in range(2)
    ]
    return gather, rounds, owners, weights


def back(pairs):
    return [(target, source) for source, target in pairs]


SWAP = [(0, 1), (1, 0)]
LINE = ("core", "tensor")


def after(value, *earlier):
    return lax.optimization_barrier((value, *earlier))[0]


def across(value, step):
    return lax.ppermute(value, "plane", [(i, i ^ step) for i in range(lax.axis_size("plane"))])


def body(
    inputs,
    attention_gain,
    feedforward_gain,
    query_weight,
    key_weight,
    value_weight,
    output_weight,
    inner_weight,
    outer_weight,
    bias_table,
    block_index,
    position_bucket,
    cotangent,
):
    length = block_index.shape[1]
    parts = lax.axis_size("tensor")
    planes = lax.axis_size("plane")
    factor = 1.0 / math.sqrt(block_index.shape[0] * length * planes * 2)
    heads = bias_table.shape[1]
    buckets = bias_table.shape[0]
    width = inputs.shape[1]
    size = query_weight.shape[1] // heads
    columns = heads * size
    each = query_weight.shape[0]
    hidden_units = inner_weight.shape[1]
    core, z, plane = lax.axis_index("core"), lax.axis_index("tensor"), lax.axis_index("plane")
    half = parts // 2
    lower = z < half
    owner = core == z // half
    outer_chip = (z == 0) | (z == parts - 1)
    group = (z % half) * 2 + core
    group_ref = group.reshape(1)
    square = planes == 4 and each % 16 == 0
    gather, rounds, owners, weight_routes = routes(parts)
    tiles = length // TILE
    at_start = (z == 0) | (z == half)
    known = jnp.where(at_start, jnp.array([0, tiles - tiles // parts]), jnp.array([tiles // parts, tiles]))
    known = known.astype(jnp.int32)
    slots = jnp.array([[0, 1, 2, 3], [1, 2, 3, 0], [2, 1, 0, 3], [3, 2, 1, 0]], jnp.int32)[z]

    def swap(value):
        return lax.ppermute(value, "core", SWAP)

    pad = jnp.zeros((each, 256 - columns), bf16)
    packed_rest = jnp.concatenate([inner_weight, outer_weight.T, output_weight.T, pad], axis=1)

    packed = jnp.concatenate([query_weight, key_weight, value_weight], axis=1)
    first = lax.ppermute(inputs, LINE, gather[0])
    first, table, block_row, packed, packed_rest = lax.optimization_barrier(
        (first, bias_table, jnp.where(owner, block_index, swap(block_index)), packed, packed_rest)
    )
    table = lax.ppermute(table, LINE, weight_routes[0])
    block_row = block_row[0]
    line_rest = lax.all_gather(packed_rest, "tensor", axis=0)
    one, two = (lax.ppermute(packed, LINE, route) for route in weight_routes)
    second = lax.ppermute(first, LINE, gather[1])
    rows, bucket = bias_rows(table, position_bucket)
    bias = bias_tiles(rows, length)
    one, two = after((one, two), bias)
    low, high = jnp.where(lower, one, two), jnp.where(lower, two, one)
    if square:
        low_x, high_y = across(low, 1), across(high, 2)
        low_y, high_x = across(low, 2), across(high, 1)
        low_xy, high_xy = across(low_x, 2), across(high_y, 1)
        weights = [low, high, low_x, high_x, low_y, high_y, low_xy, high_xy]
        order = plane ^ jnp.arange(planes, dtype=jnp.int32)
        places = jnp.stack([order * 2, order * 2 + 1], axis=1).reshape(-1)
    else:
        both = lax.all_gather(jnp.stack([low, high]), "plane", axis=0)
        weights = [both.reshape(width, 3 * columns)]
        places = jnp.zeros((1,), jnp.int32)
    end, full, most, least, clear = spans(block_row)
    marks = (attention_gain.reshape(1, width), bias, end, full, most, slots, group_ref, known)
    pieces = [jnp.where(owner, piece, swap(piece)) for piece in (inputs, first)]
    second, pieces, weights, places, marks, least, clear = lax.optimization_barrier(
        (second, pieces, weights, places, marks, least, clear)
    )
    third = lax.ppermute(jnp.where(outer_chip, inputs, second), LINE, gather[2])
    pieces = [*pieces, jnp.where(owner, second, swap(second))]
    all_rest = lax.all_gather(after(line_rest, second), ("plane", "core"), axis=0)


    _, bias, end, full, most, slots, group_ref, known = marks
    qkv, normed, weight, own_tokens, *state = attend_early(pieces, weights, places, *marks)
    third, state, cotangent = lax.optimization_barrier((third, state, cotangent))
    grad = lax.ppermute(cotangent, LINE, back(owners))
    third = jnp.where(owner, third, swap(third))
    *ots, lse, late_qkv, late_normed = attend_late(third, weight, *marks, qkv, state)
    qkv, normed = (qkv, late_qkv), (normed, late_normed)
    mixes = [ots[0]] + [lax.ppermute(ots[r], LINE, rounds[r]) for r in range(1, parts)]
    turns = (group ^ jnp.arange(parts)).astype(jnp.int32)
    if each % 16:
        all_rest = jnp.swapaxes(all_rest, 0, 1).reshape(1, parts, width, -1)
    results, feedforward_part, *gots, grads = middle(
        turns, mixes, own_tokens, grad, feedforward_gain, all_rest
    )
    if each % 16:
        grads = jnp.swapaxes(grads.reshape(parts, planes * 2, each, -1), 0, 1)
    gots = [gots[0]] + [lax.ppermute(gots[r], LINE, rounds[r]) for r in range(1, parts)]
    if square:
        order = plane ^ jnp.array([1, 3, 0, 2, 2, 3, 0, 1], jnp.int32)
        places = order * 2 + jnp.array([0, 0, 0, 0, 1, 1, 1, 1], jnp.int32)
        shares = [(2, each)] * 4
    else:
        places, shares = jnp.zeros((1,), jnp.int32), [(1, width)]
    gots, results, places, bucket = lax.optimization_barrier((gots, results, places, bucket))
    results = lax.ppermute(results, LINE, owners)

    rest = lax.psum_scatter(grads, ("plane", "core"), scatter_dimension=0)

    own, first, second, third, dqkv, bands = attend_backward(
        gots, ots, qkv, lse, end, weight, bias, least, clear, slots, group_ref
    )
    third, results = lax.optimization_barrier((third, results))
    layer_output, grad_hidden = results[0], results[1].astype(f32)
    third = third + swap(third)
    got = lax.ppermute(third, LINE, back(gather[2]))
    own, first, second = (part + swap(part) for part in (own, first, second))

    def small_step(small, axis, step):
        count = lax.axis_size(axis)
        return small + lax.ppermute(small, axis, [(i, i ^ step) for i in range(count)])

    dqkv, bands, third = lax.optimization_barrier((dqkv, bands, third))
    small, *weight_grads = attend_sums(
        dqkv, normed, weight, attention_gain, feedforward_part, bucket, bands, group_ref, places, shares
    )
    none = jnp.zeros_like(own)
    got, small, weight_grads, rest = lax.optimization_barrier((got, small, weight_grads, rest))
    rest = lax.psum_scatter(rest, "tensor", scatter_dimension=0)
    own = jnp.where(owner, jnp.where(outer_chip, own + got, own), none)
    second = jnp.where(outer_chip, second, second + got)
    got = lax.ppermute(second, LINE, back(gather[1]))
    if square:
        low_send, low, high_send, high = weight_grads
        low, high = low + across(low_send, 1), high + across(high_send, 2)
    else:
        low = high = weight_grads[0].reshape(planes, 2, each, 3 * columns)
    small = small_step(small, "core", 1)
    small = small_step(small, "tensor", 1)
    got, low, high, small = lax.optimization_barrier((got, low, high, small))
    first = jnp.where(owner, first, none) + got
    got = lax.ppermute(first, LINE, back(gather[0]))
    if square:
        low, high = low[0] + across(low[1], 2), high[0] + across(high[1], 1)
    else:
        shared = lax.psum_scatter(low, "plane", scatter_dimension=0)
        low, high = shared[0], shared[1]
    small = small_step(small, "tensor", 2)
    step = 1
    while step < planes:
        small = small_step(small, "plane", step)
        step *= 2
    attention_share = (
        lax.ppermute(jnp.where(lower, low, high), LINE, back(weight_routes[0]))
        + lax.ppermute(jnp.where(lower, high, low), LINE, back(weight_routes[1]))
    ).astype(f32) * factor
    small = small * factor
    rest_share = rest.astype(f32) * factor
    grad_first = (own + got).astype(f32)
    scaled_first, inverse_first, _ = norm_forward(inputs.astype(f32), attention_gain)
    input_grad = (
        grad_hidden + norm_backward(grad_first, scaled_first, inverse_first, attention_gain)
    ).astype(bf16)
    gain_rows = width // 128
    table_grad = small[2 * gain_rows :, : heads * 32].reshape(parts * heads, 32)[:, :buckets].T

    return (
        layer_output,
        input_grad,
        small[:gain_rows].reshape(width),
        small[gain_rows : 2 * gain_rows].reshape(width),
        attention_share[:, :columns],
        attention_share[:, columns : 2 * columns],
        attention_share[:, 2 * columns :],
        rest_share[:, 2 * hidden_units : 2 * hidden_units + columns].T,
        rest_share[:, :hidden_units],
        rest_share[:, hidden_units : 2 * hidden_units].T,
        table_grad,
    )


def solution(mesh):
    groups, parts = mesh.devices.shape
    fine = Mesh(mesh.devices.reshape(groups // 2, 2, parts), ("plane", "core", "tensor"))
    dp = ("plane", "core")
    tokens = P(("plane", "core", "tensor"), None)
    by_rows = P(dp, "tensor")
    by_columns = P("tensor", dp)
    placed = (
        tokens, P(), P(), by_rows, by_rows, by_rows, by_columns, by_rows, by_columns,
        P(None, "tensor"), P(dp, None), P(), tokens,
    )
    results = (
        tokens, tokens, P(), P(), by_rows, by_rows, by_rows, by_columns, by_rows, by_columns, P(),
    )
    return jax.shard_map(body, mesh=fine, in_specs=placed, out_specs=results, check_vma=False)
```

```python
import math

import jax
import jax.numpy as jnp
from jax import lax
from jax.experimental import pallas as pl
from jax.experimental.pallas import tpu as pltpu
from jax.sharding import Mesh, PartitionSpec as P

H = 12
EPSILON = 1e-06
MASKED = -1e30
LOG2E = 1.4426950408889634
TILE = 256
AHEAD = 2
BLOCKS = 8
VMEM_LIMIT = 60 * 1024 * 1024
f32, bf16 = jnp.float32, jnp.bfloat16


def dot(left, right, contract=((1,), (0,))):
    return lax.dot_general(left, right, (contract, ((), ())), preferred_element_type=f32)


def norm_forward(values, gain):
    inverse = lax.rsqrt(jnp.mean(values * values, axis=-1, keepdims=True) + EPSILON)
    scaled = values * inverse
    return scaled, inverse, (scaled * gain).astype(bf16)


def norm_backward(grad_normed, scaled, inverse, gain):
    grad_scaled = grad_normed * gain
    return inverse * (
        grad_scaled - scaled * jnp.mean(grad_scaled * scaled, axis=-1, keepdims=True)
    )


def gelu_parts(values):
    cumulative = 0.5 * (1.0 + lax.erf(values * (1.0 / math.sqrt(2.0))))
    density = jnp.exp(-0.5 * values * values) * (1.0 / math.sqrt(2.0 * math.pi))
    return values * cumulative, cumulative + values * density


def whole(shape):
    return pl.BlockSpec(shape, lambda *_: (0,) * len(shape), pipeline_mode=pl.Buffered(1))


def params():
    return pltpu.CompilerParams(vmem_limit_bytes=VMEM_LIMIT)


def cost(microseconds):
    return pl.CostEstimate(flops=microseconds * 10**9, bytes_accessed=0, transcendentals=0)


def bias_rows(bias_table, position_bucket):
    length = (position_bucket.shape[0] + 1) // 2
    bucket = jnp.concatenate([position_bucket, jnp.zeros((1,), jnp.int32)])[::-1]
    bucket = bucket[(length // TILE - 1 - AHEAD) * TILE :]
    names = jnp.arange(bias_table.shape[0], dtype=jnp.int32)
    onehot = (bucket[None, :] == names[:, None]).astype(f32)
    rows = lax.dot_general(
        bias_table, onehot, (((0,), (0,)), ((), ())), precision=lax.Precision.HIGHEST
    )
    return rows[:, None, :] * LOG2E, bucket[None, :]


def bias_kernel(row_ref, out_ref):
    tiles = out_ref.shape[1]

    def one(place, _):
        start = pl.multiple_of((tiles - 1 - place) * TILE, TILE)
        piece = row_ref[0, :, pl.ds(start, 2 * TILE)]
        spread = jnp.broadcast_to(piece, (TILE, 2 * TILE))
        out_ref[0, place] = pltpu.roll(spread, 0, 1, stride=1, stride_axis=0)[:, TILE:]
        return 0

    lax.fori_loop(0, tiles, one, 0)


def bias_tiles(rows, length):
    heads = rows.shape[0]
    tiles = length // TILE + AHEAD
    return pl.pallas_call(
        bias_kernel,
        grid=(heads,),
        in_specs=[pl.BlockSpec((1, 1, rows.shape[2]), lambda h: (h, 0, 0))],
        out_specs=pl.BlockSpec((1, tiles, TILE, TILE), lambda h: (h, 0, 0, 0)),
        out_shape=jax.ShapeDtypeStruct((heads, tiles, TILE, TILE), f32),
        compiler_params=params(),
        cost_estimate=cost(6),
        name="bias_tiles",
    )(rows)


def spans(block_row):
    length = block_row.shape[0]
    names = jnp.arange(BLOCKS, dtype=jnp.int32)[:, None]
    upto = jnp.sum(block_row[None, :] <= names, axis=1, dtype=jnp.int32)
    end = jnp.sum(jnp.where(block_row[None, :] == names, upto[:, None], 0), axis=0, dtype=jnp.int32)
    by_tile = end.reshape(length // TILE, TILE)
    full = by_tile[:, 0] // TILE
    most = (by_tile[:, TILE - 1] + TILE - 1) // TILE
    places = jnp.arange(length // TILE, dtype=jnp.int32)[:, None]
    least = jnp.sum(most[None, :] <= places, axis=1, dtype=jnp.int32)
    clear = jnp.sum(full[None, :] <= places, axis=1, dtype=jnp.int32)
    return end.reshape(1, length), full, most, least, clear


def query_pair(queries):
    scaled = queries.astype(f32) * LOG2E
    high = scaled.astype(bf16)
    return jnp.concatenate([high, (scaled - high.astype(f32)).astype(bf16)], axis=0)


def key_pair(keys):
    return jnp.concatenate([keys, keys], axis=0).T


def token_parts(piece, gain, by_columns, heads):
    tokens = piece.astype(f32)
    inverse = lax.rsqrt(jnp.mean(tokens * tokens, axis=-1, keepdims=True) + EPSILON)
    normed = (tokens * inverse * gain).astype(bf16)
    qkv = dot(by_columns, normed, ((1,), (1,))).astype(bf16)
    return normed, qkv.reshape(3 * heads, -1, normed.shape[0])


def attend_tiles(query, first, clear, last, state, end, queries, k_ref, vt_ref, bias_held, scores_ref):
    heads = len(queries)
    count = k_ref.shape[1] // TILE

    def scores(key):
        rows = pl.ds(pl.multiple_of(key * TILE, TILE), TILE)
        place = jnp.minimum(key - query + count - 1, bias_held.shape[1] - 1)
        return [dot(k_ref[h, rows, :], queries[h]) + bias_held[h, place] for h in range(heads)]

    def step(key, state, masked):
        slot = lax.rem(key, 2)
        ahead = scores(jnp.minimum(key + 1, last - 1))
        current = [scores_ref[slot, h] for h in range(heads)]
        start = pl.multiple_of(key * TILE, TILE)
        if masked:
            keep = lax.broadcasted_iota(jnp.int32, (TILE, TILE), 0) + start < end
            current = [jnp.where(keep, tile, MASKED) for tile in current]
        tops = [
            jnp.maximum(state[h][0], jnp.max(current[h], axis=0, keepdims=True))
            for h in range(heads)
        ]
        weights = [jnp.exp2(current[h] - tops[h]) for h in range(heads)]
        result = []
        for h in range(heads):
            top, total, mix = state[h]
            scale = jnp.exp2(top - tops[h])
            total = total * scale + jnp.sum(weights[h], axis=0, keepdims=True)
            mix = mix * scale + dot(vt_ref[h, :, pl.ds(start, TILE)], weights[h].astype(bf16))
            result.append((tops[h], total, mix))
        for h in range(heads):
            scores_ref[1 - slot, h] = ahead[h]
        return tuple(result)

    begin = jnp.minimum(first, count - 1)
    for h, tile in enumerate(scores(begin)):
        scores_ref[lax.rem(begin, 2), h] = tile
    clear = jnp.clip(clear, first, jnp.maximum(first, last))
    state = lax.fori_loop(first, clear, lambda key, s: step(key, s, False), state)
    return lax.fori_loop(clear, last, lambda key, s: step(key, s, True), state)


def empty_state(heads, size):
    return tuple(
        (jnp.full((1, TILE), MASKED, f32), jnp.zeros((1, TILE), f32), jnp.zeros((size, TILE), f32))
        for _ in range(heads)
    )


def early_kernel(full_ref, most_ref, slot_ref, group_ref, range_ref, place_ref, *refs):
    known, rows_in = slot_ref.shape[0] - 1, place_ref.shape[0]
    pieces, weights = refs[:known], refs[known : known + rows_in]
    (
        gain_ref, end_ref, bias_ref,
        qkv_ref, normed_ref, weight_ref, own_ref, top_ref, total_ref, mix_ref,
        qt_ref, k_ref, vt_ref, bias_held, scores_ref, rows_held, bias_sem,
    ) = refs[known + rows_in :]
    heads, size, length = vt_ref.shape
    part_length = length // (known + 1)
    turn = pl.program_id(0)
    load = pltpu.make_async_copy(bias_ref, bias_held, bias_sem)

    @pl.when(turn == 0)
    def _():
        load.start()
        for i, piece in enumerate(weights):
            rows = piece.shape[0]
            rows_held[pl.ds(pl.multiple_of(place_ref[i] * rows, rows), rows), :] = piece[...]
        by_columns = rows_held[...].T
        weight_ref[...] = by_columns
        for i, piece in enumerate(pieces):

            @pl.when(slot_ref[i] == group_ref[0])
            def _():
                own_ref[...] = piece[...]

            normed, qkv = token_parts(piece[...], gain_ref[...], by_columns, heads)
            normed_ref[i] = normed
            qkv_ref[i] = qkv
            places = pl.ds(pl.multiple_of(slot_ref[i] * part_length, TILE), part_length)
            for h in range(heads):
                qt_ref[h, :, places] = query_pair(qkv[h])
                k_ref[h, places, :] = key_pair(qkv[heads + h])
                vt_ref[h, :, places] = qkv[2 * heads + h]
        load.wait()

    low, high = range_ref[0], range_ref[1]
    query = low + turn
    own = pl.ds(pl.multiple_of(query * TILE, TILE), TILE)
    state = attend_tiles(
        query, low, full_ref[query], jnp.minimum(most_ref[query], high), empty_state(heads, size),
        end_ref[:, own], [qt_ref[h, :, own] for h in range(heads)],
        k_ref, vt_ref, bias_held, scores_ref,
    )
    for h, (top, total, mix) in enumerate(state):
        top_ref[h, :, own] = top
        total_ref[h, :, own] = total
        mix_ref[h, :, own] = mix


def late_kernel(full_ref, most_ref, slot_ref, group_ref, range_ref, *refs):
    parts = slot_ref.shape[0]
    (
        piece_ref, weight_ref, gain_ref, end_ref, before_ref, top_ref, total_ref, mix_ref, bias_ref,
    ) = refs[:9]
    ots = refs[9 : 9 + parts]
    (
        lse_ref, qkv_ref, normed_ref,
        qt_ref, k_ref, vt_ref, bias_held, scores_ref, held_ref, bias_sem,
    ) = refs[9 + parts :]
    heads, size, length = vt_ref.shape
    count = length // TILE
    each = count // parts
    part_length = length // parts
    query = pl.program_id(0)
    load = pltpu.make_async_copy(bias_ref, bias_held, bias_sem)

    @pl.when(query == 0)
    def _():
        load.start()
        normed, qkv = token_parts(piece_ref[...], gain_ref[...], weight_ref[...], heads)
        normed_ref[0] = normed
        qkv_ref[0] = qkv
        for i in range(parts):
            source = before_ref.at[i] if i < parts - 1 else qkv_ref.at[0]
            places = pl.ds(pl.multiple_of(slot_ref[i] * part_length, TILE), part_length)
            for h in range(heads):
                qt_ref[h, :, places] = query_pair(source[h])
                k_ref[h, places, :] = key_pair(source[heads + h])
                vt_ref[h, :, places] = source[2 * heads + h]
        load.wait()

    low, high = range_ref[0], range_ref[1]
    own = pl.ds(pl.multiple_of(query * TILE, TILE), TILE)
    begun = (query >= low) & (query < high)
    for h in range(heads):
        held_ref[h, 0:1, :] = jnp.where(begun, top_ref[h, :, own], MASKED)
        held_ref[h, 1:2, :] = jnp.where(begun, total_ref[h, :, own], 0.0)
        held_ref[h, 8:, :] = jnp.where(begun, mix_ref[h, :, own], 0.0)
    state = tuple(
        (held_ref[h, 0:1, :], held_ref[h, 1:2, :], held_ref[h, 8:, :]) for h in range(heads)
    )
    most = most_ref[query]
    first = jnp.where(begun & (low == 0), high, 0)
    last = jnp.where(begun & (low > 0), jnp.minimum(low, most), most)
    state = attend_tiles(
        query, first, full_ref[query], last, state,
        end_ref[:, own], [qt_ref[h, :, own] for h in range(heads)],
        k_ref, vt_ref, bias_held, scores_ref,
    )
    turn = (query // each) ^ group_ref[0]
    inner = pl.ds(pl.multiple_of(lax.rem(query, each) * TILE, TILE), TILE)
    mixes = [(mix * (1.0 / total)).astype(bf16) for _, total, mix in state]
    for h, (top, total, _) in enumerate(state):
        lse_ref[h] = top + jnp.log(total) * LOG2E
    for r in range(parts):

        @pl.when(turn == r)
        def _():
            for h in range(heads):
                ots[r][h * size : (h + 1) * size, inner] = mixes[h]


def shape(*dims, kind=bf16):
    return jax.ShapeDtypeStruct(dims, kind)


def sequence_held(heads, size, length, bias):
    return [
        pltpu.VMEM((heads, 2 * size, length), bf16),
        pltpu.VMEM((heads, length, 2 * size), bf16),
        pltpu.VMEM((heads, size, length), bf16),
        pltpu.VMEM(bias.shape, f32),
        pltpu.VMEM((2, heads, TILE, TILE), f32),
    ]


def attend_early(pieces, weights, places, gain, bias, end, full, most, slots, group, known):
    parts = len(pieces) + 1
    part_length, width = pieces[0].shape
    columns = weights[0].shape[1]
    heads = bias.shape[0]
    size = columns // (3 * heads)
    length = parts * part_length
    smem = pl.BlockSpec(memory_space=pltpu.SMEM)
    hbm = pl.BlockSpec(memory_space=pl.ANY)
    outs = [
        shape(parts - 1, 3 * heads, size, part_length),
        shape(parts - 1, part_length, width),
        shape(columns, width),
        shape(part_length, width),
        shape(heads, 1, length, kind=f32),
        shape(heads, 1, length, kind=f32),
        shape(heads, size, length, kind=f32),
    ]
    dense = (*pieces, *weights, gain, end)
    return pl.pallas_call(
        early_kernel,
        grid=((parts - 1) * part_length // TILE,),
        in_specs=[smem] * 6 + [whole(a.shape) for a in dense] + [hbm],
        out_specs=[whole(a.shape) for a in outs],
        out_shape=outs,
        scratch_shapes=sequence_held(heads, size, length, bias)
        + [pltpu.VMEM((width, columns), bf16), pltpu.SemaphoreType.DMA],
        compiler_params=params(),
        cost_estimate=cost(20),
        name="attend_early",
    )(full, most, slots, group, known, places, *dense, bias)


def attend_late(piece, weight, gain, bias, end, full, most, slots, group, known, qkv, state):
    part_length, width = piece.shape
    parts, heads = qkv.shape[0] + 1, bias.shape[0]
    size = qkv.shape[2]
    length = parts * part_length
    smem = pl.BlockSpec(memory_space=pltpu.SMEM)
    hbm = pl.BlockSpec(memory_space=pl.ANY)
    outs = [
        *[shape(heads * size, part_length)] * parts,
        shape(heads, 1, length, kind=f32),
        shape(1, 3 * heads, size, part_length),
        shape(1, part_length, width),
    ]
    out_specs = [whole(a.shape) for a in outs]
    out_specs[parts] = pl.BlockSpec((heads, 1, TILE), lambda i: (0, 0, i))
    dense = (piece, weight, gain, end, qkv, *state)
    return pl.pallas_call(
        late_kernel,
        grid=(length // TILE,),
        in_specs=[smem] * 5 + [whole(a.shape) for a in dense] + [hbm],
        out_specs=out_specs,
        out_shape=outs,
        scratch_shapes=sequence_held(heads, size, length, bias)
        + [pltpu.VMEM((heads, size + 8, TILE), f32), pltpu.SemaphoreType.DMA],
        compiler_params=params(),
        cost_estimate=cost(15),
        name="attend_late",
    )(full, most, slots, group, known, *dense, bias)

def backward_kernel(least_ref, clear_ref, slot_ref, group_ref, *refs):
    parts = slot_ref.shape[0]
    grads, ots = refs[:parts], refs[parts : 2 * parts]
    (
        qkv_early, qkv_late, lse_ref, end_ref, weight_ref, bias_ref,
    ) = refs[2 * parts : 2 * parts + 6]
    outs = refs[2 * parts + 6 : 3 * parts + 6]
    qkv_ref = [qkv_early.at[i] for i in range(parts - 1)] + [qkv_late.at[0]]
    (
        dqkv_ref, band_out,
        qt_ref, kt_ref, vt_ref, got_ref, pair_ref,
        dqt_acc, dk_acc, dv_acc, delta_ref, band_ref, bias_held, bias_sem, band_sem,
    ) = refs[3 * parts + 6 :]
    heads, size, length = qt_ref.shape
    columns = heads * size
    count = length // TILE
    each = count // parts
    part_length = length // parts
    key = pl.program_id(0)
    key_cols = pl.ds(pl.multiple_of(key * TILE, TILE), TILE)
    load = pltpu.make_async_copy(bias_ref, bias_held, bias_sem)
    store = pltpu.make_async_copy(band_ref, band_out, band_sem)
    every = range(heads)

    @pl.when(key == 0)
    def _():
        load.start()
        dqt_acc[...] = jnp.zeros_like(dqt_acc)
        band_ref[...] = jnp.zeros_like(band_ref)
        for i in range(parts):
            places = pl.ds(pl.multiple_of(slot_ref[i] * part_length, TILE), part_length)
            for h in every:
                qt_ref[h, :, places] = qkv_ref[i][h]
                pair_ref[h, :, places] = query_pair(qkv_ref[i][h])
                kt_ref[h, :, places] = qkv_ref[i][heads + h]
                vt_ref[h, :, places] = qkv_ref[i][2 * heads + h]
        for turn in range(parts):
            part = group_ref[0] ^ turn
            places = pl.ds(pl.multiple_of(part * part_length, TILE), part_length)
            for h in every:
                rows = slice(h * size, (h + 1) * size)
                grad = grads[turn][rows, :]
                got_ref[h, :, places] = grad
                delta_ref[h, :, places] = jnp.sum(
                    ots[turn][rows, :].astype(f32) * grad.astype(f32), axis=0, keepdims=True
                )
        load.wait()

    dk_acc[...] = jnp.zeros_like(dk_acc)
    dv_acc[...] = jnp.zeros_like(dv_acc)
    kt = [kt_ref[h, :, key_cols] for h in every]
    k = [key_pair(tile) for tile in kt]
    v = [vt_ref[h, :, key_cols].T for h in every]

    def step(query, masked):
        cols = pl.ds(pl.multiple_of(query * TILE, TILE), TILE)
        place = key - query + count - 1
        scores = [dot(k[h], pair_ref[h, :, cols]) + bias_held[h, place] for h in every]
        if masked:
            keep = lax.broadcasted_iota(jnp.int32, (TILE, TILE), 0) + key * TILE < end_ref[:, cols]
            scores = [jnp.where(keep, tile, MASKED) for tile in scores]
        grad_weights = [dot(v[h], got_ref[h, :, cols]) for h in every]
        weights = [jnp.exp2(scores[h] - lse_ref[h, :, cols]) for h in every]
        grad_scores = [weights[h] * (grad_weights[h] - delta_ref[h, :, cols]) for h in every]
        for h in every:
            band_ref[h, place] += grad_scores[h]
        rounded = [tile.astype(bf16) for tile in grad_scores]
        weights = [tile.astype(bf16) for tile in weights]
        for h in every:
            dv_acc[h] += dot(got_ref[h, :, cols], weights[h], ((1,), (1,)))
        for h in every:
            dk_acc[h] += dot(qt_ref[h, :, cols], rounded[h], ((1,), (1,)))
        for h in every:
            dqt_acc[h, :, cols] += dot(kt[h], rounded[h])

    def edge_step(query, _):
        step(query, True)
        return 0

    def full_step(query, _):
        step(query, False)
        return 0

    lax.fori_loop(least_ref[key], clear_ref[key], edge_step, 0)
    lax.fori_loop(clear_ref[key], count, full_step, 0)
    slot = jnp.int32(0)
    for i in range(parts):
        slot = jnp.where(slot_ref[i] == key // each, i, slot)
    inner = pl.ds(pl.multiple_of(lax.rem(key, each) * TILE, TILE), TILE)
    for h in every:
        dqkv_ref[slot, columns + h * size : columns + (h + 1) * size, inner] = dk_acc[h].astype(bf16)
        dqkv_ref[slot, 2 * columns + h * size : 2 * columns + (h + 1) * size, inner] = (
            dv_acc[h].astype(bf16)
        )

    @pl.when(key == count - 1)
    def _():
        for i in range(parts):
            places = pl.ds(pl.multiple_of(slot_ref[i] * part_length, TILE), part_length)
            for h in every:
                dqkv_ref[i, h * size : (h + 1) * size, :] = dqt_acc[h, :, places].astype(bf16)
        store.start()
        weight = weight_ref[...]
        for i in reversed(range(parts)):
            outs[i][...] = dot(dqkv_ref[i], weight, ((0,), (0,))).astype(bf16)
        store.wait()


def sums_kernel(group_ref, place_ref, *refs):
    (
        dqkv_ref, normed_early, normed_late, weight_ref, gain_ref, feed_gain_ref, bucket_ref, band_in, small_ref,
    ) = refs[:9]
    share_refs = refs[9:-4]
    band_ref, sum_ref, line_ref, band_sem = refs[-4:]
    load = pltpu.make_async_copy(band_in, band_ref, band_sem)
    load.start()
    parts = dqkv_ref.shape[0]
    every = range(band_ref.shape[0])
    normed_ref = [normed_early.at[i] for i in range(parts - 1)] + [normed_late.at[0]]
    weight = weight_ref[...]
    total = dot(dqkv_ref[0], normed_ref[0][...])
    for i in range(1, parts):
        total = total + dot(dqkv_ref[i], normed_ref[i][...])
    sum_ref[...] = total.T
    place = 0
    for share in share_refs:
        for i in range(share.shape[0]):
            rows = share.shape[1]
            at = pl.ds(pl.multiple_of(place_ref[place] * rows, rows), rows)
            share[i] = sum_ref[at, :].astype(bf16)
            place += 1

    small_ref[...] = jnp.zeros_like(small_ref)
    gain_grad = jnp.sum(total * weight.astype(f32), axis=0, keepdims=True) / gain_ref[...]
    lanes = small_ref.shape[1]
    each_gain = weight.shape[1] // lanes
    for row in range(each_gain):
        cut = slice(row * lanes, (row + 1) * lanes)
        small_ref[row : row + 1, :] = gain_grad[:, cut]
        small_ref[each_gain + row : each_gain + row + 1, :] = feed_gain_ref[:, cut]

    line_ref[...] = jnp.zeros_like(line_ref)
    load.wait()
    tiles = band_ref.shape[1]

    def one(pair, _):
        bands = [(place, h) for place in (2 * pair, 2 * pair + 1) for h in every]
        zero = jnp.zeros((TILE // 2, TILE // 2), f32)
        lines = []
        for place, h in bands:
            upper, lower = band_ref[h, place, : TILE // 2], band_ref[h, place, TILE // 2 :]
            lines.append(
                jnp.concatenate([zero, zero, upper], axis=1)
                + jnp.concatenate([zero, lower, zero], axis=1)
            )
        half = TILE // 4
        while half >= 1:
            turned = [pltpu.roll(line[half:], 2 * TILE - half, 1) for line in lines]
            lines = [line[:half] + turn for line, turn in zip(lines, turned)]
            half //= 2
        for (place, h), line in zip(bands, lines):
            start = pl.multiple_of((tiles - 1 - place) * TILE, TILE)
            line_ref[h : h + 1, pl.ds(start, 2 * TILE)] += line
        return 0

    lax.fori_loop(0, tiles // 2, one, 0)
    line = line_ref[0:8, :]
    terms = []
    for _ in range(3):
        term = line.astype(bf16)
        terms.append(term)
        line = line - term.astype(f32)
    names = lax.broadcasted_iota(jnp.int32, (lanes, line_ref.shape[1]), 0)
    onehot = jnp.where(lax.rem(names, lanes // 4) == bucket_ref[...], 1.0, 0.0).astype(bf16)
    sums = [dot(term, onehot, ((1,), (1,))) for term in terms]
    sums = sums[0] + sums[1] + sums[2]
    lane = lax.broadcasted_iota(jnp.int32, (1, lanes), 1)
    table = jnp.zeros((1, lanes), f32)
    for h in every:
        mine = (lane >= h * (lanes // 4)) & (lane < (h + 1) * (lanes // 4))
        table = jnp.where(mine, sums[h : h + 1], table)
    small_ref[pl.ds(2 * each_gain + group_ref[0], 1), :] = table


def attend_backward(grads, ots, qkv, lse, end, weight, bias, least, clear, slots, group):
    parts = len(grads)
    _, triple, size, part_length = qkv[0].shape
    heads, length = triple // 3, parts * part_length
    columns, width = weight.shape
    smem = pl.BlockSpec(memory_space=pltpu.SMEM)
    hbm = pl.BlockSpec(memory_space=pl.ANY)
    dense = [*grads, *ots, *qkv, lse, end, weight]
    outs = [shape(part_length, width)] * parts + [shape(parts, columns, part_length)]
    by_columns = pltpu.VMEM((heads, size, length), bf16)
    return pl.pallas_call(
        backward_kernel,
        grid=(length // TILE,),
        in_specs=[smem] * 4 + [whole(a.shape) for a in dense] + [hbm],
        out_specs=[whole(a.shape) for a in outs] + [hbm],
        out_shape=outs + [shape(*bias.shape, kind=f32)],
        scratch_shapes=[by_columns] * 4
        + [
            pltpu.VMEM((heads, 2 * size, length), bf16),
            pltpu.VMEM((heads, size, length), f32),
            pltpu.VMEM((heads, size, TILE), f32),
            pltpu.VMEM((heads, size, TILE), f32),
            pltpu.VMEM((heads, 1, length), f32),
            pltpu.VMEM(bias.shape, f32),
            pltpu.VMEM(bias.shape, f32),
            pltpu.SemaphoreType.DMA,
            pltpu.SemaphoreType.DMA,
        ],
        compiler_params=params(),
        cost_estimate=cost(45),
        name="attend_backward",
    )(least, clear, slots, group, *dense, bias)


def attend_sums(dqkv, normed, weight, gain, feed_gain_grad, bucket, bands, group, places, shares):
    parts, columns, _ = dqkv.shape
    width = weight.shape[1]
    smem = pl.BlockSpec(memory_space=pltpu.SMEM)
    dense = [dqkv, *normed, weight, gain.reshape(1, width), feed_gain_grad, bucket]
    outs = [shape(2 * (width // 128) + parts, 128, kind=f32)]
    outs += [shape(number, rows, columns) for number, rows in shares]
    return pl.pallas_call(
        sums_kernel,
        in_specs=[smem] * 2
        + [whole(a.shape) for a in dense]
        + [pl.BlockSpec(memory_space=pl.ANY)],
        out_specs=[whole(a.shape) for a in outs],
        out_shape=outs,
        scratch_shapes=[
            pltpu.VMEM(bands.shape, f32),
            pltpu.VMEM((width, columns), f32),
            pltpu.VMEM((8, bucket.shape[1]), f32),
            pltpu.SemaphoreType.DMA,
        ],
        compiler_params=params(),
        cost_estimate=cost(12),
        name="attend_sums",
    )(group, places, *dense, bands)


def middle_kernel(turn_ref, *refs):
    parts = turn_ref.shape[0]
    mixes = refs[:parts]
    x_ref, g_ref, gain_ref, weight_ref, out_ref, gain_grad_ref = refs[parts : parts + 6]
    gots = refs[parts + 6 : 2 * parts + 6]
    (
        grads_ref, w_ref, grad_ref, second_ref, acc_ref, back_ref, gh_ref, load_sem, store_sem,
    ) = refs[2 * parts + 6 :]
    width = x_ref.shape[1]
    columns = mixes[0].shape[0]
    feed = weight_ref.shape[3] - 256
    hidden_units = feed // 2
    late, early = pl.ds(feed, 256), pl.ds(0, feed)

    def load(z, which, cols):
        return pltpu.make_async_copy(
            weight_ref.at[:, z, :, cols], w_ref.at[z, :, :, cols], load_sem.at[z, which]
        )

    def store(z, which, cols):
        return pltpu.make_async_copy(
            grad_ref.at[z, :, :, cols], grads_ref.at[:, z, :, cols], store_sem.at[z, which]
        )

    for z in range(parts):
        load(z, 0, late).start()
    for z in range(parts):
        load(z, 1, early).start()
    for z in range(parts):
        load(z, 0, late).wait()

    def output_rows(turn):
        return w_ref[turn_ref[turn], :, :, feed : feed + columns].reshape(width, columns)

    hidden = x_ref[...].astype(f32)
    for turn in range(parts):
        hidden = hidden + dot(mixes[turn][...], output_rows(turn), ((0,), (1,)))
    inverse = lax.rsqrt(jnp.mean(hidden * hidden, axis=-1, keepdims=True) + EPSILON)
    second_ref[...] = (hidden * inverse * gain_ref[...]).astype(bf16)
    acc_ref[...] = hidden
    back_ref[...] = jnp.zeros_like(back_ref)
    gh_ref[...] = hidden * inverse

    def hidden_part(z, _):
        load(z, 1, early).wait()
        inner = w_ref[z, :, :, :hidden_units].reshape(width, hidden_units)
        outer = w_ref[z, :, :, hidden_units:feed].reshape(width, hidden_units)
        second = second_ref[...]
        grad = g_ref[...]
        units = dot(second, inner)
        grad_active = dot(grad, outer).astype(bf16).astype(f32)
        active, slope = gelu_parts(units)
        active = active.astype(bf16)
        grad_units = (grad_active * slope).astype(bf16)
        acc_ref[...] += dot(active, outer, ((1,), (1,)))
        back_ref[...] += dot(grad_units, inner, ((1,), (1,)))
        shape = (*grad_ref.shape[1:3], hidden_units)
        grad_ref[z, :, :, :hidden_units] = (
            dot(second, grad_units, ((0,), (0,))).astype(bf16).reshape(shape)
        )
        grad_ref[z, :, :, hidden_units:feed] = (
            dot(grad, active, ((0,), (0,))).astype(bf16).reshape(shape)
        )
        store(z, 1, early).start()
        return 0

    lax.fori_loop(0, parts, hidden_part, 0)
    out_ref[0] = acc_ref[...].astype(bf16)
    scaled = gh_ref[...]
    grad_second = back_ref[...]
    gain_grad_ref[...] = jnp.sum(grad_second * scaled, axis=0, keepdims=True)
    grad_scaled = grad_second * gain_ref[...]
    grad_hidden = g_ref[...].astype(f32) + inverse * (
        grad_scaled - scaled * jnp.mean(grad_scaled * scaled, axis=-1, keepdims=True)
    )
    rounded = grad_hidden.astype(bf16)
    out_ref[1] = rounded
    for turn in range(parts):
        grads = dot(rounded, mixes[turn][...], ((0,), (1,))).astype(bf16)
        grad_ref[turn_ref[turn], :, :, feed : feed + columns] = grads.reshape(
            *grad_ref.shape[1:3], columns
        )
        grad_ref[turn_ref[turn], :, :, feed + columns :] = jnp.zeros(
            (*grad_ref.shape[1:3], 256 - columns), bf16
        )
    for z in range(parts):
        store(z, 0, late).start()
    for turn in range(parts):
        gots[turn][...] = dot(output_rows(turn), rounded, ((0,), (1,))).astype(bf16)
    for z in range(parts):
        store(z, 0, late).wait()
        store(z, 1, early).wait()


def middle(turns, mixes, inputs, cotangent, gain, weights):
    rows, width = inputs.shape
    owners, parts, each, columns = weights.shape
    smem = pl.BlockSpec(memory_space=pltpu.SMEM)
    hbm = pl.BlockSpec(memory_space=pl.ANY)
    held = pltpu.VMEM((parts, owners, each, columns), bf16)
    dense = [*mixes, inputs, cotangent, gain.reshape(1, width)]
    outs = [
        jax.ShapeDtypeStruct((2, rows, width), bf16),
        jax.ShapeDtypeStruct((1, width), f32),
        *[jax.ShapeDtypeStruct(mix.shape, bf16) for mix in mixes],
    ]
    return pl.pallas_call(
        middle_kernel,
        in_specs=[smem] + [whole(a.shape) for a in dense] + [hbm],
        out_specs=[whole(a.shape) for a in outs] + [hbm],
        out_shape=outs + [jax.ShapeDtypeStruct(weights.shape, bf16)],
        scratch_shapes=[
            held,
            held,
            pltpu.VMEM((rows, width), bf16),
            pltpu.VMEM((rows, width), f32),
            pltpu.VMEM((rows, width), f32),
            pltpu.VMEM((rows, width), f32),
            pltpu.SemaphoreType.DMA((parts, 2)),
            pltpu.SemaphoreType.DMA((parts, 2)),
        ],
        compiler_params=params(),
        name="middle",
    )(turns, *dense, weights)


def flat(pairs, parts):
    return [(c * parts + z, d * parts + y) for (c, z), (d, y) in pairs]


def routes(parts):
    half = parts // 2
    devices = [(c, z) for c in range(2) for z in range(parts)]

    def group(c, z):
        return (z % half) * 2 + c

    gather = [
        flat([((0, z), (0, z - 1)) for z in (1, 2, 3)] + [((1, z), (1, z + 1)) for z in (0, 1, 2)], parts),
        flat([((0, z), (0, z - 1)) for z in (1, 2)] + [((1, z), (1, z + 1)) for z in (1, 2)], parts),
        flat([((0, 1), (0, 0)), ((0, 0), (0, 1)), ((1, 2), (1, 3)), ((1, 3), (1, 2))], parts),
    ]
    rounds = [
        flat([((c, z), (c ^ (r % half), z ^ (r // half))) for c, z in devices], parts)
        for r in range(parts)
    ]
    owners = flat([((c, z), (z // half, group(c, z))) for c, z in devices], parts)
    weights = [
        flat([((z // half ^ flip, group(c, z)), (c, z)) for c, z in devices], parts)
        for flip in range(2)
    ]
    return gather, rounds, owners, weights


def back(pairs):
    return [(target, source) for source, target in pairs]


SWAP = [(0, 1), (1, 0)]
LINE = ("core", "tensor")


def after(value, *earlier):
    return lax.optimization_barrier((value, *earlier))[0]


def across(value, step):
    return lax.ppermute(value, "plane", [(i, i ^ step) for i in range(lax.axis_size("plane"))])


def body(
    inputs,
    attention_gain,
    feedforward_gain,
    query_weight,
    key_weight,
    value_weight,
    output_weight,
    inner_weight,
    outer_weight,
    bias_table,
    block_index,
    position_bucket,
    cotangent,
):
    length = block_index.shape[1]
    parts = lax.axis_size("tensor")
    planes = lax.axis_size("plane")
    factor = 1.0 / math.sqrt(block_index.shape[0] * length * planes * 2)
    heads = bias_table.shape[1]
    buckets = bias_table.shape[0]
    width = inputs.shape[1]
    size = query_weight.shape[1] // heads
    columns = heads * size
    each = query_weight.shape[0]
    hidden_units = inner_weight.shape[1]
    core, z, plane = lax.axis_index("core"), lax.axis_index("tensor"), lax.axis_index("plane")
    half = parts // 2
    lower = z < half
    owner = core == z // half
    outer_chip = (z == 0) | (z == parts - 1)
    group = (z % half) * 2 + core
    group_ref = group.reshape(1)
    square = planes == 4 and each % 16 == 0
    gather, rounds, owners, weight_routes = routes(parts)
    tiles = length // TILE
    at_start = (z == 0) | (z == half)
    known = jnp.where(at_start, jnp.array([0, tiles - tiles // parts]), jnp.array([tiles // parts, tiles]))
    known = known.astype(jnp.int32)
    slots = jnp.array([[0, 1, 2, 3], [1, 2, 3, 0], [2, 1, 0, 3], [3, 2, 1, 0]], jnp.int32)[z]

    def swap(value):
        return lax.ppermute(value, "core", SWAP)

    pad = jnp.zeros((each, 256 - columns), bf16)
    packed_rest = jnp.concatenate([inner_weight, outer_weight.T, output_weight.T, pad], axis=1)

    packed = jnp.concatenate([query_weight, key_weight, value_weight], axis=1)
    first = lax.ppermute(inputs, LINE, gather[0])
    first, table, block_row, packed, packed_rest = lax.optimization_barrier(
        (first, bias_table, jnp.where(owner, block_index, swap(block_index)), packed, packed_rest)
    )
    table = lax.ppermute(table, LINE, weight_routes[0])
    block_row = block_row[0]
    line_rest = lax.all_gather(packed_rest, "tensor", axis=0)
    one, two = (lax.ppermute(packed, LINE, route) for route in weight_routes)
    second = lax.ppermute(first, LINE, gather[1])
    rows, bucket = bias_rows(table, position_bucket)
    bias = bias_tiles(rows, length)
    one, two = after((one, two), bias)
    low, high = jnp.where(lower, one, two), jnp.where(lower, two, one)
    if square:
        low_x, high_y = across(low, 1), across(high, 2)
        low_y, high_x = across(low, 2), across(high, 1)
        low_xy, high_xy = across(low_x, 2), across(high_y, 1)
        weights = [low, high, low_x, high_x, low_y, high_y, low_xy, high_xy]
        order = plane ^ jnp.arange(planes, dtype=jnp.int32)
        places = jnp.stack([order * 2, order * 2 + 1], axis=1).reshape(-1)
    else:
        both = lax.all_gather(jnp.stack([low, high]), "plane", axis=0)
        weights = [both.reshape(width, 3 * columns)]
        places = jnp.zeros((1,), jnp.int32)
    end, full, most, least, clear = spans(block_row)
    marks = (attention_gain.reshape(1, width), bias, end, full, most, slots, group_ref, known)
    pieces = [jnp.where(owner, piece, swap(piece)) for piece in (inputs, first)]
    second, pieces, weights, places, marks, least, clear = lax.optimization_barrier(
        (second, pieces, weights, places, marks, least, clear)
    )
    third = lax.ppermute(jnp.where(outer_chip, inputs, second), LINE, gather[2])
    pieces = [*pieces, jnp.where(owner, second, swap(second))]
    all_rest = lax.all_gather(after(line_rest, second), ("plane", "core"), axis=0)


    _, bias, end, full, most, slots, group_ref, known = marks
    qkv, normed, weight, own_tokens, *state = attend_early(pieces, weights, places, *marks)
    third, state, cotangent = lax.optimization_barrier((third, state, cotangent))
    grad = lax.ppermute(cotangent, LINE, back(owners))
    third = jnp.where(owner, third, swap(third))
    *ots, lse, late_qkv, late_normed = attend_late(third, weight, *marks, qkv, state)
    qkv, normed = (qkv, late_qkv), (normed, late_normed)
    mixes = [ots[0]] + [lax.ppermute(ots[r], LINE, rounds[r]) for r in range(1, parts)]
    turns = (group ^ jnp.arange(parts)).astype(jnp.int32)
    if each % 16:
        all_rest = jnp.swapaxes(all_rest, 0, 1).reshape(1, parts, width, -1)
    results, feedforward_part, *gots, grads = middle(
        turns, mixes, own_tokens, grad, feedforward_gain, all_rest
    )
    if each % 16:
        grads = jnp.swapaxes(grads.reshape(parts, planes * 2, each, -1), 0, 1)
    gots = [gots[0]] + [lax.ppermute(gots[r], LINE, rounds[r]) for r in range(1, parts)]
    if square:
        order = plane ^ jnp.array([1, 3, 0, 2, 2, 3, 0, 1], jnp.int32)
        places = order * 2 + jnp.array([0, 0, 0, 0, 1, 1, 1, 1], jnp.int32)
        shares = [(2, each)] * 4
    else:
        places, shares = jnp.zeros((1,), jnp.int32), [(1, width)]
    gots, results, places, bucket = lax.optimization_barrier((gots, results, places, bucket))
    results = lax.ppermute(results, LINE, owners)

    rest = lax.psum_scatter(grads, ("plane", "core"), scatter_dimension=0)

    own, first, second, third, dqkv, bands = attend_backward(
        gots, ots, qkv, lse, end, weight, bias, least, clear, slots, group_ref
    )
    third, results = lax.optimization_barrier((third, results))
    layer_output, grad_hidden = results[0], results[1].astype(f32)
    third = third + swap(third)
    got = lax.ppermute(third, LINE, back(gather[2]))
    own, first, second = (part + swap(part) for part in (own, first, second))

    def small_step(small, axis, step):
        count = lax.axis_size(axis)
        return small + lax.ppermute(small, axis, [(i, i ^ step) for i in range(count)])

    dqkv, bands, third = lax.optimization_barrier((dqkv, bands, third))
    small, *weight_grads = attend_sums(
        dqkv, normed, weight, attention_gain, feedforward_part, bucket, bands, group_ref, places, shares
    )
    none = jnp.zeros_like(own)
    got, small, weight_grads, rest = lax.optimization_barrier((got, small, weight_grads, rest))
    rest = lax.psum_scatter(rest, "tensor", scatter_dimension=0)
    own = jnp.where(owner, jnp.where(outer_chip, own + got, own), none)
    second = jnp.where(outer_chip, second, second + got)
    got = lax.ppermute(second, LINE, back(gather[1]))
    if square:
        low_send, low, high_send, high = weight_grads
        low, high = low + across(low_send, 1), high + across(high_send, 2)
    else:
        low = high = weight_grads[0].reshape(planes, 2, each, 3 * columns)
    small = small_step(small, "core", 1)
    small = small_step(small, "tensor", 1)
    got, low, high, small = lax.optimization_barrier((got, low, high, small))
    first = jnp.where(owner, first, none) + got
    got = lax.ppermute(first, LINE, back(gather[0]))
    if square:
        low, high = low[0] + across(low[1], 2), high[0] + across(high[1], 1)
    else:
        shared = lax.psum_scatter(low, "plane", scatter_dimension=0)
        low, high = shared[0], shared[1]
    small = small_step(small, "tensor", 2)
    step = 1
    while step < planes:
        small = small_step(small, "plane", step)
        step *= 2
    attention_share = (
        lax.ppermute(jnp.where(lower, low, high), LINE, back(weight_routes[0]))
        + lax.ppermute(jnp.where(lower, high, low), LINE, back(weight_routes[1]))
    ).astype(f32) * factor
    small = small * factor
    rest_share = rest.astype(f32) * factor
    grad_first = (own + got).astype(f32)
    scaled_first, inverse_first, _ = norm_forward(inputs.astype(f32), attention_gain)
    input_grad = (
        grad_hidden + norm_backward(grad_first, scaled_first, inverse_first, attention_gain)
    ).astype(bf16)
    gain_rows = width // 128
    table_grad = small[2 * gain_rows :, : heads * 32].reshape(parts * heads, 32)[:, :buckets].T

    return (
        layer_output,
        input_grad,
        small[:gain_rows].reshape(width),
        small[gain_rows : 2 * gain_rows].reshape(width),
        attention_share[:, :columns],
        attention_share[:, columns : 2 * columns],
        attention_share[:, 2 * columns :],
        rest_share[:, 2 * hidden_units : 2 * hidden_units + columns].T,
        rest_share[:, :hidden_units],
        rest_share[:, hidden_units : 2 * hidden_units].T,
        table_grad,
    )


def solution(mesh):
    groups, parts = mesh.devices.shape
    fine = Mesh(mesh.devices.reshape(groups // 2, 2, parts), ("plane", "core", "tensor"))
    dp = ("plane", "core")
    tokens = P(("plane", "core", "tensor"), None)
    by_rows = P(dp, "tensor")
    by_columns = P("tensor", dp)
    placed = (
        tokens, P(), P(), by_rows, by_rows, by_rows, by_columns, by_rows, by_columns,
        P(None, "tensor"), P(dp, None), P(), tokens,
    )
    results = (
        tokens, tokens, P(), P(), by_rows, by_rows, by_rows, by_columns, by_rows, by_columns, P(),
    )
    return jax.shard_map(body, mesh=fine, in_specs=placed, out_specs=results, check_vma=False)
```
